256 devices in a mesh: band: 128 (over z, y, x), feat: 2 (over core).
Axes of the slice: x: 4, y: 4, z: 8, core: 2. Of those that a mesh axis runs over, the one named last changes fastest.
Arguments:
- grid_latent: bfloat16 [131072, 512], P('band', 'feat'), may hold values from -6 to 6
- mesh_latent: bfloat16 [65536, 512], P('band', 'feat'), may hold values from -6 to 6
- encode_weights: bfloat16 [4, 512, 512], P(None, None, 'feat'), may hold values from -0.25 to 0.25
- layer_weights: bfloat16 [2, 4, 512, 512], P(None, None, None, 'feat'), may hold values from -0.25 to 0.25
- decode_weights: bfloat16 [4, 512, 512], P(None, None, 'feat'), may hold values from -0.25 to 0.25
- encode_senders: int32 [128, 5, 512], P('band'), may hold values from 0 to 1023
- encode_targets: int32 [128, 5, 512], P('band'), may hold values from 0 to 511
- encode_live: int32 [128, 5, 512], P('band'), may hold values from 0 to 1, as said below
- mesh_senders: int32 [65536, 8], P('band'), may hold values from 0 to 65535, as said below
- mesh_live: int32 [65536, 8], P('band'), may hold values 0 or 1
- decode_senders: int32 [128, 5, 1024], P('band'), may hold values from 0 to 511
- decode_targets: int32 [128, 5, 1024], P('band'), may hold values from 0 to 1023
- decode_live: int32 [128, 5, 1024], P('band'), may hold values from 0 to 1, as said below
Outputs:
- mesh_out: bfloat16 [65536, 512], P('band', 'feat')
- grid_out: bfloat16 [131072, 512], P('band', 'feat')
The draws below stay inside these ranges and needn't reach their ends.
Inputs may be any that keep to these rules, and one draw needn't show every extreme that they name: `encode_live`: A slot is live only where its band d - o + 2 exists; all slots of offset 2 (an owner's own band) are live. `decode_live`: A slot is live only where its owner d - o + 2 exists; all slots of offset 2 (a band's own owner) are live. `mesh_senders`: A mesh node's senders are nodes of its own owner or among the 64 rows at the near end of the owner before or after it.
All inputs are finite; a program needn't handle non-finite values. No bound on the sum of `mesh_live` on one device may be relied on, other than what follows from the above.
Results may differ from the reference program's by a relative error of at most 0.018.
Values may be sent and summed in bfloat16 or wider, within the bound.
No kernel may reach another device: no remote copies, remote signals or barrier semaphores. Data moves between devices by JAX's collectives and lax.ppermute only.
A program may use at most 64 MiB of HBM per device.

```python
import jax
import jax.numpy as jnp
from jax import lax

L = 512
G_DEV = 1024
M_DEV = 512
K_MESH = 8
REACH = 2
LAYERS = 2
SPAN = 5
OWNERS = 128
MARGIN = 64
CAP_G = 512
CAP_D = 1024
GRID = 131072
MESH = 65536


def live_slots(key, capacity):
    coins = jax.random.randint(jax.random.fold_in(key, 2), (OWNERS, SPAN, capacity), 0, 4)
    dest_ids = jnp.arange(OWNERS, dtype=jnp.int32)[:, None, None]
    offsets = jnp.arange(SPAN, dtype=jnp.int32)[None, :, None]
    source = dest_ids - offsets + REACH
    distance = jnp.abs(offsets - REACH)
    kept = jnp.where(distance == 0, 4, jnp.where(distance == 1, 3, 2))
    inside = (source >= 0) & (source < OWNERS)
    return jnp.where(inside & (coins < kept), 1, 0).astype(jnp.int32)


def draw_encode_live(key, part):
    key = jax.random.fold_in(key, 5)
    return live_slots(key, CAP_G)


def draw_decode_live(key, part):
    key = jax.random.fold_in(key, 6)
    return live_slots(key, CAP_D)


def draw_mesh_senders(key, part):
    key = jax.random.fold_in(key, 7)
    node_ids = jnp.arange(MESH, dtype=jnp.int32)
    owner_start = node_ids // M_DEV * M_DEV
    lowest = jnp.maximum(owner_start - MARGIN, 0)
    highest = jnp.minimum(owner_start + M_DEV + MARGIN, MESH)
    return jax.random.randint(key, (MESH, K_MESH), lowest[:, None], highest[:, None]).astype(jnp.int32)


def with_ends(values, own_key, smallest, top_value):
    index_at = [jax.random.randint(jax.random.fold_in(own_key, axis), (), 0, length) for axis, length in enumerate(values.shape)]
    longest = values.shape.index(max(values.shape))
    next_to = index_at[:longest] + [(index_at[longest] + 1) % values.shape[longest]] + index_at[longest + 1:]
    return values.at[tuple(index_at)].set(smallest).at[tuple(next_to)].set(top_value)


def levels(stream_key, shape, cuts, least, largest):
    factor_of, own = 1.0, jax.random.fold_in(stream_key, 6)
    for position, shards_of in cuts:
        draws = jnp.exp(jax.random.uniform(jax.random.fold_in(own, position), (shards_of,), jnp.float32, least / len(cuts), largest / len(cuts)))
        factor_of = factor_of * jnp.repeat(draws, shape[position] // shards_of).reshape([-1 if axis == position else 1 for axis in range(len(shape))])
    return factor_of


def noise(own_key, extent, deviation, limit, shards=(), kind=jnp.bfloat16):
    array = jax.random.normal(own_key, extent, jnp.float32) * deviation
    if len(shards) > 0:
        array = levels(own_key, extent, shards, -0.22, 0.18) * array
    return jnp.clip(array, min=-limit, max=limit).astype(kind)


def setup_inputs(seed: int = 0) -> dict:
    arg_keys = jax.random.split(jax.random.key(seed), 14)
    grid_latent = noise(arg_keys[0], (GRID, L), 1.0, 6.0, ((0, 128), (1, 2)))
    mesh_latent = noise(arg_keys[1], (MESH, L), 1.0, 6.0, ((0, 128), (1, 2)))
    encode_weights = noise(arg_keys[2], (4, L, L), L ** -0.5, 0.25, ((2, 2),))
    layer_weights = noise(arg_keys[3], (LAYERS, 4, L, L), L ** -0.5, 0.25, ((3, 2),))
    decode_weights = noise(arg_keys[4], (4, L, L), L ** -0.5, 0.25, ((2, 2),))
    encode_senders = with_ends(jax.random.randint(arg_keys[5], (OWNERS, SPAN, CAP_G), 0, G_DEV), jax.random.fold_in(arg_keys[5], 1), 0, G_DEV - 1).astype(jnp.int32)
    encode_targets = with_ends(jax.random.randint(arg_keys[6], (OWNERS, SPAN, CAP_G), 0, M_DEV), jax.random.fold_in(arg_keys[6], 1), 0, M_DEV - 1).astype(jnp.int32)
    encode_live = draw_encode_live(jax.random.fold_in(arg_keys[13], 71), 0)
    mesh_senders = draw_mesh_senders(jax.random.fold_in(arg_keys[13], 71), 0)
    mesh_live = with_ends((jax.random.randint(arg_keys[9], (MESH, K_MESH), 0, 4) < 3).astype(jnp.int32), jax.random.fold_in(arg_keys[9], 1), 0, 1)
    decode_senders = with_ends(jax.random.randint(arg_keys[10], (OWNERS, SPAN, CAP_D), 0, M_DEV), jax.random.fold_in(arg_keys[10], 1), 0, M_DEV - 1).astype(jnp.int32)
    decode_targets = with_ends(jax.random.randint(arg_keys[11], (OWNERS, SPAN, CAP_D), 0, G_DEV), jax.random.fold_in(arg_keys[11], 1), 0, G_DEV - 1).astype(jnp.int32)
    decode_live = draw_decode_live(jax.random.fold_in(arg_keys[13], 71), 0)
    return {"grid_latent": grid_latent, "mesh_latent": mesh_latent, "encode_weights": encode_weights, "layer_weights": layer_weights, "decode_weights": decode_weights, "encode_senders": encode_senders, "encode_targets": encode_targets, "encode_live": encode_live, "mesh_senders": mesh_senders, "mesh_live": mesh_live, "decode_senders": decode_senders, "decode_targets": decode_targets, "decode_live": decode_live}


def project(latent, weights):
    return jnp.dot(latent, weights, preferred_element_type=jnp.float32)


def node_update(latent, summed, weights):
    summed_b = summed.astype(jnp.bfloat16)
    update = project(latent, weights[2]) + project(summed_b, weights[3])
    return (latent.astype(jnp.float32) + jax.nn.silu(update)).astype(jnp.bfloat16)


def bucket_messages(sender_rows, receiver_side, senders, targets, live, send_count, recv_count, at_receiver):
    node_count = targets.shape[0]
    span_count = targets.shape[1]
    offsets = jnp.arange(span_count, dtype=jnp.int32)

    def one_dest(dest):
        source = jnp.clip(dest - offsets + REACH, 0, node_count - 1).astype(jnp.int32)
        if at_receiver:
            rows = senders[dest]
        else:
            rows = senders[source, offsets]
        picked = sender_rows[rows + (source * send_count)[:, None]]
        local_side = lax.dynamic_slice_in_dim(receiver_side, dest * recv_count, recv_count, 0)
        slot_targets = targets[dest]
        preact = picked.astype(jnp.float32) + local_side[slot_targets]
        message = (jax.nn.silu(preact) * live[dest][..., None].astype(jnp.float32)).astype(jnp.bfloat16)
        flat_message = message.astype(jnp.float32).reshape(-1, message.shape[-1])
        return jax.ops.segment_sum(flat_message, slot_targets.reshape(-1), num_segments=recv_count)

    summed = lax.map(one_dest, jnp.arange(node_count, dtype=jnp.int32))
    return summed.reshape(node_count * recv_count, summed.shape[-1])


def mesh_layer(mesh_now, weights, senders, live):
    layer_sent = project(mesh_now, weights[0]).astype(jnp.bfloat16)
    layer_recv = project(mesh_now, weights[1])
    preact = layer_sent[senders].astype(jnp.float32) + layer_recv[:, None, :]
    message = (jax.nn.silu(preact) * live[..., None].astype(jnp.float32)).astype(jnp.bfloat16)
    summed = jnp.sum(message.astype(jnp.float32), axis=1)
    return node_update(mesh_now, summed, weights)


def reference(grid_latent, mesh_latent, encode_weights, layer_weights, decode_weights, encode_senders, encode_targets, encode_live, mesh_senders, mesh_live, decode_senders, decode_targets, decode_live):
    encode_sent = project(grid_latent, encode_weights[0]).astype(jnp.bfloat16)
    encode_recv = project(mesh_latent, encode_weights[1])
    encode_sum = bucket_messages(encode_sent, encode_recv, encode_senders, encode_targets, encode_live, G_DEV, M_DEV, False)
    mesh_now = node_update(mesh_latent, encode_sum, encode_weights)
    for layer_idx in range(LAYERS):
        mesh_now = mesh_layer(mesh_now, layer_weights[layer_idx], mesh_senders, mesh_live)
    decode_sent = project(mesh_now, decode_weights[0]).astype(jnp.bfloat16)
    decode_recv = project(grid_latent, decode_weights[1])
    decode_sum = bucket_messages(decode_sent, decode_recv, decode_senders, decode_targets, decode_live, M_DEV, G_DEV, True)
    grid_now = node_update(grid_latent, decode_sum, decode_weights)
    return mesh_now, grid_now
```

```python
import functools

import jax
import jax.numpy as jnp
from jax import lax
from jax.experimental import pallas as pl
from jax.experimental.pallas import tpu as pltpu
from jax.sharding import PartitionSpec as P

REACH = 2
SPAN = 5
LAYERS = 2
MARGIN = 64
TILE = 256
F32 = jnp.float32
BF16 = jnp.bfloat16
VMEM_LIMIT = 40 * 1024 * 1024


def ring(value, steps):
    count = lax.axis_size("band")
    return lax.ppermute(value, "band", [(i, (i + steps) % count) for i in range(count)])


def swap(value):
    return lax.ppermute(value, "feat", [(0, 1), (1, 0)])


def silu(v):
    half = 0.5 * v
    return half + half * jnp.tanh(half)


def dot(a, b):
    return jnp.dot(a, b, preferred_element_type=F32)


def halves(feat):
    own = pl.ds(pl.multiple_of(feat * TILE, TILE), TILE)
    other = pl.ds(pl.multiple_of((1 - feat) * TILE, TILE), TILE)
    return own, other


def project(meta_ref, own, other, weights_ref):
    own_rows, other_rows = halves(meta_ref[0])
    return dot(own, weights_ref[own_rows, :]) + dot(other, weights_ref[other_rows, :])


def hot_columns(column, width):
    ids = lax.broadcasted_iota(jnp.int32, (column.shape[0], width), 1)
    return jnp.where(column == ids, 1.0, 0.0).astype(BF16)


def hot_rows(row, base, height):
    ids = lax.broadcasted_iota(jnp.int32, (height, row.shape[1]), 0) + base
    return jnp.where(row == ids, 1.0, 0.0).astype(BF16)


def call(kernel, name, operands, specs, outs, flops, scratch=()):
    size = sum(x.size * x.dtype.itemsize for x in outs)
    return pl.pallas_call(
        kernel,
        name=name,
        grid=(1,),
        in_specs=specs,
        out_specs=[whole(x) for x in outs],
        out_shape=list(outs),
        scratch_shapes=list(scratch),
        compiler_params=pltpu.CompilerParams(vmem_limit_bytes=VMEM_LIMIT),
        cost_estimate=pl.CostEstimate(flops=flops, bytes_accessed=2 * size, transcendentals=0),
    )(*operands)


def whole(x):
    return pl.BlockSpec(x.shape, lambda i, n=len(x.shape): (0,) * n)


def part(x, *index):
    lead = len(index)
    rest = x.shape[lead:]
    return pl.BlockSpec(
        (None,) * lead + rest, lambda i, where=index + (0,) * len(rest): where
    )


SMEM = pl.BlockSpec(memory_space=pltpu.SMEM)


def shape(rows, cols, dtype):
    return jax.ShapeDtypeStruct((rows, cols), dtype)


def encode_gather_kernel(meta, own, other, weights, senders, *refs):
    outs, sent = refs[:SPAN], refs[SPAN]
    for start in range(0, own.shape[0], TILE):
        rows = pl.ds(start, TILE)
        sent[rows, :] = project(meta, own[rows, :], other[rows, :], weights).astype(BF16)
    for offset in range(SPAN):
        for start in range(0, senders.shape[0], TILE):
            rows = pl.ds(start, TILE)
            hot = hot_columns(senders[rows, offset : offset + 1], sent.shape[0])
            outs[offset][rows, :] = dot(hot, sent[...]).astype(BF16)


def encode_gather(meta, own, other, weights, senders):
    slots = senders.shape[0]
    out = shape(slots, own.shape[1], BF16)
    return call(
        encode_gather_kernel,
        "encode_gather",
        (meta, own, other, weights, senders),
        [SMEM, whole(own), whole(other), part(weights, 0), whole(senders)],
        [out] * SPAN,
        2 * (SPAN * slots + 512) * own.shape[0] * own.shape[1],
        [pltpu.VMEM(own.shape, BF16)],
    )


def project_kernel(kinds, meta, own, other, *refs):
    count = len(kinds)
    for index in range(count):
        out = refs[count + index]
        for start in range(0, own.shape[0], TILE):
            rows = pl.ds(start, TILE)
            out[rows, :] = project(meta, own[rows, :], other[rows, :], refs[index]).astype(
                kinds[index]
            )


def projections(name, meta, own, other, picks, kinds):
    rows, cols = own.shape
    return call(
        functools.partial(project_kernel, kinds),
        name,
        (meta, own, other) + tuple(x for x, _ in picks),
        [SMEM, whole(own), whole(other)] + [part(x, *index) for x, index in picks],
        [shape(rows, cols, kind) for kind in kinds],
        2 * 512 * rows * cols * len(kinds),
    )


def bucket_step(rows_ref, recv_ref, sender_col, target_col, target_row, live_row, message):
    slots = target_col.shape[0]
    for start in range(0, slots, TILE):
        rows = slice(start, start + TILE)
        pre = dot(hot_columns(target_col[rows], recv_ref.shape[0]), recv_ref[...])
        if sender_col is None:
            pre = pre + rows_ref[rows, :].astype(F32)
        else:
            pre = pre + dot(hot_columns(sender_col[rows], rows_ref.shape[0]), rows_ref[...])
        message[rows, :] = silu(pre).astype(BF16)
    return jnp.where(live_row > 0, target_row, -1)


def bucket_kernel(offsets, gathers, has_total, *refs):
    count = len(offsets)
    pieces = refs[:count]
    rest = list(refs[count:])
    recv = rest.pop(0)
    total_in = rest.pop(0) if has_total else None
    senders = rest.pop(0) if gathers else None
    target_cols, target_rows, live_rows, out, total, message = rest
    nodes = recv.shape[0]
    for index, offset in enumerate(offsets):
        pick = slice(offset, offset + 1)
        where = bucket_step(
            pieces[index],
            recv,
            senders[:, pick] if gathers else None,
            target_cols[:, pick],
            target_rows[pick, :],
            live_rows[pick, :],
            message,
        )
        for start in range(0, nodes, TILE):
            rows = pl.ds(start, TILE)
            value = dot(hot_rows(where, start, TILE), message[...])
            if index > 0:
                value = value + total[rows, :]
            elif has_total:
                value = value + total_in[rows, :]
            if index == count - 1:
                out[rows, :] = value.astype(out.dtype)
            else:
                total[rows, :] = value


def buckets(name, offsets, pieces, recv, total, senders, target_cols, target_rows, live_rows, kind):
    nodes, cols = recv.shape
    slots = target_rows.shape[1]
    operands = list(pieces) + [recv]
    if total is not None:
        operands.append(total)
    if senders is not None:
        operands.append(senders)
    operands += [target_cols, target_rows, live_rows]
    return call(
        functools.partial(bucket_kernel, offsets, senders is not None, total is not None),
        name,
        operands,
        [whole(x) for x in operands],
        [shape(nodes, cols, kind)],
        2 * len(offsets) * slots * cols * (2 * nodes + (512 if senders is not None else 0)),
        [pltpu.VMEM((nodes, cols), F32), pltpu.VMEM((slots, cols), BF16)],
    )[0]


def update_kernel(last, meta, own, other, sum_own, sum_other, w2, w3, w2_other, w3_other, w0, *outs):
    total = own.shape[0]
    for start in range(0, total, TILE):
        rows = pl.ds(start, TILE)
        a, b, c, d = own[rows, :], other[rows, :], sum_own[rows, :], sum_other[rows, :]
        first = project(meta, a, b, w2) + project(meta, c, d, w3)
        outs[0][rows, :] = (a.astype(F32) + silu(first)).astype(BF16)
        second = project(meta, a, b, w2_other) + project(meta, c, d, w3_other)
        outs[1][rows, :] = (b.astype(F32) + silu(second)).astype(BF16)
    now_own, now_other = outs[0], outs[1]
    if last:
        for start in range(0, total, TILE):
            rows = pl.ds(start, TILE)
            outs[2][rows, :] = project(meta, now_own[rows, :], now_other[rows, :], w0).astype(BF16)
    else:
        for out, start in ((outs[2], 0), (outs[3], total - MARGIN)):
            rows = pl.ds(start, MARGIN)
            out[...] = project(meta, now_own[rows, :], now_other[rows, :], w0).astype(BF16)


def update(name, meta, own, other, sum_own, sum_other, w, w_other, where, w0, where0, last):
    rows, cols = own.shape
    full = shape(rows, cols, BF16)
    edge = shape(MARGIN, cols, BF16)
    operands = (meta, own, other, sum_own, sum_other, w, w, w_other, w_other, w0)
    specs = [SMEM] + [whole(x) for x in operands[1:5]]
    specs += [part(w, *where, 2), part(w, *where, 3)]
    specs += [part(w_other, *where, 2), part(w_other, *where, 3), part(w0, *where0)]
    return call(
        functools.partial(update_kernel, last),
        name,
        operands,
        specs,
        [full] * 3 if last else [full, full, edge, edge],
        2 * rows * cols * 512 * 5,
    )


def mesh_kernel(meta, sent, recv, before, after, senders, live, out, extended):
    rows_total = sent.shape[0]
    extended[0:MARGIN, :] = before[...]
    extended[MARGIN : MARGIN + rows_total, :] = sent[...]
    extended[MARGIN + rows_total :, :] = after[...]
    base = meta[1] * rows_total - MARGIN
    for start in range(0, rows_total, TILE):
        rows = pl.ds(start, TILE)
        side = recv[rows, :]
        local = senders[rows, :] - base
        flags = live[rows, :].astype(F32)
        total = jnp.zeros(side.shape, F32)
        for k in range(senders.shape[1]):
            hot = hot_columns(local[:, k : k + 1], extended.shape[0])
            message = silu(dot(hot, extended[...]) + side) * flags[:, k : k + 1]
            total = total + message.astype(BF16).astype(F32)
        out[rows, :] = total.astype(BF16)


def mesh_messages(name, meta, sent, recv, before, after, senders, live):
    rows, cols = sent.shape
    operands = (meta, sent, recv, before, after, senders, live)
    return call(
        mesh_kernel,
        name,
        operands,
        [SMEM] + [whole(x) for x in operands[1:]],
        [shape(rows, cols, BF16)],
        2 * rows * senders.shape[1] * (rows + 2 * MARGIN) * cols,
        [pltpu.VMEM((rows + 2 * MARGIN, cols), BF16)],
    )[0]


def final_kernel(meta, own, self_term, sum_own, sum_other, w3, out):
    for start in range(0, own.shape[0], TILE):
        rows = pl.ds(start, TILE)
        term = self_term[rows, :] + project(meta, sum_own[rows, :], sum_other[rows, :], w3)
        out[rows, :] = (own[rows, :].astype(F32) + silu(term)).astype(BF16)


def body(
    grid_latent,
    mesh_latent,
    encode_weights,
    layer_weights,
    decode_weights,
    encode_senders,
    encode_targets,
    encode_live,
    mesh_senders,
    mesh_live,
    decode_senders,
    decode_targets,
    decode_live,
):
    meta = jnp.stack([lax.axis_index("feat"), lax.axis_index("band")]).astype(jnp.int32)
    grid_other = swap(grid_latent)
    mesh_other = swap(mesh_latent)
    encode_other = swap(encode_weights)
    layer_other = swap(layer_weights)

    pieces = encode_gather(meta, grid_latent, grid_other, encode_weights, encode_senders[0].T)
    arrived = [x if o == REACH else ring(x, o - REACH) for o, x in enumerate(pieces)]
    (encode_recv,) = projections(
        "encode_recv", meta, mesh_latent, mesh_other, [(encode_weights, (1,))], [BF16]
    )
    targets = encode_targets[0]
    slots = (targets.T, targets, encode_live[0])
    total = buckets(
        "encode_own", (REACH,), [arrived[REACH]], encode_recv, None, None, *slots, F32
    )
    decode_recv, grid_self = projections(
        "decode_recv",
        meta,
        grid_latent,
        grid_other,
        [(decode_weights, (1,)), (decode_weights, (2,))],
        [BF16, F32],
    )
    encode_sum = buckets(
        "encode_rest",
        (0, 1, 3, 4),
        [arrived[o] for o in (0, 1, 3, 4)],
        encode_recv,
        total,
        None,
        *slots,
        BF16,
    )
    own, other, head, tail = update(
        "encode_update",
        meta,
        mesh_latent,
        mesh_other,
        encode_sum,
        swap(encode_sum),
        encode_weights,
        encode_other,
        (),
        layer_weights,
        (0, 0),
        False,
    )
    for layer in range(LAYERS):
        before = ring(tail, 1)
        after = ring(head, -1)
        sent, recv = projections(
            f"layer_project_{layer}",
            meta,
            own,
            other,
            [(layer_weights, (layer, 0)), (layer_weights, (layer, 1))],
            [BF16, F32],
        )
        summed = mesh_messages(
            f"layer_messages_{layer}", meta, sent, recv, before, after, mesh_senders, mesh_live
        )
        last = layer == LAYERS - 1
        results = update(
            f"layer_update_{layer}",
            meta,
            own,
            other,
            summed,
            swap(summed),
            layer_weights,
            layer_other,
            (layer,),
            decode_weights if last else layer_weights,
            (0,) if last else (layer + 1, 0),
            last,
        )
        own, other = results[0], results[1]
        if last:
            decode_sent = results[2]
        else:
            head, tail = results[2], results[3]

    targets = decode_targets[0]
    slots = (decode_senders[0].T, targets.T, targets, decode_live[0])
    rows = [decode_sent if o == REACH else ring(decode_sent, o - REACH) for o in range(SPAN)]
    total = buckets("decode_own", (2,), [rows[2]], decode_recv, None, *slots, F32)
    total = buckets("decode_near", (1, 3), [rows[1], rows[3]], decode_recv, total, *slots, F32)
    decode_sum = buckets("decode_far", (0, 4), [rows[0], rows[4]], decode_recv, total, *slots, BF16)
    decode_other = swap(decode_sum)
    operands = (meta, grid_latent, grid_self, decode_sum, decode_other, decode_weights)
    (grid_now,) = call(
        final_kernel,
        "final_update",
        operands,
        [SMEM] + [whole(x) for x in operands[1:5]] + [part(decode_weights, 3)],
        [shape(*grid_latent.shape, BF16)],
        2 * 512 * grid_latent.size,
    )
    return own, grid_now


def solution(mesh):
    placed = (
        P("band", "feat"),
        P("band", "feat"),
        P(None, None, "feat"),
        P(None, None, None, "feat"),
        P(None, None, "feat"),
        P("band", None, None),
        P("band", None, None),
        P("band", None, None),
        P("band", None),
        P("band", None),
        P("band", None, None),
        P("band", None, None),
        P("band", None, None),
    )
    return jax.shard_map(
        body,
        mesh=mesh,
        in_specs=placed,
        out_specs=(P("band", "feat"), P("band", "feat")),
        check_vma=False,
    )
```

```python
import functools

import jax
import jax.numpy as jnp
from jax import lax
from jax.experimental import pallas as pl
from jax.experimental.pallas import tpu as pltpu
from jax.sharding import PartitionSpec as P

REACH = 2
LAYERS = 2
MARGIN = 64
HALF = 256
LANES = 128
F32 = jnp.float32
BF16 = jnp.bfloat16
I32 = jnp.int32
VMEM_LIMIT = 36 * 1024 * 1024


def swap(value):
    return lax.ppermute(value, "feat", [(0, 1), (1, 0)])


def flat(partners):
    return [(2 * s + c, 2 * t + e) for (s, c), (t, e) in partners.items()]


def far_pairs(count):
    partners = {}
    for s in range(count):
        near = s + 1 if s % 2 else s - 1
        partners[s, 0] = (near % count, 0)
        skip = s + 2 if s % 4 >= 2 else s - 2
        partners[s, 1] = (skip if 0 <= skip < count else s ^ 1, 1)
    return flat(partners)


def line_pairs(count):
    partners = {}
    for s in range(count):
        partners[s, 0] = (s ^ 1, 0)
        partners[s, 1] = (s ^ 2, 1)
    return flat(partners)


def halo_pairs(count):
    partners = {}
    for s in range(count):
        partners[s, 1] = ((s + 1) % count, 0)
        partners[(s + 1) % count, 0] = (s, 1)
    return flat(partners)


def exchange(value, pairs):
    return lax.ppermute(value, ("band", "feat"), pairs(lax.axis_size("band")))


def silu(v):
    half = 0.5 * v
    return half + half * jnp.tanh(half)


def dot(a, b):
    return jnp.dot(a, b, preferred_element_type=F32)


def window(index, size=HALF):
    return pl.ds(pl.multiple_of(index * size, size), size)


def far_sent(meta):
    return (1 - meta[0]) * (1 + 2 * meta[2]) + meta[0] * 4 * meta[3]


def line_sent(meta):
    return (1 - meta[0]) * (3 - 2 * meta[2]) + meta[0] * (4 - 4 * meta[3])


far_received = line_sent
line_received = far_sent


def column(row):
    parts = [
        jnp.broadcast_to(row[:, start : start + LANES], (LANES, LANES)).T
        for start in range(0, row.shape[1], LANES)
    ]
    return parts[0] if len(parts) == 1 else jnp.concatenate(parts, axis=0)


def hot_columns(col, width):
    ids = lax.broadcasted_iota(I32, col.shape, 1)
    parts = [
        jnp.where(col == ids + start, 1.0, 0.0).astype(BF16) for start in range(0, width, LANES)
    ]
    return parts[0] if len(parts) == 1 else jnp.concatenate(parts, axis=1)


def hot_rows(row, height):
    ids = lax.broadcasted_iota(I32, (height, row.shape[1]), 0)
    return jnp.where(row == ids, 1.0, 0.0).astype(BF16)


def call(kernel, name, operands, specs, outs, flops, scratch=()):
    size = sum(x.size * x.dtype.itemsize for x in outs)
    return pl.pallas_call(
        kernel,
        name=name,
        grid=(1,),
        in_specs=specs,
        out_specs=[whole(x) for x in outs],
        out_shape=list(outs),
        scratch_shapes=list(scratch),
        compiler_params=pltpu.CompilerParams(vmem_limit_bytes=VMEM_LIMIT),
        cost_estimate=pl.CostEstimate(flops=flops, bytes_accessed=2 * size, transcendentals=0),
    )(*operands)


def whole(x):
    return pl.BlockSpec(x.shape, lambda i, n=len(x.shape): (0,) * n)


def part(x, *index):
    lead = len(index)
    rest = x.shape[lead:]
    return pl.BlockSpec((None,) * lead + rest, lambda i, where=index + (0,) * len(rest): where)


SMEM = pl.BlockSpec(memory_space=pltpu.SMEM)


def shape(*dims, dtype=BF16):
    return jax.ShapeDtypeStruct(dims, dtype)


def encode_begin_kernel(meta, own, w_own, out):
    for start in range(0, own.shape[0], HALF):
        rows = pl.ds(start, HALF)
        out[rows, :] = dot(own[rows, :], w_own[window(meta[0]), :])


def gather_slots(senders_row, sent, out):
    for start in range(0, senders_row.shape[1], HALF):
        col = column(senders_row[:, start : start + HALF])
        out[pl.ds(start, HALF), :] = dot(hot_columns(col, sent.shape[0]), sent[...]).astype(BF16)


def encode_far_kernel(meta, own, other, begun, w_own, w_other, senders, sent, piece):
    mine, rest = window(meta[0]), window(1 - meta[0])
    for start in range(0, own.shape[0], HALF):
        rows = pl.ds(start, HALF)
        a, b = own[rows, :], other[rows, :]
        sent[rows, mine] = (begun[rows, :] + dot(b, w_own[rest, :])).astype(BF16)
        sent[rows, rest] = (dot(a, w_other[mine, :]) + dot(b, w_other[rest, :])).astype(BF16)
    gather_slots(senders[pl.ds(far_sent(meta), 1), :], sent, piece)


def encode_line_kernel(meta, sent, senders, piece):
    gather_slots(senders[pl.ds(line_sent(meta), 1), :], sent, piece)


def scatter(row, message, total_in, nodes, put):
    for index in range(nodes // HALF):
        value = dot(hot_rows(row - index * HALF, HALF), message[...])
        if total_in is not None:
            value = value + total_in[pl.ds(index * HALF, HALF), :]
        put(index, value)


def live_targets(targets, live, offset, columns=slice(None)):
    pick = pl.ds(offset, 1)
    return jnp.where(live[pick, columns] > 0, targets[pick, columns], -1)


def encode_prepare_kernel(
    meta, own, other, w1, w1_other, w2, w2_other, sent, senders, targets, live,
    total, before_line, before_far, self_term, recv, message,
):
    mine, rest = window(meta[0]), window(1 - meta[0])
    nodes = own.shape[0]
    for start in range(0, nodes, HALF):
        rows = pl.ds(start, HALF)
        a, b = own[rows, :], other[rows, :]
        recv[rows, mine] = (dot(a, w1[mine, :]) + dot(b, w1[rest, :])).astype(BF16)
        recv[rows, rest] = (dot(a, w1_other[mine, :]) + dot(b, w1_other[rest, :])).astype(BF16)
    a, b = own[mine, :], other[mine, :]
    self_term[:, mine] = dot(a, w2[mine, :]) + dot(b, w2[rest, :])
    self_term[:, rest] = dot(a, w2_other[mine, :]) + dot(b, w2_other[rest, :])
    gather_slots(targets[pl.ds(line_received(meta), 1), :], recv, before_line)
    gather_slots(targets[pl.ds(far_received(meta), 1), :], recv, before_far)
    pick = pl.ds(REACH, 1)
    from_rows = hot_columns(column(senders[pick, mine]), sent.shape[0])
    to_rows = hot_columns(column(targets[pick, mine]), nodes)
    message[...] = silu(dot(from_rows, sent[...]) + dot(to_rows, recv[...])).astype(BF16)

    def put(index, value):
        total[pl.ds(index * HALF, HALF), :] = value

    scatter(live_targets(targets, live, REACH, mine), message, None, nodes, put)


def encode_line_sum_kernel(meta, rows, before, targets, live, total, out, message):
    message[...] = silu(rows[...].astype(F32) + before[...].astype(F32)).astype(BF16)

    def put(index, value):
        out[pl.ds(index * HALF, HALF), :] = value

    row = live_targets(targets, live, line_received(meta))
    scatter(row, message, total, total.shape[0], put)


def encode_far_sum_kernel(meta, rows, before, targets, live, total, out_own, out_other, message):
    message[...] = silu(rows[...].astype(F32) + before[...].astype(F32)).astype(BF16)
    row = live_targets(targets, live, far_received(meta))
    for out, half in ((out_other, 1 - meta[0]), (out_own, meta[0])):
        value = dot(hot_rows(row - half * HALF, HALF), message[...]) + total[window(half), :]
        out[...] = value.astype(out.dtype)


def put_edge(meta, now, w0, w0_other, edge):
    mine, rest = window(meta[0]), window(1 - meta[0])
    rows = now[pl.ds(pl.multiple_of(meta[0] * (HALF - MARGIN), MARGIN), MARGIN), :]
    edge[:, mine] = dot(rows, w0[...]).astype(BF16)
    edge[:, rest] = dot(rows, w0_other[...]).astype(BF16)


def encode_update_kernel(
    meta, own, other, self_term, sum_own, sum_other, w3, w3_other, w0, w0_other, now, edge
):
    mine, rest = window(meta[0]), window(1 - meta[0])
    summed = (sum_own[...] + sum_other[...].astype(F32)).astype(BF16)
    for cols, latent, w in ((mine, own, w3), (rest, other, w3_other)):
        step = silu(self_term[:, cols] + dot(summed, w[...]))
        now[:, cols] = (latent[mine, :].astype(F32) + step).astype(BF16)
    put_edge(meta, now, w0, w0_other, edge)


def layer_project_kernel(
    last, meta, own, other, w0, w0_other, w1, w1_other, w2, w2_other,
    sent_own, sent_other, recv, self_own, *self_other,
):
    mine, rest = window(meta[0]), window(1 - meta[0])
    for cols, w in ((mine, w0), (rest, w0_other)):
        sent_own[:, cols] = dot(own[...], w[...]).astype(BF16)
        sent_other[:, cols] = dot(other[...], w[...]).astype(BF16)
    for cols, w in ((mine, w1), (rest, w1_other)):
        recv[:, cols] = dot(own[...], w[...])
    for cols, w in ((mine, w2), (rest, w2_other)):
        self_own[:, cols] = dot(own[...], w[...])
        if last:
            self_other[0][:, cols] = dot(other[...], w[...])


def layer_gather_kernel(meta, own, other, senders, out):
    mine = window(meta[0])
    base = meta[1] * (2 * HALF)
    for k in range(senders.shape[0]):
        local = senders[k : k + 1, mine] - base
        col = column(local - meta[0] * HALF)
        col_other = column(local - (1 - meta[0]) * HALF)
        value = dot(hot_columns(col, HALF), own[...])
        value = value + dot(hot_columns(col_other, HALF), other[...])
        out[k] = value.astype(BF16)


def layer_sum(meta, gathered, recv, near, far, senders, live, halo, total):
    mine = window(meta[0])
    nodes = 2 * HALF
    base = meta[1] * nodes
    halo[pl.ds(pl.multiple_of(meta[0] * MARGIN, MARGIN), MARGIN), :] = near[...]
    halo[pl.ds(pl.multiple_of((1 - meta[0]) * MARGIN, MARGIN), MARGIN), :] = far[...]
    count = senders.shape[0]
    for k in range(count):
        local = senders[k : k + 1, mine] - base
        where = jnp.where(local < 0, local + MARGIN, local - nodes + MARGIN)
        where = jnp.where((local >= 0) & (local < nodes), -1, where)
        flags = column(live[k : k + 1, mine]).astype(F32)
        flags = jnp.concatenate([flags] * (recv.shape[1] // LANES), axis=1)
        pre = dot(hot_columns(column(where), 2 * MARGIN), halo[...])
        pre = pre + gathered[k].astype(F32) + recv[...]
        message = (silu(pre) * flags).astype(BF16).astype(F32)
        total[...] = message if k == 0 else total[...] + message
    return total[...].astype(BF16)


def layer_update_kernel(
    meta, gathered, recv, near, far, senders, live, now, self_term, w3, w3_other, w0, w0_other,
    out, edge, halo, total,
):
    mine, rest = window(meta[0]), window(1 - meta[0])
    summed = layer_sum(meta, gathered, recv, near, far, senders, live, halo, total)
    for cols, w in ((mine, w3), (rest, w3_other)):
        step = silu(self_term[:, cols] + dot(summed, w[...]))
        out[:, cols] = (now[:, cols].astype(F32) + step).astype(BF16)
    put_edge(meta, out, w0, w0_other, edge)


def layer_sum_kernel(meta, gathered, recv, near, far, senders, live, out, halo, total):
    out[...] = layer_sum(meta, gathered, recv, near, far, senders, live, halo, total)


def last_update_kernel(
    meta, now_own, now_other, self_own, self_other, sum_own, sum_other, w3, w3_other,
    w0, w0_other, out, sent, now,
):
    mine, rest = window(meta[0]), window(1 - meta[0])
    for rows, latent, self_term, summed in (
        (mine, now_own, self_own, sum_own),
        (rest, now_other, self_other, sum_other),
    ):
        for cols, w in ((mine, w3), (rest, w3_other)):
            step = silu(self_term[:, cols] + dot(summed[...], w[...]))
            now[:, cols] = (latent[:, cols].astype(F32) + step).astype(BF16)
        out[rows, :] = now[:, mine]
        for cols, w in ((mine, w0), (rest, w0_other)):
            sent[rows, cols] = dot(now[...], w[...]).astype(BF16)


def decode_prepare_kernel(
    meta, own, other, w1, w1_other, w2, targets,
    before_own, before_line, before_far, self_term, recv,
):
    mine, rest = window(meta[0]), window(1 - meta[0])
    for start in range(0, own.shape[0], HALF):
        rows = pl.ds(start, HALF)
        a, b = own[rows, :], other[rows, :]
        recv[rows, mine] = (dot(a, w1[mine, :]) + dot(b, w1[rest, :])).astype(BF16)
        recv[rows, rest] = (dot(a, w1_other[mine, :]) + dot(b, w1_other[rest, :])).astype(BF16)
        self_term[rows, :] = dot(a, w2[mine, :]) + dot(b, w2[rest, :])
    half = before_own.shape[0]
    gather_slots(targets[pl.ds(REACH, 1), window(meta[0], half)], recv, before_own)
    gather_slots(targets[pl.ds(line_received(meta), 1), :], recv, before_line)
    gather_slots(targets[pl.ds(far_received(meta), 1), :], recv, before_far)


def decode_sum_kernel(kind, meta, sent, before, senders, targets, live, *refs):
    total, out, message = refs if kind != "own" else (None,) + refs
    slots = before.shape[0]
    if kind == "own":
        offset, columns = REACH, window(meta[0], slots)
    else:
        offset = (line_received if kind == "line" else far_received)(meta)
        columns = slice(None)
    from_row = senders[pl.ds(offset, 1), columns]
    for start in range(0, slots, HALF):
        rows = pl.ds(start, HALF)
        hot = hot_columns(column(from_row[:, start : start + HALF]), sent.shape[0])
        pre = dot(hot, sent[...]) + before[rows, :].astype(F32)
        message[rows, :] = silu(pre).astype(BF16)

    def put(index, value):
        out[pl.ds(index * HALF, HALF), :] = value.astype(out.dtype)

    scatter(live_targets(targets, live, offset, columns), message, total, out.shape[0], put)


def final_kernel(meta, own, self_term, sum_own, sum_other, w3, out):
    for start in range(0, own.shape[0], HALF):
        rows = pl.ds(start, HALF)
        summed = (sum_own[rows, :].astype(F32) + sum_other[rows, :].astype(F32)).astype(BF16)
        step = silu(self_term[rows, :] + dot(summed, w3[...]))
        out[rows, :] = (own[rows, :].astype(F32) + step).astype(BF16)


def body(
    grid_latent,
    mesh_latent,
    encode_weights,
    layer_weights,
    decode_weights,
    encode_senders,
    encode_targets,
    encode_live,
    mesh_senders,
    mesh_live,
    decode_senders,
    decode_targets,
    decode_live,
):
    band = lax.axis_index("band")
    meta = jnp.stack([lax.axis_index("feat"), band, band % 2, band // 2 % 2]).astype(I32)
    grid_rows, cols = grid_latent.shape
    mesh_rows = mesh_latent.shape[0]
    full = 2 * cols
    senders, targets, live = encode_senders[0], encode_targets[0], encode_live[0]
    slots = senders.shape[1]

    grid_other = swap(grid_latent)
    first_other = swap(encode_weights[0])
    (begun,) = call(
        encode_begin_kernel,
        "encode_begin",
        (meta, grid_latent, encode_weights),
        [SMEM, whole(grid_latent), part(encode_weights, 0)],
        [shape(grid_rows, cols, dtype=F32)],
        2 * grid_rows * cols * cols,
    )
    operands = (meta, grid_latent, grid_other, begun, encode_weights, first_other, senders)
    sent, far_piece = call(
        encode_far_kernel,
        "encode_far",
        operands,
        [SMEM] + [whole(x) for x in operands[1:4]]
        + [part(encode_weights, 0), whole(first_other), whole(senders)],
        [shape(grid_rows, full), shape(slots, full)],
        2 * full * (grid_rows * full + slots * grid_rows),
    )
    far_rows = exchange(far_piece, far_pairs)
    operands = (meta, sent, senders)
    (line_piece,) = call(
        encode_line_kernel,
        "encode_line",
        operands,
        [SMEM, whole(sent), whole(senders)],
        [shape(slots, full)],
        2 * full * slots * grid_rows,
    )
    line_rows = exchange(line_piece, line_pairs)

    mesh_source, encode_source, layer_source, decode_source, _ = lax.optimization_barrier(
        (mesh_latent, encode_weights, layer_weights, decode_weights, sent)
    )
    mesh_other = swap(mesh_source)
    encode_other = swap(encode_source)
    layer_other = swap(layer_source)
    decode_other = swap(decode_source)

    operands = (
        meta, mesh_latent, mesh_other, encode_weights, encode_other, encode_weights, encode_other,
        sent, senders, targets, live,
    )
    total, before_line, before_far, self_term = call(
        encode_prepare_kernel,
        "encode_prepare",
        operands,
        [SMEM, whole(mesh_latent), whole(mesh_other)]
        + [part(operands[3 + i], 1 + i // 2) for i in range(4)]
        + [whole(x) for x in operands[7:]],
        [
            shape(mesh_rows, full, dtype=F32),
            shape(slots, full),
            shape(slots, full),
            shape(HALF, full, dtype=F32),
        ],
        2 * full * mesh_rows * (full + 3 * slots),
        [pltpu.VMEM((mesh_rows, full), BF16), pltpu.VMEM((HALF, full), BF16)],
    )
    operands = (meta, line_rows, before_line, targets, live, total)
    (total,) = call(
        encode_line_sum_kernel,
        "encode_line_sum",
        operands,
        [SMEM] + [whole(x) for x in operands[1:]],
        [shape(mesh_rows, full, dtype=F32)],
        2 * full * mesh_rows * slots,
        [pltpu.VMEM((slots, full), BF16)],
    )
    operands = (meta, far_rows, before_far, targets, live, total)
    sum_own, sum_other = call(
        encode_far_sum_kernel,
        "encode_far_sum",
        operands,
        [SMEM] + [whole(x) for x in operands[1:]],
        [shape(HALF, full, dtype=F32), shape(HALF, full)],
        2 * full * mesh_rows * slots,
        [pltpu.VMEM((slots, full), BF16)],
    )
    operands = (
        meta, mesh_latent, mesh_other, self_term, sum_own, swap(sum_other),
        encode_weights, encode_other, layer_weights, layer_other,
    )
    now, edge = call(
        encode_update_kernel,
        "encode_update",
        operands,
        [SMEM] + [whole(x) for x in operands[1:6]]
        + [part(encode_weights, 3), part(encode_other, 3)]
        + [part(layer_weights, 0, 0), part(layer_other, 0, 0)],
        [shape(HALF, full), shape(MARGIN, full)],
        2 * HALF * full * full,
    )

    senders_t, live_t = mesh_senders.T, mesh_live.T
    degree = senders_t.shape[0]
    for layer in range(LAYERS):
        last = layer == LAYERS - 1
        near = exchange(edge, halo_pairs)
        now_other = swap(now)
        operands = (meta, now, now_other) + (layer_weights, layer_other) * 3
        results = call(
            functools.partial(layer_project_kernel, last),
            f"layer_project_{layer}",
            operands,
            [SMEM, whole(now), whole(now_other)]
            + [part(operands[3 + i], layer, i // 2) for i in range(6)],
            [shape(HALF, full)] * 2 + [shape(HALF, full, dtype=F32)] * (3 if last else 2),
            2 * HALF * full * full * 4,
        )
        sent_own, sent_other, recv, self_own = results[:4]
        operands = (meta, sent_own, sent_other, senders_t)
        (gathered,) = call(
            layer_gather_kernel,
            f"layer_gather_{layer}",
            operands,
            [SMEM] + [whole(x) for x in operands[1:]],
            [shape(degree, HALF, full)],
            2 * degree * HALF * full * mesh_rows,
        )
        operands = (meta, gathered, recv, near, swap(near), senders_t, live_t)
        scratch = [pltpu.VMEM((2 * MARGIN, full), BF16), pltpu.VMEM((HALF, full), F32)]
        if last:
            (summed,) = call(
                layer_sum_kernel,
                f"layer_sum_{layer}",
                operands,
                [SMEM] + [whole(x) for x in operands[1:]],
                [shape(HALF, full)],
                2 * degree * HALF * full * 2 * MARGIN,
                scratch,
            )
            continue
        operands += (now, self_own) + (layer_weights, layer_other) * 2
        now, edge = call(
            layer_update_kernel,
            f"layer_update_{layer}",
            operands,
            [SMEM] + [whole(x) for x in operands[1:9]]
            + [part(layer_weights, layer, 3), part(layer_other, layer, 3)]
            + [part(layer_weights, layer + 1, 0), part(layer_other, layer + 1, 0)],
            [shape(HALF, full), shape(MARGIN, full)],
            2 * HALF * full * (degree * 2 * MARGIN + full),
            scratch,
        )
    operands = (
        meta, now, now_other, self_own, results[4], summed, swap(summed),
        layer_weights, layer_other, decode_weights, decode_other,
    )
    mesh_now, sent = call(
        last_update_kernel,
        "last_update",
        operands,
        [SMEM] + [whole(x) for x in operands[1:7]]
        + [part(layer_weights, LAYERS - 1, 3), part(layer_other, LAYERS - 1, 3)]
        + [part(decode_weights, 0), part(decode_other, 0)],
        [shape(mesh_rows, cols), shape(mesh_rows, full)],
        2 * mesh_rows * full * full * 2,
        [pltpu.VMEM((HALF, full), BF16)],
    )

    far_rows = exchange(sent, far_pairs)
    line_rows = exchange(sent, line_pairs)
    senders, targets, live = decode_senders[0], decode_targets[0], decode_live[0]
    slots = senders.shape[1]
    operands = (
        meta, grid_latent, grid_other, decode_weights, decode_other, decode_weights, targets
    )
    before_own, before_line, before_far, self_term = call(
        decode_prepare_kernel,
        "decode_prepare",
        operands,
        [SMEM, whole(grid_latent), whole(grid_other)]
        + [part(decode_weights, 1), part(decode_other, 1), part(decode_weights, 2), whole(targets)],
        [
            shape(slots // 2, full),
            shape(slots, full),
            shape(slots, full),
            shape(grid_rows, cols, dtype=F32),
        ],
        2 * full * grid_rows * (full + 5 * slots // 2),
        [pltpu.VMEM((grid_rows, full), BF16)],
    )
    total = None
    for kind, rows, before in (
        ("own", sent, before_own),
        ("line", line_rows, before_line),
        ("far", far_rows, before_far),
    ):
        operands = (meta, rows, before, senders, targets, live)
        if total is not None:
            operands += (total,)
        (total,) = call(
            functools.partial(decode_sum_kernel, kind),
            f"decode_{kind}",
            operands,
            [SMEM] + [whole(x) for x in operands[1:]],
            [shape(grid_rows, full, dtype=BF16 if kind == "far" else F32)],
            2 * full * before.shape[0] * (grid_rows + mesh_rows),
            [pltpu.VMEM(before.shape, BF16)],
        )
    operands = (meta, grid_latent, self_term, total, swap(total), decode_weights)
    (grid_now,) = call(
        final_kernel,
        "final_update",
        operands,
        [SMEM] + [whole(x) for x in operands[1:5]] + [part(decode_weights, 3)],
        [shape(grid_rows, cols)],
        2 * full * grid_rows * cols,
    )
    return mesh_now, grid_now


def solution(mesh):
    placed = (
        P("band", "feat"),
        P("band", "feat"),
        P(None, None, "feat"),
        P(None, None, None, "feat"),
        P(None, None, "feat"),
        P("band", None, None),
        P("band", None, None),
        P("band", None, None),
        P("band", None),
        P("band", None),
        P("band", None, None),
        P("band", None, None),
        P("band", None, None),
    )
    return jax.shard_map(
        body,
        mesh=mesh,
        in_specs=placed,
        out_specs=(P("band", "feat"), P("band", "feat")),
        check_vma=False,
    )
```

```python
import functools

import jax
import jax.numpy as jnp
from jax import lax
from jax.experimental import pallas as pl
from jax.experimental.pallas import tpu as pltpu
from jax.sharding import PartitionSpec as P

REACH = 2
LAYERS = 2
MARGIN = 64
HALF = 256
LANES = 128
F32 = jnp.float32
BF16 = jnp.bfloat16
I32 = jnp.int32
VMEM_LIMIT = 36 * 1024 * 1024


def swap(value):
    return lax.ppermute(value, "feat", [(0, 1), (1, 0)])


def flat(partners):
    return [(2 * s + c, 2 * t + e) for (s, c), (t, e) in partners.items()]


def far_pairs(count):
    partners = {}
    for s in range(count):
        near = s + 1 if s % 2 else s - 1
        partners[s, 0] = (near % count, 0)
        skip = s + 2 if s % 4 >= 2 else s - 2
        partners[s, 1] = (skip if 0 <= skip < count else s ^ 1, 1)
    return flat(partners)


def line_pairs(count):
    partners = {}
    for s in range(count):
        partners[s, 0] = (s ^ 1, 0)
        partners[s, 1] = (s ^ 2, 1)
    return flat(partners)


def halo_pairs(count):
    partners = {}
    for s in range(count):
        partners[s, 1] = ((s + 1) % count, 0)
        partners[(s + 1) % count, 0] = (s, 1)
    return flat(partners)


def halo_shift(count):
    partners = {}
    for s in range(count):
        partners[s, 1] = ((s + 1) % count, 1)
        partners[s, 0] = ((s - 1) % count, 0)
    return flat(partners)


def exchange(value, pairs):
    return lax.ppermute(value, ("band", "feat"), pairs(lax.axis_size("band")))


def after(value, other):
    return lax.optimization_barrier((value, other))[0]


def silu(v):
    half = 0.5 * v
    return half + half * jnp.tanh(half)


def dot(a, b):
    return jnp.dot(a, b, preferred_element_type=F32)


def window(index, size=HALF):
    return pl.ds(pl.multiple_of(index * size, size), size)


def far_sent(meta):
    return (1 - meta[0]) * (1 + 2 * meta[2]) + meta[0] * 4 * meta[3]


def line_sent(meta):
    return (1 - meta[0]) * (3 - 2 * meta[2]) + meta[0] * (4 - 4 * meta[3])


far_received = line_sent
line_received = far_sent


def column(row):
    parts = [
        jnp.broadcast_to(row[:, start : start + LANES], (LANES, LANES)).T
        for start in range(0, row.shape[1], LANES)
    ]
    return parts[0] if len(parts) == 1 else jnp.concatenate(parts, axis=0)


def hot_columns(col, width):
    ids = lax.broadcasted_iota(I32, col.shape, 1)
    parts = [
        jnp.where(col == ids + start, 1.0, 0.0).astype(BF16) for start in range(0, width, LANES)
    ]
    return parts[0] if len(parts) == 1 else jnp.concatenate(parts, axis=1)


def hot_rows(row, height):
    ids = lax.broadcasted_iota(I32, (height, row.shape[1]), 0)
    return jnp.where(row == ids, 1.0, 0.0).astype(BF16)


def call(kernel, name, operands, specs, outs, flops, scratch=()):
    size = sum(x.size * x.dtype.itemsize for x in outs)
    return pl.pallas_call(
        kernel,
        name=name,
        grid=(1,),
        in_specs=specs,
        out_specs=[whole(x) for x in outs],
        out_shape=list(outs),
        scratch_shapes=list(scratch),
        compiler_params=pltpu.CompilerParams(vmem_limit_bytes=VMEM_LIMIT),
        cost_estimate=pl.CostEstimate(flops=flops // 64, bytes_accessed=size // 64, transcendentals=0),
    )(*operands)


def whole(x):
    return pl.BlockSpec(x.shape, lambda i, n=len(x.shape): (0,) * n)


def part(x, *index):
    lead = len(index)
    rest = x.shape[lead:]
    return pl.BlockSpec((None,) * lead + rest, lambda i, where=index + (0,) * len(rest): where)


SMEM = pl.BlockSpec(memory_space=pltpu.SMEM)


def shape(*dims, dtype=BF16):
    return jax.ShapeDtypeStruct(dims, dtype)


def encode_begin_kernel(meta, own, w_own, out):
    for start in range(0, own.shape[0], HALF):
        rows = pl.ds(start, HALF)
        out[rows, :] = dot(own[rows, :], w_own[window(meta[0]), :])


def gather_slots(senders_row, sent, out):
    for start in range(0, senders_row.shape[1], HALF):
        col = column(senders_row[:, start : start + HALF])
        out[pl.ds(start, HALF), :] = dot(hot_columns(col, sent.shape[0]), sent[...]).astype(BF16)


def encode_far_kernel(meta, own, other, begun, w_own, w_other, senders, sent, piece):
    mine, rest = window(meta[0]), window(1 - meta[0])
    for start in range(0, own.shape[0], HALF):
        rows = pl.ds(start, HALF)
        a, b = own[rows, :], other[rows, :]
        sent[rows, mine] = (begun[rows, :] + dot(b, w_own[rest, :])).astype(BF16)
        sent[rows, rest] = (dot(a, w_other[mine, :]) + dot(b, w_other[rest, :])).astype(BF16)
    gather_slots(senders[far_sent(meta)], sent, piece)


def scatter(row, message, total_in, nodes, put):
    for index in range(nodes // HALF):
        value = dot(hot_rows(row - index * HALF, HALF), message[...])
        if total_in is not None:
            value = value + total_in[pl.ds(index * HALF, HALF), :]
        put(index, value)


def live_targets(targets, live, offset, columns=slice(None)):
    return jnp.where(live[offset, :, columns] > 0, targets[offset, :, columns], -1)


def encode_line_kernel(
    meta, own, other, w1, w1_other, w2, w2_other, sent, senders, targets, live,
    piece, total, before_line, before_far, self_term, recv, message,
):
    gather_slots(senders[line_sent(meta)], sent, piece)
    mine, rest = window(meta[0]), window(1 - meta[0])
    nodes = own.shape[0]
    for start in range(0, nodes, HALF):
        rows = pl.ds(start, HALF)
        a, b = own[rows, :], other[rows, :]
        recv[rows, mine] = (dot(a, w1[mine, :]) + dot(b, w1[rest, :])).astype(BF16)
        recv[rows, rest] = (dot(a, w1_other[mine, :]) + dot(b, w1_other[rest, :])).astype(BF16)
    a, b = own[mine, :], other[mine, :]
    self_term[:, mine] = dot(a, w2[mine, :]) + dot(b, w2[rest, :])
    self_term[:, rest] = dot(a, w2_other[mine, :]) + dot(b, w2_other[rest, :])
    gather_slots(targets[line_received(meta)], recv, before_line)
    gather_slots(targets[far_received(meta)], recv, before_far)
    from_rows = hot_columns(column(senders[REACH, :, mine]), sent.shape[0])
    to_rows = hot_columns(column(targets[REACH, :, mine]), nodes)
    message[...] = silu(dot(from_rows, sent[...]) + dot(to_rows, recv[...])).astype(BF16)

    def put(index, value):
        total[pl.ds(index * HALF, HALF), :] = value

    scatter(live_targets(targets, live, REACH, mine), message, None, nodes, put)


def encode_far_sum_kernel(meta, rows, before, targets, live, total, out, message):
    message[...] = silu(rows[...].astype(F32) + before[...].astype(F32)).astype(BF16)

    def put(index, value):
        out[pl.ds(index * HALF, HALF), :] = value

    row = live_targets(targets, live, far_received(meta))
    scatter(row, message, total, total.shape[0], put)


def encode_line_sum_kernel(meta, rows, before, targets, live, total, out_own, out_other, message):
    message[...] = silu(rows[...].astype(F32) + before[...].astype(F32)).astype(BF16)
    row = live_targets(targets, live, line_received(meta))
    for out, half in ((out_other, 1 - meta[0]), (out_own, meta[0])):
        value = dot(hot_rows(row - half * HALF, HALF), message[...]) + total[window(half), :]
        out[...] = value.astype(out.dtype)


def put_edge(meta, now, w0, w0_other, edge):
    mine, rest = window(meta[0]), window(1 - meta[0])
    rows = now[pl.ds(pl.multiple_of(meta[0] * (HALF - MARGIN), MARGIN), MARGIN), :]
    edge[:, mine] = dot(rows, w0[...]).astype(BF16)
    edge[:, rest] = dot(rows, w0_other[...]).astype(BF16)


def encode_update_kernel(
    meta, own, other, self_term, sum_own, sum_other, w3, w3_other, w0, w0_other, now, edge
):
    mine, rest = window(meta[0]), window(1 - meta[0])
    summed = (sum_own[...] + sum_other[...].astype(F32)).astype(BF16)
    for cols, latent, w in ((mine, own, w3), (rest, other, w3_other)):
        step = silu(self_term[:, cols] + dot(summed, w[...]))
        now[:, cols] = (latent[mine, :].astype(F32) + step).astype(BF16)
    put_edge(meta, now, w0, w0_other, edge)


def layer_project_kernel(
    last, meta, own, other, w0, w0_other, w1, w1_other, w2, w2_other,
    sent_own, sent_other, recv, self_own, *self_other,
):
    mine, rest = window(meta[0]), window(1 - meta[0])
    for cols, w in ((mine, w0), (rest, w0_other)):
        sent_own[:, cols] = dot(own[...], w[...]).astype(BF16)
        sent_other[:, cols] = dot(other[...], w[...]).astype(BF16)
    for cols, w in ((mine, w1), (rest, w1_other)):
        recv[:, cols] = dot(own[...], w[...])
    for cols, w in ((mine, w2), (rest, w2_other)):
        self_own[:, cols] = dot(own[...], w[...])
        if last:
            self_other[0][:, cols] = dot(other[...], w[...])


def layer_gather_kernel(meta, own, other, senders, out):
    mine = window(meta[0])
    base = meta[1] * (2 * HALF)
    for k in range(senders.shape[0]):
        local = senders[k : k + 1, mine] - base
        col = column(local - meta[0] * HALF)
        col_other = column(local - (1 - meta[0]) * HALF)
        value = dot(hot_columns(col, HALF), own[...])
        value = value + dot(hot_columns(col_other, HALF), other[...])
        out[k] = value.astype(BF16)


def layer_sum(meta, gathered, recv, far, near, senders, live, halo, total):
    mine = window(meta[0])
    nodes = 2 * HALF
    base = meta[1] * nodes
    halo[pl.ds(pl.multiple_of(meta[0] * MARGIN, MARGIN), MARGIN), :] = near[...]
    halo[pl.ds(pl.multiple_of((1 - meta[0]) * MARGIN, MARGIN), MARGIN), :] = far[...]
    count = senders.shape[0]
    for k in range(count):
        local = senders[k : k + 1, mine] - base
        where = jnp.where(local < 0, local + MARGIN, local - nodes + MARGIN)
        where = jnp.where((local >= 0) & (local < nodes), -1, where)
        flags = column(live[k : k + 1, mine]).astype(F32)
        flags = jnp.concatenate([flags] * (recv.shape[1] // LANES), axis=1)
        pre = dot(hot_columns(column(where), 2 * MARGIN), halo[...])
        pre = pre + gathered[k].astype(F32) + recv[...]
        message = (silu(pre) * flags).astype(BF16).astype(F32)
        total[...] = message if k == 0 else total[...] + message
    return total[...].astype(BF16)


def layer_update_kernel(
    meta, gathered, recv, far, near, senders, live, now, self_term, w3, w3_other, w0, w0_other,
    out, edge, halo, total,
):
    mine, rest = window(meta[0]), window(1 - meta[0])
    summed = layer_sum(meta, gathered, recv, far, near, senders, live, halo, total)
    for cols, w in ((mine, w3), (rest, w3_other)):
        step = silu(self_term[:, cols] + dot(summed, w[...]))
        out[:, cols] = (now[:, cols].astype(F32) + step).astype(BF16)
    put_edge(meta, out, w0, w0_other, edge)


def layer_sum_kernel(meta, gathered, recv, far, near, senders, live, out, halo, total):
    out[...] = layer_sum(meta, gathered, recv, far, near, senders, live, halo, total)


def last_update_kernel(
    meta, now_own, now_other, self_own, self_other, sum_own, sum_other, w3, w3_other,
    w0, w0_other, out, sent, now,
):
    mine, rest = window(meta[0]), window(1 - meta[0])
    for rows, latent, self_term, summed in (
        (mine, now_own, self_own, sum_own),
        (rest, now_other, self_other, sum_other),
    ):
        for cols, w in ((mine, w3), (rest, w3_other)):
            step = silu(self_term[:, cols] + dot(summed[...], w[...]))
            now[:, cols] = (latent[:, cols].astype(F32) + step).astype(BF16)
        out[rows, :] = now[:, mine]
        for cols, w in ((mine, w0), (rest, w0_other)):
            sent[rows, cols] = dot(now[...], w[...]).astype(BF16)


def decode_prepare_kernel(
    meta, own, other, w1, w1_other, w2, targets,
    before_own, before_line, before_far, self_term, recv,
):
    mine, rest = window(meta[0]), window(1 - meta[0])
    for start in range(0, own.shape[0], HALF):
        rows = pl.ds(start, HALF)
        a, b = own[rows, :], other[rows, :]
        recv[rows, mine] = (dot(a, w1[mine, :]) + dot(b, w1[rest, :])).astype(BF16)
        recv[rows, rest] = (dot(a, w1_other[mine, :]) + dot(b, w1_other[rest, :])).astype(BF16)
        self_term[rows, :] = dot(a, w2[mine, :]) + dot(b, w2[rest, :])
    half = before_own.shape[0]
    gather_slots(targets[REACH, :, window(meta[0], half)], recv, before_own)
    gather_slots(targets[line_received(meta)], recv, before_line)
    gather_slots(targets[far_received(meta)], recv, before_far)


def decode_sum_kernel(kind, meta, sent, before, senders, targets, live, *refs):
    total, out, message = refs if kind != "own" else (None,) + refs
    slots = before.shape[0]
    if kind == "own":
        offset, columns = REACH, window(meta[0], slots)
    else:
        offset = (line_received if kind == "line" else far_received)(meta)
        columns = slice(None)
    from_row = senders[offset, :, columns]
    for start in range(0, slots, HALF):
        rows = pl.ds(start, HALF)
        hot = hot_columns(column(from_row[:, start : start + HALF]), sent.shape[0])
        pre = dot(hot, sent[...]) + before[rows, :].astype(F32)
        message[rows, :] = silu(pre).astype(BF16)

    def put(index, value):
        out[pl.ds(index * HALF, HALF), :] = value.astype(out.dtype)

    scatter(live_targets(targets, live, offset, columns), message, total, out.shape[0], put)


def final_kernel(meta, own, self_term, sum_own, sum_other, w3, out):
    for start in range(0, own.shape[0], HALF):
        rows = pl.ds(start, HALF)
        summed = (sum_own[rows, :].astype(F32) + sum_other[rows, :].astype(F32)).astype(BF16)
        step = silu(self_term[rows, :] + dot(summed, w3[...]))
        out[rows, :] = (own[rows, :].astype(F32) + step).astype(BF16)


def body(
    grid_latent,
    mesh_latent,
    encode_weights,
    layer_weights,
    decode_weights,
    encode_senders,
    encode_targets,
    encode_live,
    mesh_senders,
    mesh_live,
    decode_senders,
    decode_targets,
    decode_live,
):
    band = lax.axis_index("band")
    meta = jnp.stack([lax.axis_index("feat"), band, band % 2, band // 2 % 2]).astype(I32)
    grid_rows, cols = grid_latent.shape
    mesh_rows = mesh_latent.shape[0]
    full = 2 * cols
    senders, targets, live = (x.transpose(1, 0, 2) for x in (encode_senders, encode_targets, encode_live))
    slots = senders.shape[2]

    grid_other = swap(grid_latent)
    encode_other = swap(encode_weights)
    mesh_other = swap(mesh_latent)
    (begun,) = call(
        encode_begin_kernel,
        "encode_begin",
        (meta, grid_latent, encode_weights),
        [SMEM, whole(grid_latent), part(encode_weights, 0)],
        [shape(grid_rows, cols, dtype=F32)],
        2 * grid_rows * cols * cols,
    )
    operands = (meta, grid_latent, grid_other, begun, encode_weights, encode_other, senders)
    sent, far_piece = call(
        encode_far_kernel,
        "encode_far",
        operands,
        [SMEM] + [whole(x) for x in operands[1:4]]
        + [part(encode_weights, 0), part(encode_other, 0), whole(senders)],
        [shape(grid_rows, full), shape(slots, full)],
        2 * full * (grid_rows * full + slots * grid_rows),
    )
    far_rows = exchange(far_piece, far_pairs)
    layer_other = swap(after(layer_weights, far_piece))
    operands = (
        meta, mesh_latent, mesh_other, encode_weights, encode_other, encode_weights, encode_other,
        sent, senders, targets, live,
    )
    line_piece, total, before_line, before_far, self_term = call(
        encode_line_kernel,
        "encode_line",
        operands,
        [SMEM, whole(mesh_latent), whole(mesh_other)]
        + [part(operands[3 + i], 1 + i // 2) for i in range(4)]
        + [whole(x) for x in operands[7:]],
        [
            shape(slots, full),
            shape(mesh_rows, full, dtype=F32),
            shape(slots, full),
            shape(slots, full),
            shape(HALF, full, dtype=F32),
        ],
        2 * full * mesh_rows * (full + 5 * slots),
        [pltpu.VMEM((mesh_rows, full), BF16), pltpu.VMEM((HALF, full), BF16)],
    )
    line_rows = exchange(line_piece, line_pairs)
    operands = (meta, far_rows, before_far, targets, live, total)
    (total,) = call(
        encode_far_sum_kernel,
        "encode_far_sum",
        operands,
        [SMEM] + [whole(x) for x in operands[1:]],
        [shape(mesh_rows, full, dtype=F32)],
        2 * full * mesh_rows * slots,
        [pltpu.VMEM((slots, full), BF16)],
    )
    operands = (meta, line_rows, before_line, targets, live, total)
    sum_own, sum_other = call(
        encode_line_sum_kernel,
        "encode_line_sum",
        operands,
        [SMEM] + [whole(x) for x in operands[1:]],
        [shape(HALF, full, dtype=F32), shape(HALF, full)],
        2 * full * mesh_rows * slots,
        [pltpu.VMEM((slots, full), BF16)],
    )
    operands = (
        meta, mesh_latent, mesh_other, self_term, sum_own, swap(sum_other),
        encode_weights, encode_other, layer_weights, layer_other,
    )
    now, edge = call(
        encode_update_kernel,
        "encode_update",
        operands,
        [SMEM] + [whole(x) for x in operands[1:6]]
        + [part(encode_weights, 3), part(encode_other, 3)]
        + [part(layer_weights, 0, 0), part(layer_other, 0, 0)],
        [shape(HALF, full), shape(MARGIN, full)],
        2 * HALF * full * full,
    )

    decode_other = swap(after(decode_weights, now))
    senders_t, live_t = mesh_senders.T, mesh_live.T
    degree = senders_t.shape[0]
    for layer in range(LAYERS):
        last = layer == LAYERS - 1
        far = exchange(edge, halo_shift)
        near = exchange(edge, halo_pairs)
        now_other = swap(now)
        operands = (meta, now, now_other) + (layer_weights, layer_other) * 3
        results = call(
            functools.partial(layer_project_kernel, last),
            f"layer_project_{layer}",
            operands,
            [SMEM, whole(now), whole(now_other)]
            + [part(operands[3 + i], layer, i // 2) for i in range(6)],
            [shape(HALF, full)] * 2 + [shape(HALF, full, dtype=F32)] * (3 if last else 2),
            2 * HALF * full * full * 4,
        )
        sent_own, sent_other, recv, self_own = results[:4]
        operands = (meta, sent_own, sent_other, senders_t)
        (gathered,) = call(
            layer_gather_kernel,
            f"layer_gather_{layer}",
            operands,
            [SMEM] + [whole(x) for x in operands[1:]],
            [shape(degree, HALF, full)],
            2 * degree * HALF * full * mesh_rows,
        )
        operands = (meta, gathered, recv, far, near, senders_t, live_t)
        scratch = [pltpu.VMEM((2 * MARGIN, full), BF16), pltpu.VMEM((HALF, full), F32)]
        if last:
            (summed,) = call(
                layer_sum_kernel,
                f"layer_sum_{layer}",
                operands,
                [SMEM] + [whole(x) for x in operands[1:]],
                [shape(HALF, full)],
                2 * degree * HALF * full * 2 * MARGIN,
                scratch,
            )
            continue
        operands += (now, self_own) + (layer_weights, layer_other) * 2
        now, edge = call(
            layer_update_kernel,
            f"layer_update_{layer}",
            operands,
            [SMEM] + [whole(x) for x in operands[1:9]]
            + [part(layer_weights, layer, 3), part(layer_other, layer, 3)]
            + [part(layer_weights, layer + 1, 0), part(layer_other, layer + 1, 0)],
            [shape(HALF, full), shape(MARGIN, full)],
            2 * HALF * full * (degree * 2 * MARGIN + full),
            scratch,
        )
    operands = (
        meta, now, now_other, self_own, results[4], summed, swap(summed),
        layer_weights, layer_other, decode_weights, decode_other,
    )
    mesh_now, sent = call(
        last_update_kernel,
        "last_update",
        operands,
        [SMEM] + [whole(x) for x in operands[1:7]]
        + [part(layer_weights, LAYERS - 1, 3), part(layer_other, LAYERS - 1, 3)]
        + [part(decode_weights, 0), part(decode_other, 0)],
        [shape(mesh_rows, cols), shape(mesh_rows, full)],
        2 * mesh_rows * full * full * 2,
        [pltpu.VMEM((HALF, full), BF16)],
    )

    far_rows = exchange(sent, far_pairs)
    line_rows = exchange(sent, line_pairs)
    senders, targets, live = (x.transpose(1, 0, 2) for x in (decode_senders, decode_targets, decode_live))
    slots = senders.shape[2]
    operands = (
        meta, grid_latent, grid_other, decode_weights, decode_other, decode_weights, targets
    )
    before_own, before_line, before_far, self_term = call(
        decode_prepare_kernel,
        "decode_prepare",
        operands,
        [SMEM, whole(grid_latent), whole(grid_other)]
        + [part(decode_weights, 1), part(decode_other, 1), part(decode_weights, 2), whole(targets)],
        [
            shape(slots // 2, full),
            shape(slots, full),
            shape(slots, full),
            shape(grid_rows, cols, dtype=F32),
        ],
        2 * full * grid_rows * (full + 5 * slots // 2),
        [pltpu.VMEM((grid_rows, full), BF16)],
    )
    total = None
    for kind, rows, before in (
        ("own", sent, before_own),
        ("far", far_rows, before_far),
        ("line", line_rows, before_line),
    ):
        operands = (meta, rows, before, senders, targets, live)
        if total is not None:
            operands += (total,)
        (total,) = call(
            functools.partial(decode_sum_kernel, kind),
            f"decode_{kind}",
            operands,
            [SMEM] + [whole(x) for x in operands[1:]],
            [shape(grid_rows, full, dtype=BF16 if kind == "line" else F32)],
            2 * full * before.shape[0] * (grid_rows + mesh_rows),
            [pltpu.VMEM(before.shape, BF16)],
        )
    operands = (meta, grid_latent, self_term, total, swap(total), decode_weights)
    (grid_now,) = call(
        final_kernel,
        "final_update",
        operands,
        [SMEM] + [whole(x) for x in operands[1:5]] + [part(decode_weights, 3)],
        [shape(grid_rows, cols)],
        2 * full * grid_rows * cols,
    )
    return mesh_now, grid_now


def solution(mesh):
    placed = (
        P("band", "feat"),
        P("band", "feat"),
        P(None, None, "feat"),
        P(None, None, None, "feat"),
        P(None, None, "feat"),
        P("band", None, None),
        P("band", None, None),
        P("band", None, None),
        P("band", None),
        P("band", None),
        P("band", None, None),
        P("band", None, None),
        P("band", None, None),
    )
    return jax.shard_map(
        body,
        mesh=mesh,
        in_specs=placed,
        out_specs=(P("band", "feat"), P("band", "feat")),
        check_vma=False,
    )
```

```python
import functools

import jax
import jax.numpy as jnp
from jax import lax
from jax.experimental import pallas as pl
from jax.experimental.pallas import tpu as pltpu
from jax.sharding import PartitionSpec as P

REACH = 2
LAYERS = 2
MARGIN = 64
HALF = 256
LANES = 128
F32 = jnp.float32
BF16 = jnp.bfloat16
I32 = jnp.int32
VMEM_LIMIT = 36 * 1024 * 1024


def swap(value):
    return lax.ppermute(value, "feat", [(0, 1), (1, 0)])


def flat(partners):
    return [(2 * s + c, 2 * t + e) for (s, c), (t, e) in partners.items()]


def shift(steps, up, count):
    partners = {}
    for s in range(count):
        partners[s, up] = (s + steps, up) if s + steps < count else (s, 1 - up)
        partners[s, 1 - up] = (s - steps, 1 - up) if s >= steps else (s, up)
    return flat(partners)


near_shift = functools.partial(shift, 1, 0)
skip_shift = functools.partial(shift, 2, 0)
halo_shift = functools.partial(shift, 1, 1)


def halo_pairs(count):
    partners = {}
    for s in range(count):
        partners[s, 1] = ((s + 1) % count, 0)
        partners[(s + 1) % count, 0] = (s, 1)
    return flat(partners)


def exchange(value, pairs):
    return lax.ppermute(value, ("band", "feat"), pairs(lax.axis_size("band")))


def after(value, other):
    return lax.optimization_barrier((value, other))[0]


def silu(v):
    half = 0.5 * v
    return half + half * jnp.tanh(half)


def dot(a, b):
    return jnp.dot(a, b, preferred_element_type=F32)


def window(index, size=HALF):
    return pl.ds(pl.multiple_of(index * size, size), size)


def near_offset(meta):
    return 3 - 2 * meta[0]


def skip_offset(meta):
    return 4 - 4 * meta[0]


def column(row):
    parts = [
        jnp.broadcast_to(row[:, start : start + LANES], (LANES, LANES)).T
        for start in range(0, row.shape[1], LANES)
    ]
    return parts[0] if len(parts) == 1 else jnp.concatenate(parts, axis=0)


def hot_columns(col, width):
    ids = lax.broadcasted_iota(I32, col.shape, 1)
    parts = [
        jnp.where(col == ids + start, 1.0, 0.0).astype(BF16) for start in range(0, width, LANES)
    ]
    return parts[0] if len(parts) == 1 else jnp.concatenate(parts, axis=1)


def hot_rows(row, height):
    ids = lax.broadcasted_iota(I32, (height, row.shape[1]), 0)
    return jnp.where(row == ids, 1.0, 0.0).astype(BF16)


def call(kernel, name, operands, specs, outs, flops, scratch=()):
    size = sum(x.size * x.dtype.itemsize for x in outs)
    return pl.pallas_call(
        kernel,
        name=name,
        grid=(1,),
        in_specs=specs,
        out_specs=[whole(x) for x in outs],
        out_shape=list(outs),
        scratch_shapes=list(scratch),
        compiler_params=pltpu.CompilerParams(vmem_limit_bytes=VMEM_LIMIT),
        cost_estimate=pl.CostEstimate(flops=flops // 64, bytes_accessed=size // 64, transcendentals=0),
    )(*operands)


def whole(x):
    return pl.BlockSpec(x.shape, lambda i, n=len(x.shape): (0,) * n)


def part(x, *index):
    lead = len(index)
    rest = x.shape[lead:]
    return pl.BlockSpec((None,) * lead + rest, lambda i, where=index + (0,) * len(rest): where)


SMEM = pl.BlockSpec(memory_space=pltpu.SMEM)


def shape(*dims, dtype=BF16):
    return jax.ShapeDtypeStruct(dims, dtype)


def encode_begin_kernel(meta, own, w_own, out):
    for start in range(0, own.shape[0], HALF):
        rows = pl.ds(start, HALF)
        out[rows, :] = dot(own[rows, :], w_own[window(meta[0]), :])


def gather_slots(senders_row, sent, out):
    for start in range(0, senders_row.shape[1], HALF):
        col = column(senders_row[:, start : start + HALF])
        out[pl.ds(start, HALF), :] = dot(hot_columns(col, sent.shape[0]), sent[...]).astype(BF16)


def encode_near_kernel(meta, own, other, begun, w_own, w_other, senders, sent, piece):
    mine, rest = window(meta[0]), window(1 - meta[0])
    for start in range(0, own.shape[0], HALF):
        rows = pl.ds(start, HALF)
        a, b = own[rows, :], other[rows, :]
        sent[rows, mine] = (begun[rows, :] + dot(b, w_own[rest, :])).astype(BF16)
        sent[rows, rest] = (dot(a, w_other[mine, :]) + dot(b, w_other[rest, :])).astype(BF16)
    gather_slots(senders[near_offset(meta)], sent, piece)


def live_targets(targets, live, offset, columns=slice(None)):
    return jnp.where(live[offset, :, columns] > 0, targets[offset, :, columns], -1)


def encode_skip_kernel(
    meta, own, other, w1, w1_other, sent, senders, targets, piece, recv, before
):
    gather_slots(senders[skip_offset(meta)], sent, piece)
    mine, rest = window(meta[0]), window(1 - meta[0])
    for start in range(0, own.shape[0], HALF):
        rows = pl.ds(start, HALF)
        a, b = own[rows, :], other[rows, :]
        recv[rows, mine] = (dot(a, w1[mine, :]) + dot(b, w1[rest, :])).astype(BF16)
        recv[rows, rest] = (dot(a, w1_other[mine, :]) + dot(b, w1_other[rest, :])).astype(BF16)
    gather_slots(targets[near_offset(meta)], recv, before)


def encode_near_sum_kernel(
    meta, rows, before, recv, sent, own, other, w2, w2_other, senders, targets, live,
    total, before_skip, self_term, message, own_message,
):
    mine, rest = window(meta[0]), window(1 - meta[0])
    nodes = recv.shape[0]
    message[...] = silu(rows[...].astype(F32) + before[...].astype(F32)).astype(BF16)
    from_rows = hot_columns(column(senders[REACH, :, mine]), sent.shape[0])
    to_rows = hot_columns(column(targets[REACH, :, mine]), nodes)
    own_message[...] = silu(dot(from_rows, sent[...]) + dot(to_rows, recv[...])).astype(BF16)
    row = live_targets(targets, live, near_offset(meta))
    own_row = live_targets(targets, live, REACH, mine)
    for start in range(0, nodes, HALF):
        value = dot(hot_rows(row - start, HALF), message[...])
        value = value + dot(hot_rows(own_row - start, HALF), own_message[...])
        total[pl.ds(start, HALF), :] = value
    gather_slots(targets[skip_offset(meta)], recv, before_skip)
    a, b = own[mine, :], other[mine, :]
    self_term[:, mine] = dot(a, w2[mine, :]) + dot(b, w2[rest, :])
    self_term[:, rest] = dot(a, w2_other[mine, :]) + dot(b, w2_other[rest, :])


def encode_skip_sum_kernel(meta, rows, before, targets, live, total, out_own, out_other, message):
    message[...] = silu(rows[...].astype(F32) + before[...].astype(F32)).astype(BF16)
    row = live_targets(targets, live, skip_offset(meta))
    for out, half in ((out_other, 1 - meta[0]), (out_own, meta[0])):
        value = dot(hot_rows(row - half * HALF, HALF), message[...]) + total[window(half), :]
        out[...] = value.astype(out.dtype)


def put_edge(meta, now, w0, w0_other, edge):
    mine, rest = window(meta[0]), window(1 - meta[0])
    rows = now[pl.ds(pl.multiple_of(meta[0] * (HALF - MARGIN), MARGIN), MARGIN), :]
    edge[:, mine] = dot(rows, w0[...]).astype(BF16)
    edge[:, rest] = dot(rows, w0_other[...]).astype(BF16)


def encode_update_kernel(
    meta, own, other, self_term, sum_own, sum_other, w3, w3_other, w0, w0_other, now, edge
):
    mine, rest = window(meta[0]), window(1 - meta[0])
    summed = (sum_own[...] + sum_other[...].astype(F32)).astype(BF16)
    for cols, latent, w in ((mine, own, w3), (rest, other, w3_other)):
        step = silu(self_term[:, cols] + dot(summed, w[...]))
        now[:, cols] = (latent[mine, :].astype(F32) + step).astype(BF16)
    put_edge(meta, now, w0, w0_other, edge)


def layer_project_kernel(
    last, meta, own, other, w0, w0_other, w1, w1_other, w2, w2_other,
    sent_own, sent_other, recv, self_own, *self_other,
):
    mine, rest = window(meta[0]), window(1 - meta[0])
    for cols, w in ((mine, w0), (rest, w0_other)):
        sent_own[:, cols] = dot(own[...], w[...]).astype(BF16)
        sent_other[:, cols] = dot(other[...], w[...]).astype(BF16)
    for cols, w in ((mine, w1), (rest, w1_other)):
        recv[:, cols] = dot(own[...], w[...])
    for cols, w in ((mine, w2), (rest, w2_other)):
        self_own[:, cols] = dot(own[...], w[...])
        if last:
            self_other[0][:, cols] = dot(other[...], w[...])


def layer_gather_kernel(meta, own, other, senders, out):
    mine = window(meta[0])
    base = meta[1] * (2 * HALF)
    for k in range(senders.shape[0]):
        local = senders[k : k + 1, mine] - base
        col = column(local - meta[0] * HALF)
        col_other = column(local - (1 - meta[0]) * HALF)
        value = dot(hot_columns(col, HALF), own[...])
        value = value + dot(hot_columns(col_other, HALF), other[...])
        out[k] = value.astype(BF16)


def layer_sum(meta, gathered, recv, far, near, senders, live, halo, total):
    mine = window(meta[0])
    nodes = 2 * HALF
    base = meta[1] * nodes
    halo[pl.ds(pl.multiple_of(meta[0] * MARGIN, MARGIN), MARGIN), :] = near[...]
    halo[pl.ds(pl.multiple_of((1 - meta[0]) * MARGIN, MARGIN), MARGIN), :] = far[...]
    count = senders.shape[0]
    for k in range(count):
        local = senders[k : k + 1, mine] - base
        where = jnp.where(local < 0, local + MARGIN, local - nodes + MARGIN)
        where = jnp.where((local >= 0) & (local < nodes), -1, where)
        flags = column(live[k : k + 1, mine]).astype(F32)
        flags = jnp.concatenate([flags] * (recv.shape[1] // LANES), axis=1)
        pre = dot(hot_columns(column(where), 2 * MARGIN), halo[...])
        pre = pre + gathered[k].astype(F32) + recv[...]
        message = (silu(pre) * flags).astype(BF16).astype(F32)
        total[...] = message if k == 0 else total[...] + message
    return total[...].astype(BF16)


def layer_update_kernel(
    meta, gathered, recv, far, near, senders, live, now, self_term, w3, w3_other, w0, w0_other,
    out, edge, halo, total,
):
    mine, rest = window(meta[0]), window(1 - meta[0])
    summed = layer_sum(meta, gathered, recv, far, near, senders, live, halo, total)
    for cols, w in ((mine, w3), (rest, w3_other)):
        step = silu(self_term[:, cols] + dot(summed, w[...]))
        out[:, cols] = (now[:, cols].astype(F32) + step).astype(BF16)
    put_edge(meta, out, w0, w0_other, edge)


def layer_sum_kernel(meta, gathered, recv, far, near, senders, live, out, halo, total):
    out[...] = layer_sum(meta, gathered, recv, far, near, senders, live, halo, total)


def last_update_kernel(
    meta, now_own, now_other, self_own, self_other, sum_own, sum_other, w3, w3_other,
    w0, w0_other, out, sent, now,
):
    mine, rest = window(meta[0]), window(1 - meta[0])
    for rows, latent, self_term, summed in (
        (mine, now_own, self_own, sum_own),
        (rest, now_other, self_other, sum_other),
    ):
        for cols, w in ((mine, w3), (rest, w3_other)):
            step = silu(self_term[:, cols] + dot(summed[...], w[...]))
            now[:, cols] = (latent[:, cols].astype(F32) + step).astype(BF16)
        out[rows, :] = now[:, mine]
        for cols, w in ((mine, w0), (rest, w0_other)):
            sent[rows, cols] = dot(now[...], w[...]).astype(BF16)


def decode_prepare_kernel(
    meta, own, other, w1, w1_other, w2, targets,
    before_own, before_near, before_skip, self_term, recv,
):
    mine, rest = window(meta[0]), window(1 - meta[0])
    for start in range(0, own.shape[0], HALF):
        rows = pl.ds(start, HALF)
        a, b = own[rows, :], other[rows, :]
        recv[rows, mine] = (dot(a, w1[mine, :]) + dot(b, w1[rest, :])).astype(BF16)
        recv[rows, rest] = (dot(a, w1_other[mine, :]) + dot(b, w1_other[rest, :])).astype(BF16)
        self_term[rows, :] = dot(a, w2[mine, :]) + dot(b, w2[rest, :])
    half = before_own.shape[0]
    gather_slots(targets[REACH, :, window(meta[0], half)], recv, before_own)
    gather_slots(targets[near_offset(meta)], recv, before_near)
    gather_slots(targets[skip_offset(meta)], recv, before_skip)


def decode_sum_kernel(kind, meta, sent, before, senders, targets, live, *refs):
    total, out, message = refs if kind != "own" else (None,) + refs
    slots = before.shape[0]
    if kind == "own":
        offset, columns = REACH, window(meta[0], slots)
    else:
        offset = (near_offset if kind == "near" else skip_offset)(meta)
        columns = slice(None)
    from_row = senders[offset, :, columns]
    for start in range(0, slots, HALF):
        rows = pl.ds(start, HALF)
        hot = hot_columns(column(from_row[:, start : start + HALF]), sent.shape[0])
        pre = dot(hot, sent[...]) + before[rows, :].astype(F32)
        message[rows, :] = silu(pre).astype(BF16)

    row = live_targets(targets, live, offset, columns)
    for start in range(0, out.shape[0], HALF):
        nodes = pl.ds(start, HALF)
        value = dot(hot_rows(row - start, HALF), message[...])
        if total is not None:
            value = value + total[nodes, :]
        out[nodes, :] = value.astype(out.dtype)


def final_kernel(meta, own, self_term, sum_own, sum_other, w3, out):
    for start in range(0, own.shape[0], HALF):
        rows = pl.ds(start, HALF)
        summed = (sum_own[rows, :].astype(F32) + sum_other[rows, :].astype(F32)).astype(BF16)
        step = silu(self_term[rows, :] + dot(summed, w3[...]))
        out[rows, :] = (own[rows, :].astype(F32) + step).astype(BF16)


def body(
    grid_latent,
    mesh_latent,
    encode_weights,
    layer_weights,
    decode_weights,
    encode_senders,
    encode_targets,
    encode_live,
    mesh_senders,
    mesh_live,
    decode_senders,
    decode_targets,
    decode_live,
):
    meta = jnp.stack([lax.axis_index("feat"), lax.axis_index("band")]).astype(I32)
    grid_rows, cols = grid_latent.shape
    mesh_rows = mesh_latent.shape[0]
    full = 2 * cols
    senders, targets, live = (x.transpose(1, 0, 2) for x in (encode_senders, encode_targets, encode_live))
    slots = senders.shape[2]

    grid_other = swap(grid_latent)
    encode_other = swap(encode_weights)
    mesh_other = swap(mesh_latent)
    (begun,) = call(
        encode_begin_kernel,
        "encode_begin",
        (meta, grid_latent, encode_weights),
        [SMEM, whole(grid_latent), part(encode_weights, 0)],
        [shape(grid_rows, cols, dtype=F32)],
        2 * grid_rows * cols * cols,
    )
    operands = (meta, grid_latent, grid_other, begun, encode_weights, encode_other, senders)
    sent, near_piece = call(
        encode_near_kernel,
        "encode_near",
        operands,
        [SMEM] + [whole(x) for x in operands[1:4]]
        + [part(encode_weights, 0), part(encode_other, 0), whole(senders)],
        [shape(grid_rows, full), shape(slots, full)],
        2 * full * (grid_rows * full + slots * grid_rows),
    )
    near_rows = exchange(near_piece, near_shift)
    layer_other = swap(after(layer_weights, near_piece))
    operands = (
        meta, mesh_latent, mesh_other, encode_weights, encode_other, sent, senders, targets
    )
    skip_piece, recv, before_near = call(
        encode_skip_kernel,
        "encode_skip",
        operands,
        [SMEM, whole(mesh_latent), whole(mesh_other)]
        + [part(encode_weights, 1), part(encode_other, 1)]
        + [whole(x) for x in operands[5:]],
        [shape(slots, full), shape(mesh_rows, full), shape(slots, full)],
        2 * full * (mesh_rows * full + slots * (grid_rows + mesh_rows)),
    )
    skip_rows = exchange(skip_piece, skip_shift)
    operands = (
        meta, near_rows, before_near, recv, sent, mesh_latent, mesh_other,
        encode_weights, encode_other, senders, targets, live,
    )
    total, before_skip, self_term = call(
        encode_near_sum_kernel,
        "encode_near_sum",
        operands,
        [SMEM] + [whole(x) for x in operands[1:7]]
        + [part(encode_weights, 2), part(encode_other, 2)]
        + [whole(x) for x in operands[9:]],
        [
            shape(mesh_rows, full, dtype=F32),
            shape(slots, full),
            shape(HALF, full, dtype=F32),
        ],
        2 * full * mesh_rows * slots * 3,
        [pltpu.VMEM((slots, full), BF16), pltpu.VMEM((HALF, full), BF16)],
    )
    operands = (meta, skip_rows, before_skip, targets, live, total)
    sum_own, sum_other = call(
        encode_skip_sum_kernel,
        "encode_skip_sum",
        operands,
        [SMEM] + [whole(x) for x in operands[1:]],
        [shape(HALF, full, dtype=F32), shape(HALF, full)],
        2 * full * mesh_rows * slots,
        [pltpu.VMEM((slots, full), BF16)],
    )
    operands = (
        meta, mesh_latent, mesh_other, self_term, sum_own, swap(sum_other),
        encode_weights, encode_other, layer_weights, layer_other,
    )
    now, edge = call(
        encode_update_kernel,
        "encode_update",
        operands,
        [SMEM] + [whole(x) for x in operands[1:6]]
        + [part(encode_weights, 3), part(encode_other, 3)]
        + [part(layer_weights, 0, 0), part(layer_other, 0, 0)],
        [shape(HALF, full), shape(MARGIN, full)],
        2 * HALF * full * full,
    )

    decode_other = swap(after(decode_weights, now))
    senders_t, live_t = mesh_senders.T, mesh_live.T
    degree = senders_t.shape[0]
    for layer in range(LAYERS):
        last = layer == LAYERS - 1
        far = exchange(edge, halo_shift)
        near = exchange(edge, halo_pairs)
        now_other = swap(now)
        operands = (meta, now, now_other) + (layer_weights, layer_other) * 3
        results = call(
            functools.partial(layer_project_kernel, last),
            f"layer_project_{layer}",
            operands,
            [SMEM, whole(now), whole(now_other)]
            + [part(operands[3 + i], layer, i // 2) for i in range(6)],
            [shape(HALF, full)] * 2 + [shape(HALF, full, dtype=F32)] * (3 if last else 2),
            2 * HALF * full * full * 4,
        )
        sent_own, sent_other, recv, self_own = results[:4]
        operands = (meta, sent_own, sent_other, senders_t)
        (gathered,) = call(
            layer_gather_kernel,
            f"layer_gather_{layer}",
            operands,
            [SMEM] + [whole(x) for x in operands[1:]],
            [shape(degree, HALF, full)],
            2 * degree * HALF * full * mesh_rows,
        )
        operands = (meta, gathered, recv, far, near, senders_t, live_t)
        scratch = [pltpu.VMEM((2 * MARGIN, full), BF16), pltpu.VMEM((HALF, full), F32)]
        if last:
            (summed,) = call(
                layer_sum_kernel,
                f"layer_sum_{layer}",
                operands,
                [SMEM] + [whole(x) for x in operands[1:]],
                [shape(HALF, full)],
                2 * degree * HALF * full * 2 * MARGIN,
                scratch,
            )
            continue
        operands += (now, self_own) + (layer_weights, layer_other) * 2
        now, edge = call(
            layer_update_kernel,
            f"layer_update_{layer}",
            operands,
            [SMEM] + [whole(x) for x in operands[1:9]]
            + [part(layer_weights, layer, 3), part(layer_other, layer, 3)]
            + [part(layer_weights, layer + 1, 0), part(layer_other, layer + 1, 0)],
            [shape(HALF, full), shape(MARGIN, full)],
            2 * HALF * full * (degree * 2 * MARGIN + full),
            scratch,
        )
    operands = (
        meta, now, now_other, self_own, results[4], summed, swap(summed),
        layer_weights, layer_other, decode_weights, decode_other,
    )
    mesh_now, sent = call(
        last_update_kernel,
        "last_update",
        operands,
        [SMEM] + [whole(x) for x in operands[1:7]]
        + [part(layer_weights, LAYERS - 1, 3), part(layer_other, LAYERS - 1, 3)]
        + [part(decode_weights, 0), part(decode_other, 0)],
        [shape(mesh_rows, cols), shape(mesh_rows, full)],
        2 * mesh_rows * full * full * 2,
        [pltpu.VMEM((HALF, full), BF16)],
    )

    near_rows = exchange(sent, near_shift)
    skip_rows = exchange(sent, skip_shift)
    senders, targets, live = (x.transpose(1, 0, 2) for x in (decode_senders, decode_targets, decode_live))
    slots = senders.shape[2]
    operands = (
        meta, grid_latent, grid_other, decode_weights, decode_other, decode_weights, targets
    )
    before_own, before_near, before_skip, self_term = call(
        decode_prepare_kernel,
        "decode_prepare",
        operands,
        [SMEM, whole(grid_latent), whole(grid_other)]
        + [part(decode_weights, 1), part(decode_other, 1), part(decode_weights, 2), whole(targets)],
        [
            shape(slots // 2, full),
            shape(slots, full),
            shape(slots, full),
            shape(grid_rows, cols, dtype=F32),
        ],
        2 * full * grid_rows * (full + 5 * slots // 2),
        [pltpu.VMEM((grid_rows, full), BF16)],
    )
    total = None
    for kind, rows, before in (
        ("own", sent, before_own),
        ("near", near_rows, before_near),
        ("skip", skip_rows, before_skip),
    ):
        operands = (meta, rows, before, senders, targets, live)
        if total is not None:
            operands += (total,)
        (total,) = call(
            functools.partial(decode_sum_kernel, kind),
            f"decode_{kind}",
            operands,
            [SMEM] + [whole(x) for x in operands[1:]],
            [shape(grid_rows, full, dtype=BF16 if kind == "skip" else F32)],
            2 * full * before.shape[0] * (grid_rows + mesh_rows),
            [pltpu.VMEM(before.shape, BF16)],
        )
    operands = (meta, grid_latent, self_term, total, swap(total), decode_weights)
    (grid_now,) = call(
        final_kernel,
        "final_update",
        operands,
        [SMEM] + [whole(x) for x in operands[1:5]] + [part(decode_weights, 3)],
        [shape(grid_rows, cols)],
        2 * full * grid_rows * cols,
    )
    return mesh_now, grid_now


def solution(mesh):
    placed = (
        P("band", "feat"),
        P("band", "feat"),
        P(None, None, "feat"),
        P(None, None, None, "feat"),
        P(None, None, "feat"),
        P("band", None, None),
        P("band", None, None),
        P("band", None, None),
        P("band", None),
        P("band", None),
        P("band", None, None),
        P("band", None, None),
        P("band", None, None),
    )
    return jax.shard_map(
        body,
        mesh=mesh,
        in_specs=placed,
        out_specs=(P("band", "feat"), P("band", "feat")),
        check_vma=False,
    )
```

```python
import functools

import jax
import jax.numpy as jnp
from jax import lax
from jax.experimental import pallas as pl
from jax.experimental.pallas import tpu as pltpu
from jax.sharding import PartitionSpec as P

REACH = 2
LAYERS = 2
MARGIN = 64
HALF = 256
LANES = 128
F32 = jnp.float32
BF16 = jnp.bfloat16
I32 = jnp.int32
VMEM_LIMIT = 36 * 1024 * 1024


def swap(value):
    return lax.ppermute(value, "feat", [(0, 1), (1, 0)])


def flat(partners):
    return [(2 * s + c, 2 * t + e) for (s, c), (t, e) in partners.items()]


def shift(steps, up, count):
    partners = {}
    for s in range(count):
        partners[s, up] = (s + steps, up) if s + steps < count else (s, 1 - up)
        partners[s, 1 - up] = (s - steps, 1 - up) if s >= steps else (s, up)
    return flat(partners)


near_shift = functools.partial(shift, 1, 0)
skip_shift = functools.partial(shift, 2, 0)
halo_shift = functools.partial(shift, 1, 1)


def halo_pairs(count):
    partners = {}
    for s in range(count):
        partners[s, 1] = ((s + 1) % count, 0)
        partners[(s + 1) % count, 0] = (s, 1)
    return flat(partners)


def exchange(value, pairs):
    return lax.ppermute(value, ("band", "feat"), pairs(lax.axis_size("band")))


def after(value, other):
    return lax.optimization_barrier((value, other))[0]


def silu(v):
    half = 0.5 * v
    return half + half * jnp.tanh(half)


def silu_message(v):
    half = v.astype(BF16) * BF16(0.5)
    return half + half * jnp.tanh(half)


def dot(a, b):
    return jnp.dot(a, b, preferred_element_type=F32)


def window(index, size=HALF):
    return pl.ds(pl.multiple_of(index * size, size), size)


def near_offset(meta):
    return 3 - 2 * meta[0]


def skip_offset(meta):
    return 4 - 4 * meta[0]


def column(row):
    parts = [
        jnp.broadcast_to(row[:, start : start + LANES], (LANES, LANES)).T
        for start in range(0, row.shape[1], LANES)
    ]
    return parts[0] if len(parts) == 1 else jnp.concatenate(parts, axis=0)


def hot_columns(col, width):
    col = col.astype(jnp.int16)
    ids = lax.broadcasted_iota(I32, col.shape, 1).astype(jnp.int16)
    one, zero = BF16(1), BF16(0)
    parts = [
        jnp.where(col == ids + jnp.int16(start), one, zero) for start in range(0, width, LANES)
    ]
    return parts[0] if len(parts) == 1 else jnp.concatenate(parts, axis=1)


def hot_rows(row, height):
    ids = lax.broadcasted_iota(I32, (height, row.shape[1]), 0)
    return jnp.where(row == ids, 1.0, 0.0).astype(BF16)


class Fetch:
    def __init__(self, index=(), axis=None, size=None):
        self.index, self.axis, self.size = index, axis, size

    def block(self, operand):
        return operand.shape[len(self.index) :]

    def count(self, operand):
        return 1 if self.axis is None else self.block(operand)[self.axis] // self.size


class Fetched:
    def __init__(self, spec, source, buffer, sems):
        self.buffer, self.shape, self.spec = buffer, buffer.shape, spec
        self.copies = []
        if spec.index:
            source = source.at[spec.index]
        for tile in range(sems.shape[0]):
            where = self.where(tile)
            self.copies.append(
                pltpu.make_async_copy(source.at[where], buffer.at[where], sems.at[tile])
            )
        self.pending = set(range(len(self.copies)))

    def where(self, tile):
        if self.spec.axis is None:
            return (slice(None),) * len(self.shape)
        size = self.spec.size
        return (slice(None),) * self.spec.axis + (pl.ds(tile * size, size),)

    def start(self):
        for copy in self.copies:
            copy.start()

    def wait(self, tile):
        if tile in self.pending:
            self.pending.discard(tile)
            self.copies[tile].wait()

    def finish(self):
        for tile in range(len(self.copies)):
            self.wait(tile)

    def tile(self, tile):
        self.wait(tile)
        return self.buffer[self.where(tile)]

    def __getitem__(self, where):
        self.finish()
        return self.buffer[where]


class Sent:
    def __init__(self, target, buffer, sems):
        self.target, self.buffer, self.sems = target, buffer, sems
        self.shape, self.dtype = target.shape, target.dtype
        self.copies = []

    def put(self, start, value):
        rows = pl.ds(start, value.shape[0])
        self.buffer[rows, :] = value.astype(self.dtype)
        copy = pltpu.make_async_copy(
            self.buffer.at[rows, :], self.target.at[rows, :], self.sems.at[len(self.copies)]
        )
        copy.start()
        self.copies.append(copy)

    def finish(self):
        for copy in self.copies:
            copy.wait()


def call(kernel, name, operands, specs, outs, flops, scratch=(), tiles=0):
    fetches = [isinstance(spec, Fetch) for spec in specs]
    any_space = pl.BlockSpec(memory_space=pl.ANY)
    buffers = list(scratch)
    for x, spec in zip(operands, specs):
        if isinstance(spec, Fetch):
            buffers += [pltpu.VMEM(spec.block(x), x.dtype)]
            buffers += [pltpu.SemaphoreType.DMA((spec.count(x),))]
    if tiles:
        for x in outs:
            buffers += [pltpu.VMEM(x.shape, x.dtype), pltpu.SemaphoreType.DMA((tiles,))]

    def wrapped(*refs):
        refs = list(refs)
        sources, refs = refs[: len(specs)], refs[len(specs) :]
        targets, refs = refs[: len(outs)], refs[len(outs) :]
        own, refs = refs[: len(scratch)], refs[len(scratch) :]
        fetched = []
        for index, spec in enumerate(specs):
            if fetches[index]:
                sources[index] = Fetched(spec, sources[index], refs.pop(0), refs.pop(0))
                sources[index].start()
                fetched.append(sources[index])
        if tiles:
            targets = [Sent(x, refs.pop(0), refs.pop(0)) for x in targets]
        kernel(*sources, *targets, *own)
        for x in fetched + (targets if tiles else []):
            x.finish()

    size = sum(x.size * x.dtype.itemsize for x in outs)
    return pl.pallas_call(
        wrapped,
        name=name,
        grid=(1,),
        in_specs=[any_space if f else spec for f, spec in zip(fetches, specs)],
        out_specs=[any_space if tiles else whole(x) for x in outs],
        out_shape=list(outs),
        scratch_shapes=buffers,
        compiler_params=pltpu.CompilerParams(vmem_limit_bytes=VMEM_LIMIT),
        cost_estimate=pl.CostEstimate(
            flops=flops // 64, bytes_accessed=size // 64, transcendentals=0
        ),
    )(*operands)


def whole(x):
    return pl.BlockSpec(x.shape, lambda i, n=len(x.shape): (0,) * n)


def fetch(x):
    return Fetch()


def part(x, *index):
    return Fetch(index)


def rows_of(size=HALF):
    return Fetch(axis=0, size=size)


SMEM = pl.BlockSpec(memory_space=pltpu.SMEM)


def shape(*dims, dtype=BF16):
    return jax.ShapeDtypeStruct(dims, dtype)


def encode_begin_kernel(meta, own, w_own, out):
    for start in range(0, own.shape[0], HALF):
        rows = pl.ds(start, HALF)
        out[rows, :] = dot(own[rows, :], w_own[window(meta[0]), :])


def gather_slots(senders_row, sent, out):
    for start in range(0, senders_row.shape[1], HALF):
        col = column(senders_row[:, start : start + HALF])
        out[pl.ds(start, HALF), :] = dot(hot_columns(col, sent.shape[0]), sent[...]).astype(BF16)


def encode_near_kernel(meta, own, other, begun, w_own, w_other, senders, sent, piece):
    mine, rest = window(meta[0]), window(1 - meta[0])
    for start in range(0, own.shape[0], HALF):
        rows = pl.ds(start, HALF)
        a, b = own[rows, :], other[rows, :]
        sent[rows, mine] = (begun[rows, :] + dot(b, w_own[rest, :])).astype(BF16)
        sent[rows, rest] = (dot(a, w_other[mine, :]) + dot(b, w_other[rest, :])).astype(BF16)
    gather_slots(senders[near_offset(meta)], sent, piece)


def live_targets(targets, live, offset, columns=slice(None)):
    return jnp.where(live[offset, :, columns] > 0, targets[offset, :, columns], -1)


def encode_skip_kernel(
    meta, own, other, w1, w1_other, sent, senders, targets, piece, recv, before
):
    gather_slots(senders[skip_offset(meta)], sent, piece)
    mine, rest = window(meta[0]), window(1 - meta[0])
    for start in range(0, own.shape[0], HALF):
        rows = pl.ds(start, HALF)
        a, b = own[rows, :], other[rows, :]
        recv[rows, mine] = (dot(a, w1[mine, :]) + dot(b, w1[rest, :])).astype(BF16)
        recv[rows, rest] = (dot(a, w1_other[mine, :]) + dot(b, w1_other[rest, :])).astype(BF16)
    gather_slots(targets[near_offset(meta)], recv, before)


def encode_near_sum_kernel(
    meta, rows, before, recv, sent, own, other, w2, w2_other, senders, targets, live,
    total, before_skip, self_term, message, own_message,
):
    mine, rest = window(meta[0]), window(1 - meta[0])
    nodes = recv.shape[0]
    from_rows = hot_columns(column(senders[REACH, :, mine]), sent.shape[0])
    to_rows = hot_columns(column(targets[REACH, :, mine]), nodes)
    own_message[...] = silu_message(dot(from_rows, sent[...]) + dot(to_rows, recv[...]))
    message[...] = silu_message(rows[...] + before[...])
    row = live_targets(targets, live, near_offset(meta))
    own_row = live_targets(targets, live, REACH, mine)
    for start in range(0, nodes, HALF):
        value = dot(hot_rows(row - start, HALF), message[...])
        value = value + dot(hot_rows(own_row - start, HALF), own_message[...])
        total[pl.ds(start, HALF), :] = value
    gather_slots(targets[skip_offset(meta)], recv, before_skip)
    a, b = own[mine, :], other[mine, :]
    self_term[:, mine] = (dot(a, w2[mine, :]) + dot(b, w2[rest, :])).astype(BF16)
    self_term[:, rest] = (dot(a, w2_other[mine, :]) + dot(b, w2_other[rest, :])).astype(BF16)


def encode_skip_sum_kernel(meta, rows, before, targets, live, total, out_own, out_other, message):
    message[...] = silu_message(rows[...] + before[...])
    row = live_targets(targets, live, skip_offset(meta))
    for out, half in ((out_other, 1 - meta[0]), (out_own, meta[0])):
        value = dot(hot_rows(row - half * HALF, HALF), message[...]) + total[window(half), :]
        out[...] = value.astype(out.dtype)


def put_edge(meta, now, w0, w0_other, edge):
    mine, rest = window(meta[0]), window(1 - meta[0])
    rows = now[pl.ds(pl.multiple_of(meta[0] * (HALF - MARGIN), MARGIN), MARGIN), :]
    edge[:, mine] = dot(rows, w0[...]).astype(BF16)
    edge[:, rest] = dot(rows, w0_other[...]).astype(BF16)


def encode_update_kernel(
    meta, own, other, self_term, sum_own, sum_other, w3, w3_other, w0, w0_other, now, edge
):
    mine, rest = window(meta[0]), window(1 - meta[0])
    summed = (sum_own[...] + sum_other[...].astype(F32)).astype(BF16)
    for cols, latent, w in ((mine, own, w3), (rest, other, w3_other)):
        step = silu(self_term[:, cols] + dot(summed, w[...]))
        now[:, cols] = (latent[mine, :].astype(F32) + step).astype(BF16)
    put_edge(meta, now, w0, w0_other, edge)


def layer_project_kernel(
    last, meta, own, other, w0, w0_other, w1, w1_other, w2, w2_other,
    sent_own, sent_other, recv, self_own, *self_other,
):
    mine, rest = window(meta[0]), window(1 - meta[0])
    for cols, w in ((mine, w0), (rest, w0_other)):
        sent_own[:, cols] = dot(own[...], w[...]).astype(BF16)
        sent_other[:, cols] = dot(other[...], w[...]).astype(BF16)
    for cols, w in ((mine, w1), (rest, w1_other)):
        recv[:, cols] = dot(own[...], w[...]).astype(BF16)
    for cols, w in ((mine, w2), (rest, w2_other)):
        self_own[:, cols] = dot(own[...], w[...]).astype(BF16)
        if last:
            self_other[0][:, cols] = dot(other[...], w[...]).astype(BF16)


def layer_gather_kernel(meta, own, other, senders, out):
    mine = window(meta[0])
    base = meta[1] * (2 * HALF)
    for k in range(senders.shape[0]):
        local = senders[k : k + 1, mine] - base
        col = column(local - meta[0] * HALF)
        col_other = column(local - (1 - meta[0]) * HALF)
        value = dot(hot_columns(col, HALF), own[...])
        value = value + dot(hot_columns(col_other, HALF), other[...])
        out[k] = value.astype(BF16)


def layer_sum(meta, gathered, recv, far, near, senders, live, halo, total):
    mine = window(meta[0])
    nodes = 2 * HALF
    base = meta[1] * nodes
    count = senders.shape[0]
    hots, flags = [], []
    for k in range(count):
        local = senders[k : k + 1, mine] - base
        where = jnp.where(local < 0, local + MARGIN, local - nodes + MARGIN)
        where = jnp.where((local >= 0) & (local < nodes), -1, where)
        hots.append(hot_columns(column(where), 2 * MARGIN))
        flags.append(column(live[k : k + 1, mine]).astype(BF16))
    halo[pl.ds(pl.multiple_of(meta[0] * MARGIN, MARGIN), MARGIN), :] = near[...]
    halo[pl.ds(pl.multiple_of((1 - meta[0]) * MARGIN, MARGIN), MARGIN), :] = far[...]
    outside = dot(jnp.concatenate(hots, axis=0), halo[...]).astype(BF16)
    step = 32
    for start in range(0, HALF, step):
        tile, lead = divmod(start, gathered.spec.size)
        inside = gathered.tile(tile)[:, lead : lead + step, :]
        side = recv[pl.ds(start, step), :]
        running = None
        for k in range(count):
            row = k * HALF + start
            message = silu_message(outside[row : row + step, :] + inside[k] + side)
            flag = jnp.concatenate([flags[k][start : start + step, :]] * 4, axis=1)
            message = (message * flag).astype(F32)
            running = message if running is None else running + message
        total[pl.ds(start, step), :] = running.astype(BF16)


def layer_update_kernel(
    meta, gathered, recv, far, near, senders, live, now, self_term, w3, w3_other, w0, w0_other,
    out, edge, halo, total,
):
    mine, rest = window(meta[0]), window(1 - meta[0])
    layer_sum(meta, gathered, recv, far, near, senders, live, halo, total)
    summed = total[...]
    for cols, w in ((mine, w3), (rest, w3_other)):
        step = silu(self_term[:, cols] + dot(summed, w[...]))
        out[:, cols] = (now[:, cols].astype(F32) + step).astype(BF16)
    put_edge(meta, out, w0, w0_other, edge)


def layer_sum_kernel(meta, gathered, recv, far, near, senders, live, out, halo):
    layer_sum(meta, gathered, recv, far, near, senders, live, halo, out)


def last_update_kernel(
    meta, now_own, now_other, self_own, self_other, sum_own, sum_other, w3, w3_other,
    w0, w0_other, out, sent, now,
):
    mine, rest = window(meta[0]), window(1 - meta[0])
    for rows, latent, self_term, summed in (
        (mine, now_own, self_own, sum_own),
        (rest, now_other, self_other, sum_other),
    ):
        for cols, w in ((mine, w3), (rest, w3_other)):
            step = silu(self_term[:, cols] + dot(summed[...], w[...]))
            now[:, cols] = (latent[:, cols].astype(F32) + step).astype(BF16)
        out[rows, :] = now[:, mine]
        for cols, w in ((mine, w0), (rest, w0_other)):
            sent[rows, cols] = dot(now[...], w[...]).astype(BF16)


def decode_prepare_kernel(
    meta, own, other, w1, w1_other, w2, targets,
    before_own, before_near, before_skip, self_term, recv,
):
    mine, rest = window(meta[0]), window(1 - meta[0])
    for start in range(0, own.shape[0], HALF):
        rows = pl.ds(start, HALF)
        a, b = own[rows, :], other[rows, :]
        recv[rows, mine] = (dot(a, w1[mine, :]) + dot(b, w1[rest, :])).astype(BF16)
        recv[rows, rest] = (dot(a, w1_other[mine, :]) + dot(b, w1_other[rest, :])).astype(BF16)
        self_term[rows, :] = (dot(a, w2[mine, :]) + dot(b, w2[rest, :])).astype(BF16)
    half = before_own.shape[0]
    gather_slots(targets[REACH, :, window(meta[0], half)], recv, before_own)
    gather_slots(targets[near_offset(meta)], recv, before_near)
    gather_slots(targets[skip_offset(meta)], recv, before_skip)


def decode_sum_kernel(kind, meta, sent, before, senders, targets, live, *refs):
    total, out, message = refs if kind != "own" else (None,) + refs
    slots = before.shape[0]
    if kind == "own":
        offset, columns = REACH, window(meta[0], slots)
    else:
        offset = (near_offset if kind == "near" else skip_offset)(meta)
        columns = slice(None)
    from_row = senders[offset, :, columns]
    for start in range(0, slots, HALF):
        hot = hot_columns(column(from_row[:, start : start + HALF]), sent.shape[0])
        pre = dot(hot, sent[...]) + before.tile(start // HALF).astype(F32)
        message[pl.ds(start, HALF), :] = silu_message(pre)
    row = live_targets(targets, live, offset, columns)
    for start in range(0, out.shape[0], HALF):
        value = dot(hot_rows(row - start, HALF), message[...])
        if total is not None:
            value = value + total.tile(start // HALF).astype(F32)
        out.put(start, value)


def final_kernel(meta, own, self_term, sum_own, sum_other, w3, out):
    for start in range(0, own.shape[0], HALF):
        tile = start // HALF
        summed = sum_own.tile(tile).astype(F32) + sum_other.tile(tile).astype(F32)
        step = silu(self_term.tile(tile).astype(F32) + dot(summed.astype(BF16), w3[...]))
        out.put(start, own.tile(tile).astype(F32) + step)


def body(
    grid_latent,
    mesh_latent,
    encode_weights,
    layer_weights,
    decode_weights,
    encode_senders,
    encode_targets,
    encode_live,
    mesh_senders,
    mesh_live,
    decode_senders,
    decode_targets,
    decode_live,
):
    meta = jnp.stack([lax.axis_index("feat"), lax.axis_index("band")]).astype(I32)
    grid_rows, cols = grid_latent.shape
    mesh_rows = mesh_latent.shape[0]
    full = 2 * cols
    senders, targets, live = (x.transpose(1, 0, 2) for x in (encode_senders, encode_targets, encode_live))
    slots = senders.shape[2]

    grid_other = swap(grid_latent)
    encode_other = swap(encode_weights)
    mesh_other = swap(mesh_latent)
    (begun,) = call(
        encode_begin_kernel,
        "encode_begin",
        (meta, grid_latent, encode_weights),
        [SMEM, fetch(grid_latent), part(encode_weights, 0)],
        [shape(grid_rows, cols, dtype=F32)],
        2 * grid_rows * cols * cols,
    )
    operands = (meta, grid_latent, grid_other, begun, encode_weights, encode_other, senders)
    sent, near_piece = call(
        encode_near_kernel,
        "encode_near",
        operands,
        [SMEM] + [fetch(x) for x in operands[1:4]]
        + [part(encode_weights, 0), part(encode_other, 0), whole(senders)],
        [shape(grid_rows, full), shape(slots, full)],
        2 * full * (grid_rows * full + slots * grid_rows),
    )
    near_rows = exchange(near_piece, near_shift)
    layer_other = swap(after(layer_weights, near_piece))
    operands = (
        meta, mesh_latent, mesh_other, encode_weights, encode_other, sent, senders, targets
    )
    skip_piece, recv, before_near = call(
        encode_skip_kernel,
        "encode_skip",
        operands,
        [SMEM, fetch(mesh_latent), fetch(mesh_other)]
        + [part(encode_weights, 1), part(encode_other, 1)]
        + [fetch(sent), whole(senders), whole(targets)],
        [shape(slots, full), shape(mesh_rows, full), shape(slots, full)],
        2 * full * (mesh_rows * full + slots * (grid_rows + mesh_rows)),
    )
    skip_rows = exchange(skip_piece, skip_shift)
    operands = (
        meta, near_rows, before_near, recv, sent, mesh_latent, mesh_other,
        encode_weights, encode_other, senders, targets, live,
    )
    total, before_skip, self_term = call(
        encode_near_sum_kernel,
        "encode_near_sum",
        operands,
        [SMEM] + [fetch(x) for x in operands[1:7]]
        + [part(encode_weights, 2), part(encode_other, 2)]
        + [whole(x) for x in operands[9:]],
        [
            shape(mesh_rows, full, dtype=F32),
            shape(slots, full),
            shape(HALF, full),
        ],
        2 * full * mesh_rows * slots * 3,
        [pltpu.VMEM((slots, full), BF16), pltpu.VMEM((HALF, full), BF16)],
    )
    operands = (meta, skip_rows, before_skip, targets, live, total)
    sum_own, sum_other = call(
        encode_skip_sum_kernel,
        "encode_skip_sum",
        operands,
        [SMEM, fetch(skip_rows), fetch(before_skip), whole(targets), whole(live), fetch(total)],
        [shape(HALF, full, dtype=F32), shape(HALF, full)],
        2 * full * mesh_rows * slots,
        [pltpu.VMEM((slots, full), BF16)],
    )
    operands = (
        meta, mesh_latent, mesh_other, self_term, sum_own, swap(sum_other),
        encode_weights, encode_other, layer_weights, layer_other,
    )
    now, edge = call(
        encode_update_kernel,
        "encode_update",
        operands,
        [SMEM] + [fetch(x) for x in operands[1:6]]
        + [part(encode_weights, 3), part(encode_other, 3)]
        + [part(layer_weights, 0, 0), part(layer_other, 0, 0)],
        [shape(HALF, full), shape(MARGIN, full)],
        2 * HALF * full * full,
    )

    decode_other = swap(after(decode_weights, now))
    senders_t, live_t = mesh_senders.T, mesh_live.T
    degree = senders_t.shape[0]
    for layer in range(LAYERS):
        last = layer == LAYERS - 1
        far = exchange(edge, halo_shift)
        near = exchange(edge, halo_pairs)
        now_other = swap(now)
        operands = (meta, now, now_other) + (layer_weights, layer_other) * 3
        results = call(
            functools.partial(layer_project_kernel, last),
            f"layer_project_{layer}",
            operands,
            [SMEM, fetch(now), fetch(now_other)]
            + [part(operands[3 + i], layer, i // 2) for i in range(6)],
            [shape(HALF, full)] * (5 if last else 4),
            2 * HALF * full * full * 4,
        )
        sent_own, sent_other, recv, self_own = results[:4]
        operands = (meta, sent_own, sent_other, senders_t)
        (gathered,) = call(
            layer_gather_kernel,
            f"layer_gather_{layer}",
            operands,
            [SMEM, fetch(sent_own), fetch(sent_other), whole(senders_t)],
            [shape(degree, HALF, full)],
            2 * degree * HALF * full * mesh_rows,
        )
        operands = (meta, gathered, recv, far, near, senders_t, live_t)
        scratch = [pltpu.VMEM((2 * MARGIN, full), BF16)]
        sum_specs = (
            [SMEM, Fetch(axis=1, size=MARGIN)]
            + [fetch(x) for x in operands[2:5]]
            + [whole(senders_t), whole(live_t)]
        )
        if last:
            (summed,) = call(
                layer_sum_kernel,
                f"layer_sum_{layer}",
                operands,
                sum_specs,
                [shape(HALF, full)],
                2 * degree * HALF * full * 2 * MARGIN,
                scratch,
            )
            continue
        operands += (now, self_own) + (layer_weights, layer_other) * 2
        now, edge = call(
            layer_update_kernel,
            f"layer_update_{layer}",
            operands,
            sum_specs + [fetch(now), fetch(self_own)]
            + [part(layer_weights, layer, 3), part(layer_other, layer, 3)]
            + [part(layer_weights, layer + 1, 0), part(layer_other, layer + 1, 0)],
            [shape(HALF, full), shape(MARGIN, full)],
            2 * HALF * full * (degree * 2 * MARGIN + full),
            scratch + [pltpu.VMEM((HALF, full), BF16)],
        )
    operands = (
        meta, now, now_other, self_own, results[4], summed, swap(summed),
        layer_weights, layer_other, decode_weights, decode_other,
    )
    mesh_now, sent = call(
        last_update_kernel,
        "last_update",
        operands,
        [SMEM] + [fetch(x) for x in operands[1:7]]
        + [part(layer_weights, LAYERS - 1, 3), part(layer_other, LAYERS - 1, 3)]
        + [part(decode_weights, 0), part(decode_other, 0)],
        [shape(mesh_rows, cols), shape(mesh_rows, full)],
        2 * mesh_rows * full * full * 2,
        [pltpu.VMEM((HALF, full), BF16)],
    )

    near_rows = exchange(sent, near_shift)
    skip_rows = exchange(sent, skip_shift)
    senders, targets, live = (x.transpose(1, 0, 2) for x in (decode_senders, decode_targets, decode_live))
    slots = senders.shape[2]
    operands = (
        meta, grid_latent, grid_other, decode_weights, decode_other, decode_weights, targets
    )
    before_own, before_near, before_skip, self_term = call(
        decode_prepare_kernel,
        "decode_prepare",
        operands,
        [SMEM, fetch(grid_latent), fetch(grid_other)]
        + [part(decode_weights, 1), part(decode_other, 1), part(decode_weights, 2), whole(targets)],
        [
            shape(slots // 2, full),
            shape(slots, full),
            shape(slots, full),
            shape(grid_rows, cols),
        ],
        2 * full * grid_rows * (full + 5 * slots // 2),
        [pltpu.VMEM((grid_rows, full), BF16)],
    )
    total = None
    for kind, rows, before in (
        ("own", sent, before_own),
        ("near", near_rows, before_near),
        ("skip", skip_rows, before_skip),
    ):
        operands = (meta, rows, before, senders, targets, live)
        if total is not None:
            operands += (total,)
        (total,) = call(
            functools.partial(decode_sum_kernel, kind),
            f"decode_{kind}",
            operands,
            [SMEM, fetch(rows), rows_of()]
            + [whole(x) for x in operands[3:6]]
            + [rows_of()] * (len(operands) - 6),
            [shape(grid_rows, full)],
            2 * full * before.shape[0] * (grid_rows + mesh_rows),
            [pltpu.VMEM(before.shape, BF16)],
            tiles=grid_rows // HALF,
        )
    operands = (meta, grid_latent, self_term, total, swap(total), decode_weights)
    (grid_now,) = call(
        final_kernel,
        "final_update",
        operands,
        [SMEM] + [rows_of() for x in operands[1:5]] + [part(decode_weights, 3)],
        [shape(grid_rows, cols)],
        2 * full * grid_rows * cols,
        tiles=grid_rows // HALF,
    )
    return mesh_now, grid_now


def solution(mesh):
    placed = (
        P("band", "feat"),
        P("band", "feat"),
        P(None, None, "feat"),
        P(None, None, None, "feat"),
        P(None, None, "feat"),
        P("band", None, None),
        P("band", None, None),
        P("band", None, None),
        P("band", None),
        P("band", None),
        P("band", None, None),
        P("band", None, None),
        P("band", None, None),
    )
    return jax.shard_map(
        body,
        mesh=mesh,
        in_specs=placed,
        out_specs=(P("band", "feat"), P("band", "feat")),
        check_vma=False,
    )
```

```python
import functools

import jax
import jax.numpy as jnp
from jax import lax
from jax.experimental import pallas as pl
from jax.experimental.pallas import tpu as pltpu
from jax.sharding import PartitionSpec as P

REACH = 2
LAYERS = 2
MARGIN = 64
HALF = 256
LANES = 128
F32 = jnp.float32
BF16 = jnp.bfloat16
I32 = jnp.int32
VMEM_LIMIT = 36 * 1024 * 1024


def swap(value):
    return lax.ppermute(value, "feat", [(0, 1), (1, 0)])


def flat(partners):
    return [(2 * s + c, 2 * t + e) for (s, c), (t, e) in partners.items()]


def shift(steps, up, count):
    partners = {}
    for s in range(count):
        partners[s, up] = (s + steps, up) if s + steps < count else (s, 1 - up)
        partners[s, 1 - up] = (s - steps, 1 - up) if s >= steps else (s, up)
    return flat(partners)


near_shift = functools.partial(shift, 1, 0)
skip_shift = functools.partial(shift, 2, 0)
halo_shift = functools.partial(shift, 1, 1)


def halo_pairs(count):
    partners = {}
    for s in range(count):
        partners[s, 1] = ((s + 1) % count, 0)
        partners[(s + 1) % count, 0] = (s, 1)
    return flat(partners)


def exchange(value, pairs):
    return lax.ppermute(value, ("band", "feat"), pairs(lax.axis_size("band")))


def after(value, other):
    return lax.optimization_barrier((value, other))[0]


def silu(v):
    half = 0.5 * v
    return half + half * jnp.tanh(half)


def silu_message(v):
    half = v.astype(BF16) * BF16(0.5)
    return half + half * jnp.tanh(half)


def dot(a, b):
    return jnp.dot(a, b, preferred_element_type=F32)


def window(index, size=HALF):
    return pl.ds(pl.multiple_of(index * size, size), size)


def near_offset(meta):
    return 3 - 2 * meta[0]


def skip_offset(meta):
    return 4 - 4 * meta[0]


def column(row):
    parts = [
        jnp.broadcast_to(row[:, start : start + LANES], (LANES, LANES)).T
        for start in range(0, row.shape[1], LANES)
    ]
    return parts[0] if len(parts) == 1 else jnp.concatenate(parts, axis=0)


def hot_columns(col, width):
    col = col.astype(jnp.int16)
    ids = lax.broadcasted_iota(I32, col.shape, 1).astype(jnp.int16)
    one, zero = BF16(1), BF16(0)
    parts = [
        jnp.where(col == ids + jnp.int16(start), one, zero) for start in range(0, width, LANES)
    ]
    return parts[0] if len(parts) == 1 else jnp.concatenate(parts, axis=1)


def hot_rows(row, height):
    ids = lax.broadcasted_iota(I32, (height, row.shape[1]), 0)
    return jnp.where(row == ids, 1.0, 0.0).astype(BF16)


def call(kernel, name, operands, specs, outs, flops, scratch=()):
    size = sum(x.size * x.dtype.itemsize for x in outs)
    return pl.pallas_call(
        kernel,
        name=name,
        grid=(1,),
        in_specs=specs,
        out_specs=[whole(x) for x in outs],
        out_shape=list(outs),
        scratch_shapes=list(scratch),
        compiler_params=pltpu.CompilerParams(vmem_limit_bytes=VMEM_LIMIT),
        cost_estimate=pl.CostEstimate(
            flops=flops // 64, bytes_accessed=size // 64, transcendentals=0
        ),
    )(*operands)


def whole(x):
    return pl.BlockSpec(x.shape, lambda i, n=len(x.shape): (0,) * n)


def part(x, *index):
    lead = len(index)
    rest = x.shape[lead:]
    return pl.BlockSpec((None,) * lead + rest, lambda i, where=index + (0,) * len(rest): where)


SMEM = pl.BlockSpec(memory_space=pltpu.SMEM)


def shape(*dims, dtype=BF16):
    return jax.ShapeDtypeStruct(dims, dtype)


def encode_begin_kernel(meta, own, w_own, out):
    for start in range(0, own.shape[0], HALF):
        rows = pl.ds(start, HALF)
        out[rows, :] = dot(own[rows, :], w_own[window(meta[0]), :])


def gather_slots(senders_row, sent, out):
    for start in range(0, senders_row.shape[1], HALF):
        col = column(senders_row[:, start : start + HALF])
        out[pl.ds(start, HALF), :] = dot(hot_columns(col, sent.shape[0]), sent[...]).astype(BF16)


def encode_near_kernel(meta, own, other, begun, w_own, w_other, senders, sent, piece):
    mine, rest = window(meta[0]), window(1 - meta[0])
    for start in range(0, own.shape[0], HALF):
        rows = pl.ds(start, HALF)
        a, b = own[rows, :], other[rows, :]
        sent[rows, mine] = (begun[rows, :] + dot(b, w_own[rest, :])).astype(BF16)
        sent[rows, rest] = (dot(a, w_other[mine, :]) + dot(b, w_other[rest, :])).astype(BF16)
    gather_slots(senders[near_offset(meta)], sent, piece)


def live_targets(targets, live, offset, columns=slice(None)):
    return jnp.where(live[offset, :, columns] > 0, targets[offset, :, columns], -1)


def encode_skip_kernel(
    meta, own, other, w1, w1_other, sent, senders, targets, piece, recv, before
):
    gather_slots(senders[skip_offset(meta)], sent, piece)
    mine, rest = window(meta[0]), window(1 - meta[0])
    for start in range(0, own.shape[0], HALF):
        rows = pl.ds(start, HALF)
        a, b = own[rows, :], other[rows, :]
        recv[rows, mine] = (dot(a, w1[mine, :]) + dot(b, w1[rest, :])).astype(BF16)
        recv[rows, rest] = (dot(a, w1_other[mine, :]) + dot(b, w1_other[rest, :])).astype(BF16)
    gather_slots(targets[near_offset(meta)], recv, before)


def encode_near_sum_kernel(
    meta, rows, before, recv, sent, own, other, w2, w2_other, senders, targets, live,
    total, before_skip, self_term, message, own_message,
):
    mine, rest = window(meta[0]), window(1 - meta[0])
    nodes = recv.shape[0]
    from_rows = hot_columns(column(senders[REACH, :, mine]), sent.shape[0])
    to_rows = hot_columns(column(targets[REACH, :, mine]), nodes)
    own_message[...] = silu_message(dot(from_rows, sent[...]) + dot(to_rows, recv[...]))
    message[...] = silu_message(rows[...] + before[...])
    row = live_targets(targets, live, near_offset(meta))
    own_row = live_targets(targets, live, REACH, mine)
    for start in range(0, nodes, HALF):
        value = dot(hot_rows(row - start, HALF), message[...])
        value = value + dot(hot_rows(own_row - start, HALF), own_message[...])
        total[pl.ds(start, HALF), :] = value
    gather_slots(targets[skip_offset(meta)], recv, before_skip)
    a, b = own[mine, :], other[mine, :]
    self_term[:, mine] = (dot(a, w2[mine, :]) + dot(b, w2[rest, :])).astype(BF16)
    self_term[:, rest] = (dot(a, w2_other[mine, :]) + dot(b, w2_other[rest, :])).astype(BF16)


def encode_skip_sum_kernel(meta, rows, before, targets, live, total, out_own, out_other, message):
    message[...] = silu_message(rows[...] + before[...])
    row = live_targets(targets, live, skip_offset(meta))
    for out, half in ((out_other, 1 - meta[0]), (out_own, meta[0])):
        value = dot(hot_rows(row - half * HALF, HALF), message[...]) + total[window(half), :]
        out[...] = value.astype(out.dtype)


def put_edge(meta, now, w0, w0_other, edge):
    mine, rest = window(meta[0]), window(1 - meta[0])
    rows = now[pl.ds(pl.multiple_of(meta[0] * (HALF - MARGIN), MARGIN), MARGIN), :]
    edge[:, mine] = dot(rows, w0[...]).astype(BF16)
    edge[:, rest] = dot(rows, w0_other[...]).astype(BF16)


def encode_update_kernel(
    meta, own, other, self_term, sum_own, sum_other, w3, w3_other, w0, w0_other, now, edge
):
    mine, rest = window(meta[0]), window(1 - meta[0])
    summed = (sum_own[...] + sum_other[...].astype(F32)).astype(BF16)
    for cols, latent, w in ((mine, own, w3), (rest, other, w3_other)):
        step = silu(self_term[:, cols] + dot(summed, w[...]))
        now[:, cols] = (latent[mine, :].astype(F32) + step).astype(BF16)
    put_edge(meta, now, w0, w0_other, edge)


def layer_project_kernel(
    last, meta, own, other, w0, w0_other, w1, w1_other, w2, w2_other,
    sent_own, sent_other, recv, self_own, *self_other,
):
    mine, rest = window(meta[0]), window(1 - meta[0])
    for cols, w in ((mine, w0), (rest, w0_other)):
        sent_own[:, cols] = dot(own[...], w[...]).astype(BF16)
        sent_other[:, cols] = dot(other[...], w[...]).astype(BF16)
    for cols, w in ((mine, w1), (rest, w1_other)):
        recv[:, cols] = dot(own[...], w[...]).astype(BF16)
    for cols, w in ((mine, w2), (rest, w2_other)):
        self_own[:, cols] = dot(own[...], w[...]).astype(BF16)
        if last:
            self_other[0][:, cols] = dot(other[...], w[...]).astype(BF16)


def layer_gather_kernel(meta, own, other, senders, out):
    mine = window(meta[0])
    base = meta[1] * (2 * HALF)
    for k in range(senders.shape[0]):
        local = senders[k : k + 1, mine] - base
        col = column(local - meta[0] * HALF)
        col_other = column(local - (1 - meta[0]) * HALF)
        value = dot(hot_columns(col, HALF), own[...])
        value = value + dot(hot_columns(col_other, HALF), other[...])
        out[k] = value.astype(BF16)


def layer_sum(meta, gathered, recv, far, near, senders, live, halo, total):
    mine = window(meta[0])
    nodes = 2 * HALF
    base = meta[1] * nodes
    count = senders.shape[0]
    hots, flags = [], []
    for k in range(count):
        local = senders[k : k + 1, mine] - base
        where = jnp.where(local < 0, local + MARGIN, local - nodes + MARGIN)
        where = jnp.where((local >= 0) & (local < nodes), -1, where)
        hots.append(hot_columns(column(where), 2 * MARGIN))
        flags.append(column(live[k : k + 1, mine]).astype(BF16))
    halo[pl.ds(pl.multiple_of(meta[0] * MARGIN, MARGIN), MARGIN), :] = near[...]
    halo[pl.ds(pl.multiple_of((1 - meta[0]) * MARGIN, MARGIN), MARGIN), :] = far[...]
    outside = dot(jnp.concatenate(hots, axis=0), halo[...]).astype(BF16)
    step = 32
    for start in range(0, HALF, step):
        rows = pl.ds(start, step)
        side = recv[rows, :]
        running = None
        for k in range(count):
            row = k * HALF + start
            message = silu_message(outside[row : row + step, :] + gathered[k, rows, :] + side)
            flag = jnp.concatenate([flags[k][start : start + step, :]] * 4, axis=1)
            message = (message * flag).astype(F32)
            running = message if running is None else running + message
        total[rows, :] = running.astype(BF16)


def layer_update_kernel(
    meta, gathered, recv, far, near, senders, live, now, self_term, w3, w3_other, w0, w0_other,
    out, edge, halo, total,
):
    mine, rest = window(meta[0]), window(1 - meta[0])
    layer_sum(meta, gathered, recv, far, near, senders, live, halo, total)
    summed = total[...]
    for cols, w in ((mine, w3), (rest, w3_other)):
        step = silu(self_term[:, cols] + dot(summed, w[...]))
        out[:, cols] = (now[:, cols].astype(F32) + step).astype(BF16)
    put_edge(meta, out, w0, w0_other, edge)


def layer_sum_kernel(meta, gathered, recv, far, near, senders, live, out, halo):
    layer_sum(meta, gathered, recv, far, near, senders, live, halo, out)


def last_update_kernel(
    meta, now_own, now_other, self_own, self_other, sum_own, sum_other, w3, w3_other,
    w0, w0_other, out, sent, now,
):
    mine, rest = window(meta[0]), window(1 - meta[0])
    for rows, latent, self_term, summed in (
        (mine, now_own, self_own, sum_own),
        (rest, now_other, self_other, sum_other),
    ):
        for cols, w in ((mine, w3), (rest, w3_other)):
            step = silu(self_term[:, cols] + dot(summed[...], w[...]))
            now[:, cols] = (latent[:, cols].astype(F32) + step).astype(BF16)
        out[rows, :] = now[:, mine]
        for cols, w in ((mine, w0), (rest, w0_other)):
            sent[rows, cols] = dot(now[...], w[...]).astype(BF16)


def decode_prepare_kernel(
    meta, own, other, w1, w1_other, w2, targets,
    before_own, before_near, before_skip, self_term, recv,
):
    mine, rest = window(meta[0]), window(1 - meta[0])
    for start in range(0, own.shape[0], HALF):
        rows = pl.ds(start, HALF)
        a, b = own[rows, :], other[rows, :]
        recv[rows, mine] = (dot(a, w1[mine, :]) + dot(b, w1[rest, :])).astype(BF16)
        recv[rows, rest] = (dot(a, w1_other[mine, :]) + dot(b, w1_other[rest, :])).astype(BF16)
        self_term[rows, :] = (dot(a, w2[mine, :]) + dot(b, w2[rest, :])).astype(BF16)
    half = before_own.shape[0]
    gather_slots(targets[REACH, :, window(meta[0], half)], recv, before_own)
    gather_slots(targets[near_offset(meta)], recv, before_near)
    gather_slots(targets[skip_offset(meta)], recv, before_skip)


def decode_messages(meta, offset, columns, sent, before, senders, message):
    from_row = senders[offset, :, columns]
    for start in range(0, before.shape[0], HALF):
        rows = pl.ds(start, HALF)
        hot = hot_columns(column(from_row[:, start : start + HALF]), sent.shape[0])
        pre = dot(hot, sent[...]) + before[rows, :].astype(F32)
        message[rows, :] = silu_message(pre)


def decode_scatter(row, message, total, first, out):
    for start in range(0, out.shape[0], HALF):
        value = dot(hot_rows(row - (first + start), HALF), message[...])
        if total is not None:
            value = value + total[pl.ds(first + start, HALF), :].astype(F32)
        out[pl.ds(start, HALF), :] = value.astype(BF16)


def decode_own_kernel(meta, sent, before, senders, targets, live, out, message):
    columns = window(meta[0], before.shape[0])
    decode_messages(meta, REACH, columns, sent, before, senders, message)
    decode_scatter(live_targets(targets, live, REACH, columns), message, None, 0, out)


def decode_near_kernel(meta, sent, before, senders, targets, live, total, out, message):
    offset = near_offset(meta)
    decode_messages(meta, offset, slice(None), sent, before, senders, message)
    decode_scatter(live_targets(targets, live, offset), message, total, 0, out)


def decode_skip_kernel(meta, sent, before, senders, targets, live, total, out, message):
    offset = skip_offset(meta)
    decode_messages(meta, offset, slice(None), sent, before, senders, message)
    decode_scatter(live_targets(targets, live, offset), message, total, 0, out)


def decode_rest_kernel(meta, message, targets, live, total, out):
    row = live_targets(targets, live, skip_offset(meta))
    decode_scatter(row, message, total, out.shape[0], out)


def final_kernel(meta, own, self_term, sum_own, sum_other, w3, *refs):
    out = refs[-1]
    for start in range(0, own.shape[0], HALF):
        rows = pl.ds(start, HALF)
        summed = sum_own[rows, :] + sum_other[rows, :]
        step = silu(self_term[rows, :].astype(F32) + dot(summed, w3[...]))
        out[rows, :] = (own[rows, :].astype(F32) + step).astype(BF16)


def body(
    grid_latent,
    mesh_latent,
    encode_weights,
    layer_weights,
    decode_weights,
    encode_senders,
    encode_targets,
    encode_live,
    mesh_senders,
    mesh_live,
    decode_senders,
    decode_targets,
    decode_live,
):
    meta = jnp.stack([lax.axis_index("feat"), lax.axis_index("band")]).astype(I32)
    grid_rows, cols = grid_latent.shape
    mesh_rows = mesh_latent.shape[0]
    full = 2 * cols
    senders, targets, live = (x.transpose(1, 0, 2) for x in (encode_senders, encode_targets, encode_live))
    slots = senders.shape[2]

    grid_other = swap(grid_latent)
    encode_other = swap(encode_weights)
    mesh_other = swap(mesh_latent)
    (begun,) = call(
        encode_begin_kernel,
        "encode_begin",
        (meta, grid_latent, encode_weights),
        [SMEM, whole(grid_latent), part(encode_weights, 0)],
        [shape(grid_rows, cols, dtype=F32)],
        2 * grid_rows * cols * cols,
    )
    operands = (meta, grid_latent, grid_other, begun, encode_weights, encode_other, senders)
    sent, near_piece = call(
        encode_near_kernel,
        "encode_near",
        operands,
        [SMEM] + [whole(x) for x in operands[1:4]]
        + [part(encode_weights, 0), part(encode_other, 0), whole(senders)],
        [shape(grid_rows, full), shape(slots, full)],
        2 * full * (grid_rows * full + slots * grid_rows),
    )
    near_rows = exchange(near_piece, near_shift)
    layer_other = swap(after(layer_weights, near_piece))
    operands = (
        meta, mesh_latent, mesh_other, encode_weights, encode_other, sent, senders, targets
    )
    skip_piece, recv, before_near = call(
        encode_skip_kernel,
        "encode_skip",
        operands,
        [SMEM, whole(mesh_latent), whole(mesh_other)]
        + [part(encode_weights, 1), part(encode_other, 1)]
        + [whole(sent), whole(senders), whole(targets)],
        [shape(slots, full), shape(mesh_rows, full), shape(slots, full)],
        2 * full * (mesh_rows * full + slots * (grid_rows + mesh_rows)),
    )
    skip_rows = exchange(skip_piece, skip_shift)
    operands = (
        meta, near_rows, before_near, recv, sent, mesh_latent, mesh_other,
        encode_weights, encode_other, senders, targets, live,
    )
    total, before_skip, self_term = call(
        encode_near_sum_kernel,
        "encode_near_sum",
        operands,
        [SMEM] + [whole(x) for x in operands[1:7]]
        + [part(encode_weights, 2), part(encode_other, 2)]
        + [whole(x) for x in operands[9:]],
        [
            shape(mesh_rows, full, dtype=F32),
            shape(slots, full),
            shape(HALF, full),
        ],
        2 * full * mesh_rows * slots * 3,
        [pltpu.VMEM((slots, full), BF16), pltpu.VMEM((HALF, full), BF16)],
    )
    operands = (meta, skip_rows, before_skip, targets, live, total)
    sum_own, sum_other = call(
        encode_skip_sum_kernel,
        "encode_skip_sum",
        operands,
        [SMEM, whole(skip_rows), whole(before_skip), whole(targets), whole(live), whole(total)],
        [shape(HALF, full, dtype=F32), shape(HALF, full)],
        2 * full * mesh_rows * slots,
        [pltpu.VMEM((slots, full), BF16)],
    )
    operands = (
        meta, mesh_latent, mesh_other, self_term, sum_own, swap(sum_other),
        encode_weights, encode_other, layer_weights, layer_other,
    )
    now, edge = call(
        encode_update_kernel,
        "encode_update",
        operands,
        [SMEM] + [whole(x) for x in operands[1:6]]
        + [part(encode_weights, 3), part(encode_other, 3)]
        + [part(layer_weights, 0, 0), part(layer_other, 0, 0)],
        [shape(HALF, full), shape(MARGIN, full)],
        2 * HALF * full * full,
    )

    decode_other = swap(after(decode_weights, now))
    senders_t, live_t = mesh_senders.T, mesh_live.T
    degree = senders_t.shape[0]
    for layer in range(LAYERS):
        last = layer == LAYERS - 1
        far = exchange(edge, halo_shift)
        near = exchange(edge, halo_pairs)
        now_other = swap(now)
        operands = (meta, now, now_other) + (layer_weights, layer_other) * 3
        results = call(
            functools.partial(layer_project_kernel, last),
            f"layer_project_{layer}",
            operands,
            [SMEM, whole(now), whole(now_other)]
            + [part(operands[3 + i], layer, i // 2) for i in range(6)],
            [shape(HALF, full)] * (5 if last else 4),
            2 * HALF * full * full * 4,
        )
        sent_own, sent_other, recv, self_own = results[:4]
        operands = (meta, sent_own, sent_other, senders_t)
        (gathered,) = call(
            layer_gather_kernel,
            f"layer_gather_{layer}",
            operands,
            [SMEM, whole(sent_own), whole(sent_other), whole(senders_t)],
            [shape(degree, HALF, full)],
            2 * degree * HALF * full * mesh_rows,
        )
        operands = (meta, gathered, recv, far, near, senders_t, live_t)
        scratch = [pltpu.VMEM((2 * MARGIN, full), BF16)]
        sum_specs = (
            [SMEM] + [whole(x) for x in operands[1:5]]
            + [whole(senders_t), whole(live_t)]
        )
        if last:
            (summed,) = call(
                layer_sum_kernel,
                f"layer_sum_{layer}",
                operands,
                sum_specs,
                [shape(HALF, full)],
                2 * degree * HALF * full * 2 * MARGIN,
                scratch,
            )
            continue
        operands += (now, self_own) + (layer_weights, layer_other) * 2
        now, edge = call(
            layer_update_kernel,
            f"layer_update_{layer}",
            operands,
            sum_specs + [whole(now), whole(self_own)]
            + [part(layer_weights, layer, 3), part(layer_other, layer, 3)]
            + [part(layer_weights, layer + 1, 0), part(layer_other, layer + 1, 0)],
            [shape(HALF, full), shape(MARGIN, full)],
            2 * HALF * full * (degree * 2 * MARGIN + full),
            scratch + [pltpu.VMEM((HALF, full), BF16)],
        )
    operands = (
        meta, now, now_other, self_own, results[4], summed, swap(summed),
        layer_weights, layer_other, decode_weights, decode_other,
    )
    mesh_now, sent = call(
        last_update_kernel,
        "last_update",
        operands,
        [SMEM] + [whole(x) for x in operands[1:7]]
        + [part(layer_weights, LAYERS - 1, 3), part(layer_other, LAYERS - 1, 3)]
        + [part(decode_weights, 0), part(decode_other, 0)],
        [shape(mesh_rows, cols), shape(mesh_rows, full)],
        2 * mesh_rows * full * full * 2,
        [pltpu.VMEM((HALF, full), BF16)],
    )

    near_rows = exchange(sent, near_shift)
    skip_rows = exchange(sent, skip_shift)
    senders, targets, live = (x.transpose(1, 0, 2) for x in (decode_senders, decode_targets, decode_live))
    slots = senders.shape[2]
    operands = (
        meta, grid_latent, grid_other, decode_weights, decode_other, decode_weights, targets
    )
    before_own, before_near, before_skip, self_term = call(
        decode_prepare_kernel,
        "decode_prepare",
        operands,
        [SMEM, whole(grid_latent), whole(grid_other)]
        + [part(decode_weights, 1), part(decode_other, 1), part(decode_weights, 2), whole(targets)],
        [
            shape(slots // 2, full),
            shape(slots, full),
            shape(slots, full),
            shape(grid_rows, cols),
        ],
        2 * full * grid_rows * (full + 5 * slots // 2),
        [pltpu.VMEM((grid_rows, full), BF16)],
    )
    flops = 2 * full * slots * (grid_rows + mesh_rows)
    message_space = [pltpu.VMEM((slots, full), BF16)]
    operands = (meta, sent, before_own, senders, targets, live)
    (total,) = call(
        decode_own_kernel,
        "decode_own",
        operands,
        [SMEM] + [whole(x) for x in operands[1:]],
        [shape(grid_rows, full)],
        flops // 2,
        [pltpu.VMEM(before_own.shape, BF16)],
    )
    operands = (meta, near_rows, before_near, senders, targets, live, total)
    (total,) = call(
        decode_near_kernel,
        "decode_near",
        operands,
        [SMEM] + [whole(x) for x in operands[1:]],
        [shape(grid_rows, full)],
        flops,
        message_space,
    )
    half = grid_rows // 2
    operands = (meta, skip_rows, before_skip, senders, targets, live, total)
    head, message = call(
        decode_skip_kernel,
        "decode_skip",
        operands,
        [SMEM] + [whole(x) for x in operands[1:]],
        [shape(half, full), shape(slots, full)],
        flops,
    )
    operands = (meta, message, targets, live, total)
    (tail,) = call(
        decode_rest_kernel,
        "decode_rest",
        operands,
        [SMEM] + [whole(x) for x in operands[1:]],
        [shape(half, full)],
        flops // 2,
    )
    grid_now = None
    for index, summed in enumerate((head, tail)):
        block = pl.BlockSpec((half, cols), lambda i, index=index: (index, 0))
        operands = (meta, grid_latent, self_term, summed, swap(summed), decode_weights)
        specs = [SMEM, block, block, whole(summed), whole(summed), part(decode_weights, 3)]
        aliases = {}
        if index:
            operands, specs, aliases = operands + (grid_now,), specs + [pl.BlockSpec(memory_space=pl.ANY)], {6: 0}
        grid_now = pl.pallas_call(
            final_kernel,
            name=f"final_update_{index}",
            grid=(1,),
            in_specs=specs,
            out_specs=block,
            out_shape=shape(grid_rows, cols),
            input_output_aliases=aliases,
            compiler_params=pltpu.CompilerParams(vmem_limit_bytes=VMEM_LIMIT),
        )(*operands)
    return mesh_now, grid_now


def solution(mesh):
    placed = (
        P("band", "feat"),
        P("band", "feat"),
        P(None, None, "feat"),
        P(None, None, None, "feat"),
        P(None, None, "feat"),
        P("band", None, None),
        P("band", None, None),
        P("band", None, None),
        P("band", None),
        P("band", None),
        P("band", None, None),
        P("band", None, None),
        P("band", None, None),
    )
    return jax.shard_map(
        body,
        mesh=mesh,
        in_specs=placed,
        out_specs=(P("band", "feat"), P("band", "feat")),
        check_vma=False,
    )
```

```python
import functools

import jax
import jax.numpy as jnp
from jax import lax
from jax.experimental import pallas as pl
from jax.experimental.pallas import tpu as pltpu
from jax.sharding import PartitionSpec as P

REACH = 2
LAYERS = 2
MARGIN = 64
HALF = 256
LANES = 128
F32 = jnp.float32
BF16 = jnp.bfloat16
I32 = jnp.int32
VMEM_LIMIT = 36 * 1024 * 1024


def swap(value):
    return lax.ppermute(value, "feat", [(0, 1), (1, 0)])


def flat(partners):
    return [(2 * s + c, 2 * t + e) for (s, c), (t, e) in partners.items()]


def shift(steps, up, count):
    partners = {}
    for s in range(count):
        partners[s, up] = (s + steps, up) if s + steps < count else (s, 1 - up)
        partners[s, 1 - up] = (s - steps, 1 - up) if s >= steps else (s, up)
    return flat(partners)


near_shift = functools.partial(shift, 1, 0)
skip_shift = functools.partial(shift, 2, 0)
halo_shift = functools.partial(shift, 1, 1)


def halo_pairs(count):
    partners = {}
    for s in range(count):
        partners[s, 1] = ((s + 1) % count, 0)
        partners[(s + 1) % count, 0] = (s, 1)
    return flat(partners)


def exchange(value, pairs):
    return lax.ppermute(value, ("band", "feat"), pairs(lax.axis_size("band")))


def after(value, other):
    return lax.optimization_barrier((value, other))[0]


def silu(v):
    half = 0.5 * v
    return half + half * jnp.tanh(half)


def silu_message(v):
    half = v.astype(BF16) * BF16(0.5)
    return half + half * jnp.tanh(half)


def dot(a, b):
    return jnp.dot(a, b, preferred_element_type=F32)


def window(index, size=HALF):
    return pl.ds(pl.multiple_of(index * size, size), size)


def near_offset(meta):
    return 3 - 2 * meta[0]


def skip_offset(meta):
    return 4 - 4 * meta[0]


def column(row):
    parts = [
        jnp.broadcast_to(row[:, start : start + LANES], (LANES, LANES)).T
        for start in range(0, row.shape[1], LANES)
    ]
    return parts[0] if len(parts) == 1 else jnp.concatenate(parts, axis=0)


def hot_columns(col, width):
    col = col.astype(jnp.int16)
    ids = lax.broadcasted_iota(I32, col.shape, 1).astype(jnp.int16)
    one, zero = BF16(1), BF16(0)
    parts = [
        jnp.where(col == ids + jnp.int16(start), one, zero) for start in range(0, width, LANES)
    ]
    return parts[0] if len(parts) == 1 else jnp.concatenate(parts, axis=1)


def hot_rows(row, height):
    ids = lax.broadcasted_iota(I32, (height, row.shape[1]), 0)
    return jnp.where(row == ids, 1.0, 0.0).astype(BF16)


class Part:
    def __init__(self, spec, index):
        self.spec, self.index = spec, index


def call(kernel, name, operands, specs, outs, flops, scratch=()):
    def viewed(*refs):
        refs = [
            ref.at[specs[i].index] if i < len(specs) and isinstance(specs[i], Part) else ref
            for i, ref in enumerate(refs)
        ]
        kernel(*refs)

    size = sum(x.size * x.dtype.itemsize for x in outs)
    return pl.pallas_call(
        viewed,
        name=name,
        grid=(1,),
        in_specs=[spec.spec if isinstance(spec, Part) else spec for spec in specs],
        out_specs=[whole(x) for x in outs],
        out_shape=list(outs),
        scratch_shapes=list(scratch),
        compiler_params=pltpu.CompilerParams(vmem_limit_bytes=VMEM_LIMIT),
        cost_estimate=pl.CostEstimate(
            flops=flops // 64, bytes_accessed=size // 64, transcendentals=0
        ),
    )(*operands)


def whole(x):
    return pl.BlockSpec(x.shape, lambda i, n=len(x.shape): (0,) * n)


def part(x, *index):
    return Part(whole(x), index)


SMEM = pl.BlockSpec(memory_space=pltpu.SMEM)


def shape(*dims, dtype=BF16):
    return jax.ShapeDtypeStruct(dims, dtype)


def encode_begin_kernel(meta, own, w_own, out):
    for start in range(0, own.shape[0], HALF):
        rows = pl.ds(start, HALF)
        out[rows, :] = dot(own[rows, :], w_own[window(meta[0]), :])


def gather_slots(senders_row, sent, out):
    for start in range(0, senders_row.shape[1], HALF):
        col = column(senders_row[:, start : start + HALF])
        out[pl.ds(start, HALF), :] = dot(hot_columns(col, sent.shape[0]), sent[...]).astype(BF16)


def encode_near_kernel(meta, own, other, begun, w_own, w_other, senders, sent, piece):
    mine, rest = window(meta[0]), window(1 - meta[0])
    for start in range(0, own.shape[0], HALF):
        rows = pl.ds(start, HALF)
        a, b = own[rows, :], other[rows, :]
        sent[rows, mine] = (begun[rows, :] + dot(b, w_own[rest, :])).astype(BF16)
        sent[rows, rest] = (dot(a, w_other[mine, :]) + dot(b, w_other[rest, :])).astype(BF16)
    gather_slots(senders[near_offset(meta)], sent, piece)


def live_targets(targets, live, offset, columns=slice(None)):
    return jnp.where(live[offset, :, columns] > 0, targets[offset, :, columns], -1)


def encode_skip_kernel(
    meta, own, other, w1, w1_other, sent, senders, targets, piece, recv, before
):
    gather_slots(senders[skip_offset(meta)], sent, piece)
    mine, rest = window(meta[0]), window(1 - meta[0])
    for start in range(0, own.shape[0], HALF):
        rows = pl.ds(start, HALF)
        a, b = own[rows, :], other[rows, :]
        recv[rows, mine] = (dot(a, w1[mine, :]) + dot(b, w1[rest, :])).astype(BF16)
        recv[rows, rest] = (dot(a, w1_other[mine, :]) + dot(b, w1_other[rest, :])).astype(BF16)
    gather_slots(targets[near_offset(meta)], recv, before)


def encode_near_sum_kernel(
    meta, rows, before, recv, sent, own, other, w2, w2_other, senders, targets, live,
    total, before_skip, self_term, message, own_message,
):
    mine, rest = window(meta[0]), window(1 - meta[0])
    nodes = recv.shape[0]
    from_rows = hot_columns(column(senders[REACH, :, mine]), sent.shape[0])
    to_rows = hot_columns(column(targets[REACH, :, mine]), nodes)
    own_message[...] = silu_message(dot(from_rows, sent[...]) + dot(to_rows, recv[...]))
    message[...] = silu_message(rows[...] + before[...])
    row = live_targets(targets, live, near_offset(meta))
    own_row = live_targets(targets, live, REACH, mine)
    for start in range(0, nodes, HALF):
        value = dot(hot_rows(row - start, HALF), message[...])
        value = value + dot(hot_rows(own_row - start, HALF), own_message[...])
        total[pl.ds(start, HALF), :] = value
    gather_slots(targets[skip_offset(meta)], recv, before_skip)
    a, b = own[mine, :], other[mine, :]
    self_term[:, mine] = (dot(a, w2[mine, :]) + dot(b, w2[rest, :])).astype(BF16)
    self_term[:, rest] = (dot(a, w2_other[mine, :]) + dot(b, w2_other[rest, :])).astype(BF16)


def encode_skip_sum_kernel(meta, rows, before, targets, live, total, out_own, out_other, message):
    message[...] = silu_message(rows[...] + before[...])
    row = live_targets(targets, live, skip_offset(meta))
    for out, half in ((out_other, 1 - meta[0]), (out_own, meta[0])):
        value = dot(hot_rows(row - half * HALF, HALF), message[...]) + total[window(half), :]
        out[...] = value.astype(out.dtype)


def put_edge(meta, now, w0, w0_other, edge):
    mine, rest = window(meta[0]), window(1 - meta[0])
    rows = now[pl.ds(pl.multiple_of(meta[0] * (HALF - MARGIN), MARGIN), MARGIN), :]
    edge[:, mine] = dot(rows, w0[...]).astype(BF16)
    edge[:, rest] = dot(rows, w0_other[...]).astype(BF16)


def encode_update_kernel(
    meta, own, other, self_term, sum_own, sum_other, w3, w3_other, w0, w0_other, now, edge
):
    mine, rest = window(meta[0]), window(1 - meta[0])
    summed = (sum_own[...] + sum_other[...].astype(F32)).astype(BF16)
    for cols, latent, w in ((mine, own, w3), (rest, other, w3_other)):
        step = silu(self_term[:, cols] + dot(summed, w[...]))
        now[:, cols] = (latent[mine, :].astype(F32) + step).astype(BF16)
    put_edge(meta, now, w0, w0_other, edge)


def layer_project_kernel(
    last, meta, own, other, w0, w0_other, w1, w1_other, w2, w2_other,
    sent_own, sent_other, recv, self_own, *self_other,
):
    mine, rest = window(meta[0]), window(1 - meta[0])
    for cols, w in ((mine, w0), (rest, w0_other)):
        sent_own[:, cols] = dot(own[...], w[...]).astype(BF16)
        sent_other[:, cols] = dot(other[...], w[...]).astype(BF16)
    for cols, w in ((mine, w1), (rest, w1_other)):
        recv[:, cols] = dot(own[...], w[...]).astype(BF16)
    for cols, w in ((mine, w2), (rest, w2_other)):
        self_own[:, cols] = dot(own[...], w[...]).astype(BF16)
        if last:
            self_other[0][:, cols] = dot(other[...], w[...]).astype(BF16)


def layer_gather_kernel(meta, own, other, senders, out):
    mine = window(meta[0])
    base = meta[1] * (2 * HALF)
    for k in range(senders.shape[0]):
        local = senders[k : k + 1, mine] - base
        col = column(local - meta[0] * HALF)
        col_other = column(local - (1 - meta[0]) * HALF)
        value = dot(hot_columns(col, HALF), own[...])
        value = value + dot(hot_columns(col_other, HALF), other[...])
        out[k] = value.astype(BF16)


def layer_sum(meta, gathered, recv, near, far, senders, live, halo, total):
    mine = window(meta[0])
    nodes = 2 * HALF
    base = meta[1] * nodes
    count = senders.shape[0]
    hots, flags = [], []
    for k in range(count):
        local = senders[k : k + 1, mine] - base
        where = jnp.where(local < 0, local + MARGIN, local - nodes + MARGIN)
        where = jnp.where((local >= 0) & (local < nodes), -1, where)
        hots.append(hot_columns(column(where), 2 * MARGIN))
        flags.append(column(live[k : k + 1, mine]).astype(BF16))
    halo[pl.ds(pl.multiple_of(meta[0] * MARGIN, MARGIN), MARGIN), :] = near[...]
    halo[pl.ds(pl.multiple_of((1 - meta[0]) * MARGIN, MARGIN), MARGIN), :] = far[...]
    outside = dot(jnp.concatenate(hots, axis=0), halo[...]).astype(BF16)
    step = 32
    for start in range(0, HALF, step):
        rows = pl.ds(start, step)
        side = recv[rows, :]
        running = None
        for k in range(count):
            row = k * HALF + start
            message = silu_message(outside[row : row + step, :] + gathered[k, rows, :] + side)
            flag = jnp.concatenate([flags[k][start : start + step, :]] * 4, axis=1)
            message = (message * flag).astype(F32)
            running = message if running is None else running + message
        total[rows, :] = running.astype(BF16)


def layer_update_kernel(
    meta, gathered, recv, near, far, senders, live, now, self_term, w3, w3_other, w0, w0_other,
    out, edge, halo, total,
):
    mine, rest = window(meta[0]), window(1 - meta[0])
    layer_sum(meta, gathered, recv, near, far, senders, live, halo, total)
    summed = total[...]
    for cols, w in ((mine, w3), (rest, w3_other)):
        step = silu(self_term[:, cols] + dot(summed, w[...]))
        out[:, cols] = (now[:, cols].astype(F32) + step).astype(BF16)
    put_edge(meta, out, w0, w0_other, edge)


def layer_sum_kernel(meta, gathered, recv, near, far, senders, live, out, halo):
    layer_sum(meta, gathered, recv, near, far, senders, live, halo, out)


def last_update_kernel(
    meta, now_own, now_other, self_own, self_other, sum_own, sum_other, w3, w3_other,
    w0, w0_other, out, sent, now,
):
    mine, rest = window(meta[0]), window(1 - meta[0])
    for rows, latent, self_term, summed in (
        (mine, now_own, self_own, sum_own),
        (rest, now_other, self_other, sum_other),
    ):
        for cols, w in ((mine, w3), (rest, w3_other)):
            step = silu(self_term[:, cols] + dot(summed[...], w[...]))
            now[:, cols] = (latent[:, cols].astype(F32) + step).astype(BF16)
        out[rows, :] = now[:, mine]
        for cols, w in ((mine, w0), (rest, w0_other)):
            sent[rows, cols] = dot(now[...], w[...]).astype(BF16)


def decode_prepare_kernel(
    meta, own, other, w1, w1_other, w2, targets,
    before_own, before_near, before_skip, self_term, recv,
):
    mine, rest = window(meta[0]), window(1 - meta[0])
    for start in range(0, own.shape[0], HALF):
        rows = pl.ds(start, HALF)
        a, b = own[rows, :], other[rows, :]
        recv[rows, mine] = (dot(a, w1[mine, :]) + dot(b, w1[rest, :])).astype(BF16)
        recv[rows, rest] = (dot(a, w1_other[mine, :]) + dot(b, w1_other[rest, :])).astype(BF16)
        self_term[rows, :] = (dot(a, w2[mine, :]) + dot(b, w2[rest, :])).astype(BF16)
    half = before_own.shape[0]
    gather_slots(targets[REACH, :, window(meta[0], half)], recv, before_own)
    gather_slots(targets[near_offset(meta)], recv, before_near)
    gather_slots(targets[skip_offset(meta)], recv, before_skip)


def decode_messages(meta, offset, columns, sent, before, senders, message):
    from_row = senders[offset, :, columns]
    for start in range(0, before.shape[0], HALF):
        rows = pl.ds(start, HALF)
        hot = hot_columns(column(from_row[:, start : start + HALF]), sent.shape[0])
        pre = dot(hot, sent[...]) + before[rows, :].astype(F32)
        message[rows, :] = silu_message(pre)


def decode_scatter(row, message, total, first, out):
    for start in range(0, out.shape[0], HALF):
        value = dot(hot_rows(row - (first + start), HALF), message[...])
        if total is not None:
            value = value + total[pl.ds(first + start, HALF), :].astype(F32)
        out[pl.ds(start, HALF), :] = value.astype(BF16)


def decode_own_kernel(meta, sent, before, senders, targets, live, out, message):
    columns = window(meta[0], before.shape[0])
    decode_messages(meta, REACH, columns, sent, before, senders, message)
    decode_scatter(live_targets(targets, live, REACH, columns), message, None, 0, out)


def decode_near_kernel(meta, sent, before, senders, targets, live, total, out, message):
    offset = near_offset(meta)
    decode_messages(meta, offset, slice(None), sent, before, senders, message)
    decode_scatter(live_targets(targets, live, offset), message, total, 0, out)


def decode_skip_kernel(meta, sent, before, senders, targets, live, total, out, message):
    offset = skip_offset(meta)
    decode_messages(meta, offset, slice(None), sent, before, senders, message)
    decode_scatter(live_targets(targets, live, offset), message, total, 0, out)


def decode_rest_kernel(meta, message, targets, live, total, out):
    row = live_targets(targets, live, skip_offset(meta))
    decode_scatter(row, message, total, out.shape[0], out)


def final_kernel(first, meta, own, self_term, sum_own, sum_other, weights, *refs):
    out, w3 = refs[-1], weights.at[3]
    for start in range(0, out.shape[0], HALF):
        rows, from_rows = pl.ds(start, HALF), pl.ds(first + start, HALF)
        summed = sum_own[rows, :] + sum_other[rows, :]
        step = silu(self_term[from_rows, :].astype(F32) + dot(summed, w3[...]))
        out[rows, :] = (own[from_rows, :].astype(F32) + step).astype(BF16)


def body(
    grid_latent,
    mesh_latent,
    encode_weights,
    layer_weights,
    decode_weights,
    encode_senders,
    encode_targets,
    encode_live,
    mesh_senders,
    mesh_live,
    decode_senders,
    decode_targets,
    decode_live,
):
    meta = jnp.stack([lax.axis_index("feat"), lax.axis_index("band")]).astype(I32)
    grid_rows, cols = grid_latent.shape
    mesh_rows = mesh_latent.shape[0]
    full = 2 * cols
    senders, targets, live = (x.transpose(1, 0, 2) for x in (encode_senders, encode_targets, encode_live))
    slots = senders.shape[2]

    grid_other = swap(grid_latent)
    encode_other = swap(encode_weights)
    mesh_other = swap(mesh_latent)
    (begun,) = call(
        encode_begin_kernel,
        "encode_begin",
        (meta, grid_latent, encode_weights),
        [SMEM, whole(grid_latent), part(encode_weights, 0)],
        [shape(grid_rows, cols, dtype=F32)],
        2 * grid_rows * cols * cols,
    )
    grid_other, mesh_other = lax.optimization_barrier((grid_other, mesh_other))
    operands = (meta, grid_latent, grid_other, begun, encode_weights, encode_other, senders)
    sent, near_piece = call(
        encode_near_kernel,
        "encode_near",
        operands,
        [SMEM] + [whole(x) for x in operands[1:4]]
        + [part(encode_weights, 0), part(encode_other, 0), whole(senders)],
        [shape(grid_rows, full), shape(slots, full)],
        2 * full * (grid_rows * full + slots * grid_rows),
    )
    near_rows = exchange(near_piece, near_shift)
    layer_other = swap(after(layer_weights, near_piece))
    operands = (
        meta, mesh_latent, mesh_other, encode_weights, encode_other, sent, senders, targets
    )
    skip_piece, recv, before_near = call(
        encode_skip_kernel,
        "encode_skip",
        operands,
        [SMEM, whole(mesh_latent), whole(mesh_other)]
        + [part(encode_weights, 1), part(encode_other, 1)]
        + [whole(sent), whole(senders), whole(targets)],
        [shape(slots, full), shape(mesh_rows, full), shape(slots, full)],
        2 * full * (mesh_rows * full + slots * (grid_rows + mesh_rows)),
    )
    skip_rows = exchange(skip_piece, skip_shift)
    operands = (
        meta, near_rows, before_near, recv, sent, mesh_latent, mesh_other,
        encode_weights, encode_other, senders, targets, live,
    )
    total, before_skip, self_term = call(
        encode_near_sum_kernel,
        "encode_near_sum",
        operands,
        [SMEM] + [whole(x) for x in operands[1:7]]
        + [part(encode_weights, 2), part(encode_other, 2)]
        + [whole(x) for x in operands[9:]],
        [
            shape(mesh_rows, full, dtype=F32),
            shape(slots, full),
            shape(HALF, full),
        ],
        2 * full * mesh_rows * slots * 3,
        [pltpu.VMEM((slots, full), BF16), pltpu.VMEM((HALF, full), BF16)],
    )
    operands = (meta, skip_rows, before_skip, targets, live, total)
    sum_own, sum_other = call(
        encode_skip_sum_kernel,
        "encode_skip_sum",
        operands,
        [SMEM, whole(skip_rows), whole(before_skip), whole(targets), whole(live), whole(total)],
        [shape(HALF, full, dtype=F32), shape(HALF, full)],
        2 * full * mesh_rows * slots,
        [pltpu.VMEM((slots, full), BF16)],
    )
    operands = (
        meta, mesh_latent, mesh_other, self_term, sum_own, swap(sum_other),
        encode_weights, encode_other, layer_weights, layer_other,
    )
    now, edge = call(
        encode_update_kernel,
        "encode_update",
        operands,
        [SMEM] + [whole(x) for x in operands[1:6]]
        + [part(encode_weights, 3), part(encode_other, 3)]
        + [part(layer_weights, 0, 0), part(layer_other, 0, 0)],
        [shape(HALF, full), shape(MARGIN, full)],
        2 * HALF * full * full,
    )

    decode_other = swap(after(decode_weights, now))
    senders_t, live_t = mesh_senders.T, mesh_live.T
    degree = senders_t.shape[0]
    for layer in range(LAYERS):
        last = layer == LAYERS - 1
        far = exchange(edge, halo_shift)
        near = exchange(edge, halo_pairs)
        now_other = swap(now)
        operands = (meta, now, now_other) + (layer_weights, layer_other) * 3
        results = call(
            functools.partial(layer_project_kernel, last),
            f"layer_project_{layer}",
            operands,
            [SMEM, whole(now), whole(now_other)]
            + [part(operands[3 + i], layer, i // 2) for i in range(6)],
            [shape(HALF, full)] * (5 if last else 4),
            2 * HALF * full * full * 4,
        )
        sent_own, sent_other, recv, self_own = results[:4]
        operands = (meta, sent_own, sent_other, senders_t)
        (gathered,) = call(
            layer_gather_kernel,
            f"layer_gather_{layer}",
            operands,
            [SMEM, whole(sent_own), whole(sent_other), whole(senders_t)],
            [shape(degree, HALF, full)],
            2 * degree * HALF * full * mesh_rows,
        )
        operands = (meta, gathered, recv, near, far, senders_t, live_t)
        scratch = [pltpu.VMEM((2 * MARGIN, full), BF16)]
        sum_specs = (
            [SMEM] + [whole(x) for x in operands[1:5]]
            + [whole(senders_t), whole(live_t)]
        )
        if last:
            (summed,) = call(
                layer_sum_kernel,
                f"layer_sum_{layer}",
                operands,
                sum_specs,
                [shape(HALF, full)],
                2 * degree * HALF * full * 2 * MARGIN,
                scratch,
            )
            continue
        operands += (now, self_own) + (layer_weights, layer_other) * 2
        now, edge = call(
            layer_update_kernel,
            f"layer_update_{layer}",
            operands,
            sum_specs + [whole(now), whole(self_own)]
            + [part(layer_weights, layer, 3), part(layer_other, layer, 3)]
            + [part(layer_weights, layer + 1, 0), part(layer_other, layer + 1, 0)],
            [shape(HALF, full), shape(MARGIN, full)],
            2 * HALF * full * (degree * 2 * MARGIN + full),
            scratch + [pltpu.VMEM((HALF, full), BF16)],
        )
    operands = (
        meta, now, now_other, self_own, results[4], summed, swap(summed),
        layer_weights, layer_other, decode_weights, decode_other,
    )
    mesh_now, sent = call(
        last_update_kernel,
        "last_update",
        operands,
        [SMEM] + [whole(x) for x in operands[1:7]]
        + [part(layer_weights, LAYERS - 1, 3), part(layer_other, LAYERS - 1, 3)]
        + [part(decode_weights, 0), part(decode_other, 0)],
        [shape(mesh_rows, cols), shape(mesh_rows, full)],
        2 * mesh_rows * full * full * 2,
        [pltpu.VMEM((HALF, full), BF16)],
    )

    near_rows = exchange(sent, near_shift)
    skip_rows = exchange(sent, skip_shift)
    senders, targets, live = (x.transpose(1, 0, 2) for x in (decode_senders, decode_targets, decode_live))
    slots = senders.shape[2]
    operands = (
        meta, grid_latent, grid_other, decode_weights, decode_other, decode_weights, targets
    )
    before_own, before_near, before_skip, self_term = call(
        decode_prepare_kernel,
        "decode_prepare",
        operands,
        [SMEM, whole(grid_latent), whole(grid_other)]
        + [part(decode_weights, 1), part(decode_other, 1), part(decode_weights, 2), whole(targets)],
        [
            shape(slots // 2, full),
            shape(slots, full),
            shape(slots, full),
            shape(grid_rows, cols),
        ],
        2 * full * grid_rows * (full + 5 * slots // 2),
        [pltpu.VMEM((grid_rows, full), BF16)],
    )
    flops = 2 * full * slots * (grid_rows + mesh_rows)
    message_space = [pltpu.VMEM((slots, full), BF16)]
    operands = (meta, sent, before_own, senders, targets, live)
    (total,) = call(
        decode_own_kernel,
        "decode_own",
        operands,
        [SMEM] + [whole(x) for x in operands[1:]],
        [shape(grid_rows, full)],
        flops // 2,
        [pltpu.VMEM(before_own.shape, BF16)],
    )
    operands = (meta, near_rows, before_near, senders, targets, live, total)
    (total,) = call(
        decode_near_kernel,
        "decode_near",
        operands,
        [SMEM] + [whole(x) for x in operands[1:]],
        [shape(grid_rows, full)],
        flops,
        message_space,
    )
    half = grid_rows // 2
    operands = (meta, skip_rows, before_skip, senders, targets, live, total)
    head, message = call(
        decode_skip_kernel,
        "decode_skip",
        operands,
        [SMEM] + [whole(x) for x in operands[1:]],
        [shape(half, full), shape(slots, full)],
        flops,
    )
    operands = (meta, message, targets, live, total)
    (tail,) = call(
        decode_rest_kernel,
        "decode_rest",
        operands,
        [SMEM] + [whole(x) for x in operands[1:]],
        [shape(half, full)],
        flops // 2,
    )
    grid_now = None
    for index, summed in enumerate((head, tail)):
        block = pl.BlockSpec((half, cols), lambda i, index=index: (index, 0))
        operands = (meta, grid_latent, self_term, summed, swap(summed), decode_weights)
        specs = [SMEM] + [whole(x) for x in operands[1:]]
        aliases = {}
        if index:
            operands, specs, aliases = operands + (grid_now,), specs + [pl.BlockSpec(memory_space=pl.ANY)], {6: 0}
        grid_now = pl.pallas_call(
            functools.partial(final_kernel, index * half),
            name=f"final_update_{index}",
            grid=(1,),
            in_specs=specs,
            out_specs=block,
            out_shape=shape(grid_rows, cols),
            input_output_aliases=aliases,
            compiler_params=pltpu.CompilerParams(vmem_limit_bytes=VMEM_LIMIT),
        )(*operands)
    return mesh_now, grid_now


def solution(mesh):
    placed = (
        P("band", "feat"),
        P("band", "feat"),
        P(None, None, "feat"),
        P(None, None, None, "feat"),
        P(None, None, "feat"),
        P("band", None, None),
        P("band", None, None),
        P("band", None, None),
        P("band", None),
        P("band", None),
        P("band", None, None),
        P("band", None, None),
        P("band", None, None),
    )
    return jax.shard_map(
        body,
        mesh=mesh,
        in_specs=placed,
        out_specs=(P("band", "feat"), P("band", "feat")),
        check_vma=False,
    )
```

```python
import functools

import jax
import jax.numpy as jnp
from jax import lax
from jax.experimental import pallas as pl
from jax.experimental.pallas import tpu as pltpu
from jax.sharding import PartitionSpec as P

REACH = 2
LAYERS = 2
MARGIN = 64
HALF = 256
HELD = HALF + MARGIN
LANES = 128
F32 = jnp.float32
BF16 = jnp.bfloat16
I32 = jnp.int32
VMEM_LIMIT = 36 * 1024 * 1024


def swap(value):
    return lax.ppermute(value, "feat", [(0, 1), (1, 0)])


def flat(partners):
    return [(2 * s + c, 2 * t + e) for (s, c), (t, e) in partners.items()]


def shift(steps, up, count):
    partners = {}
    for s in range(count):
        partners[s, up] = (s + steps, up) if s + steps < count else (s, 1 - up)
        partners[s, 1 - up] = (s - steps, 1 - up) if s >= steps else (s, up)
    return flat(partners)


near_shift = functools.partial(shift, 1, 0)
skip_shift = functools.partial(shift, 2, 0)


def cross_pairs(count):
    partners = {}
    for s in range(count):
        other = s + 1 if s % 2 else s - 1
        for c in range(2):
            partners[s, c] = (other, c) if 0 <= other < count else (s, 1 - c)
    return flat(partners)


def line_pairs(count):
    return flat({(s, c): (s ^ 1, c) for s in range(count) for c in range(2)})


def exchange(value, pairs):
    return lax.ppermute(value, ("band", "feat"), pairs(lax.axis_size("band")))


def after(value, other):
    return lax.optimization_barrier((value, other))[0]


def silu(v):
    half = 0.5 * v
    return half + half * jnp.tanh(half)


def silu_message(v):
    half = v.astype(BF16) * BF16(0.5)
    return half + half * jnp.tanh(half)


def dot(a, b):
    return jnp.dot(a, b, preferred_element_type=F32)


def window(index, size=HALF):
    return pl.ds(pl.multiple_of(index * size, size), size)


def extra_rows(meta):
    return pl.ds(pl.multiple_of((1 - meta[0]) * (HALF - MARGIN), MARGIN), MARGIN)


def margin_rows(meta):
    return pl.ds(pl.multiple_of((1 - meta[0]) * (2 * HALF - MARGIN), MARGIN), MARGIN)


def near_offset(meta):
    return 3 - 2 * meta[0]


def skip_offset(meta):
    return 4 - 4 * meta[0]


def column(row):
    parts = [
        jnp.broadcast_to(row[:, start : start + LANES], (LANES, LANES)).T
        for start in range(0, row.shape[1], LANES)
    ]
    return parts[0] if len(parts) == 1 else jnp.concatenate(parts, axis=0)


def hot_columns(col, width):
    col = col.astype(jnp.int16)
    ids = lax.broadcasted_iota(I32, col.shape, 1).astype(jnp.int16)
    one, zero = BF16(1), BF16(0)
    parts = [
        jnp.where(col == ids + jnp.int16(start), one, zero) for start in range(0, width, LANES)
    ]
    return parts[0] if len(parts) == 1 else jnp.concatenate(parts, axis=1)


def hot_rows(row, height):
    ids = lax.broadcasted_iota(I32, (height, row.shape[1]), 0)
    return jnp.where(row == ids, 1.0, 0.0).astype(BF16)


class Part:
    def __init__(self, spec, index):
        self.spec, self.index = spec, index


def call(kernel, name, operands, specs, outs, flops, scratch=()):
    def viewed(*refs):
        refs = [
            ref.at[specs[i].index] if i < len(specs) and isinstance(specs[i], Part) else ref
            for i, ref in enumerate(refs)
        ]
        kernel(*refs)

    size = sum(x.size * x.dtype.itemsize for x in outs)
    return pl.pallas_call(
        viewed,
        name=name,
        grid=(1,),
        in_specs=[spec.spec if isinstance(spec, Part) else spec for spec in specs],
        out_specs=[whole(x) for x in outs],
        out_shape=list(outs),
        scratch_shapes=list(scratch),
        compiler_params=pltpu.CompilerParams(vmem_limit_bytes=VMEM_LIMIT),
        cost_estimate=pl.CostEstimate(
            flops=flops // 64, bytes_accessed=size // 64, transcendentals=0
        ),
    )(*operands)


def whole(x):
    return pl.BlockSpec(x.shape, lambda i, n=len(x.shape): (0,) * n)


def part(x, *index):
    return Part(whole(x), index)


SMEM = pl.BlockSpec(memory_space=pltpu.SMEM)


def shape(*dims, dtype=BF16):
    return jax.ShapeDtypeStruct(dims, dtype)


def encode_begin_kernel(meta, own, w_own, out):
    out[...] = dot(own[pl.ds(0, HALF), :], w_own[window(meta[0]), :])


def gather_slots(senders_row, sent, out):
    for start in range(0, senders_row.shape[1], HALF):
        col = column(senders_row[:, start : start + HALF])
        out[pl.ds(start, HALF), :] = dot(hot_columns(col, sent.shape[0]), sent[...]).astype(BF16)


def encode_near_kernel(meta, own, other, begun, w_own, w_other, senders, sent, piece):
    mine, rest = window(meta[0]), window(1 - meta[0])
    for start in range(0, own.shape[0], HALF):
        rows = pl.ds(start, HALF)
        a, b = own[rows, :], other[rows, :]
        first = begun[...] if start == 0 else dot(a, w_own[mine, :])
        sent[rows, mine] = (first + dot(b, w_own[rest, :])).astype(BF16)
        sent[rows, rest] = (dot(a, w_other[mine, :]) + dot(b, w_other[rest, :])).astype(BF16)
    gather_slots(senders[near_offset(meta)], sent, piece)


def live_targets(targets, live, offset, columns=slice(None)):
    return jnp.where(live[offset, :, columns] > 0, targets[offset, :, columns], -1)


def encode_skip_kernel(
    meta, own, other, w1, w1_other, sent, senders, targets, piece, recv, before
):
    gather_slots(senders[skip_offset(meta)], sent, piece)
    mine, rest = window(meta[0]), window(1 - meta[0])
    for start in range(0, own.shape[0], HALF):
        rows = pl.ds(start, HALF)
        a, b = own[rows, :], other[rows, :]
        recv[rows, mine] = (dot(a, w1[mine, :]) + dot(b, w1[rest, :])).astype(BF16)
        recv[rows, rest] = (dot(a, w1_other[mine, :]) + dot(b, w1_other[rest, :])).astype(BF16)
    gather_slots(targets[near_offset(meta)], recv, before)


def encode_near_sum_kernel(
    meta, rows, before, recv, sent, own, other, w2, w2_other, senders, targets, live,
    total, before_skip, self_term, message, own_message,
):
    mine, rest = window(meta[0]), window(1 - meta[0])
    nodes = recv.shape[0]
    from_rows = hot_columns(column(senders[REACH, :, mine]), sent.shape[0])
    to_rows = hot_columns(column(targets[REACH, :, mine]), nodes)
    own_message[...] = silu_message(dot(from_rows, sent[...]) + dot(to_rows, recv[...]))
    message[...] = silu_message(rows[...] + before[...])
    row = live_targets(targets, live, near_offset(meta))
    own_row = live_targets(targets, live, REACH, mine)
    for start in range(0, nodes, HALF):
        value = dot(hot_rows(row - start, HALF), message[...])
        value = value + dot(hot_rows(own_row - start, HALF), own_message[...])
        total[pl.ds(start, HALF), :] = value
    gather_slots(targets[skip_offset(meta)], recv, before_skip)
    far = margin_rows(meta)
    for held, rows in ((pl.ds(0, HALF), mine), (pl.ds(HALF, MARGIN), far)):
        a, b = own[rows, :], other[rows, :]
        self_term[held, mine] = (dot(a, w2[mine, :]) + dot(b, w2[rest, :])).astype(BF16)
        self_term[held, rest] = (dot(a, w2_other[mine, :]) + dot(b, w2_other[rest, :])).astype(BF16)


def encode_skip_sum_kernel(
    meta, rows, before, targets, live, total, out_own, out_other, message, halves
):
    message[...] = silu_message(rows[...] + before[...])
    row = live_targets(targets, live, skip_offset(meta))
    for index, half in enumerate((1 - meta[0], meta[0])):
        value = dot(hot_rows(row - half * HALF, HALF), message[...]) + total[window(half), :]
        halves[index] = value.astype(BF16)
    held, far = pl.ds(0, HALF), pl.ds(HALF, MARGIN)
    out_own[held, :] = halves[1]
    out_own[far, :] = halves[0, extra_rows(meta), :]
    out_other[held, :] = halves[0]
    start = pl.multiple_of(meta[0] * (HALF - MARGIN), MARGIN)
    out_other[far, :] = halves[1, pl.ds(start, MARGIN), :]


def put_edges(meta, now, w0, w0_other, cross, line):
    mine, rest = window(meta[0]), window(1 - meta[0])
    odd = meta[1] % 2
    head, tail = HALF * meta[0], HALF - MARGIN * meta[0]
    for edge, start in (
        (cross, (1 - odd) * head + odd * tail),
        (line, (1 - odd) * tail + odd * head),
    ):
        rows = now[pl.ds(pl.multiple_of(start, MARGIN), MARGIN), :]
        edge[:, mine] = dot(rows, w0[...]).astype(BF16)
        edge[:, rest] = dot(rows, w0_other[...]).astype(BF16)


def encode_update_kernel(
    meta, own, other, self_term, sum_own, sum_other, w3, w3_other, w0, w0_other,
    now, cross, line, held_now,
):
    mine, rest = window(meta[0]), window(1 - meta[0])
    summed = sum_own[...] + sum_other[...]
    far = margin_rows(meta)
    for cols, latent, w in ((mine, own, w3), (rest, other, w3_other)):
        step = silu(self_term[:, cols].astype(F32) + dot(summed, w[...]))
        for held, rows in ((slice(0, HALF), mine), (slice(HALF, HELD), far)):
            held_now[held, cols] = (latent[rows, :].astype(F32) + step[held, :]).astype(BF16)
    now[...] = held_now[pl.ds(0, HALF), :]
    put_edges(meta, held_now, w0, w0_other, cross, line)


def layer_project_kernel(
    last, meta, own, other, w0, w0_other, w1, w1_other, w2, w2_other,
    sent_own, sent_other, recv, self_own, *self_other,
):
    mine, rest = window(meta[0]), window(1 - meta[0])
    held, far = pl.ds(0, HALF), pl.ds(HALF, MARGIN)
    for cols, w in ((mine, w0), (rest, w0_other)):
        sent_own[:, cols] = dot(own[...], w[...]).astype(BF16)
        sent_other[:, cols] = dot(other[...], w[...]).astype(BF16)
    for cols, w in ((mine, w1), (rest, w1_other)):
        recv[held, cols] = dot(own[...], w[...]).astype(BF16)
        if not last:
            recv[far, cols] = dot(other[extra_rows(meta), :], w[...]).astype(BF16)
    for cols, w in ((mine, w2), (rest, w2_other)):
        self_own[held, cols] = dot(own[...], w[...]).astype(BF16)
        if last:
            self_other[0][:, cols] = dot(other[...], w[...]).astype(BF16)
        else:
            self_own[far, cols] = dot(other[extra_rows(meta), :], w[...]).astype(BF16)


def held_slots(meta, slots):
    tail = pltpu.roll(slots[:, 2 * HALF - LANES :], LANES - MARGIN, 1)
    far = jnp.where(meta[0] == 0, tail, slots[:, :LANES])
    return jnp.concatenate([slots[:, window(meta[0])], far], axis=1)


def layer_gather_kernel(meta, own, other, senders, out):
    base = meta[1] * (2 * HALF)
    nodes = out.shape[1]
    held = held_slots(meta, senders) - base
    for k in range(senders.shape[0]):
        local = held[k : k + 1, :]
        col = column(local - meta[0] * HALF)[:nodes]
        col_other = column(local - (1 - meta[0]) * HALF)[:nodes]
        value = dot(hot_columns(col, HALF), own[...])
        value = value + dot(hot_columns(col_other, HALF), other[...])
        out[k] = value.astype(BF16)


def layer_sum(meta, gathered, recv, cross, line, senders, live, halo, total):
    nodes = 2 * HALF
    base = meta[1] * nodes
    count, held = gathered.shape[0], gathered.shape[1]
    hots, flags = [], []
    slots, alive = held_slots(meta, senders) - base, held_slots(meta, live)
    for k in range(count):
        local = slots[k : k + 1, :]
        where = jnp.where(local < 0, local + MARGIN, local - nodes + MARGIN)
        where = jnp.where((local >= 0) & (local < nodes), -1, where)
        hots.append(hot_columns(column(where)[:held], 2 * MARGIN))
        flags.append(column(alive[k : k + 1, :])[:held].astype(BF16))
    odd = meta[1] % 2
    halo[pl.ds(pl.multiple_of(odd * MARGIN, MARGIN), MARGIN), :] = cross[...]
    halo[pl.ds(pl.multiple_of((1 - odd) * MARGIN, MARGIN), MARGIN), :] = line[...]
    outside = dot(jnp.concatenate(hots, axis=0), halo[...]).astype(BF16)
    step = 32
    for start in range(0, held, step):
        rows = pl.ds(start, step)
        side = recv[rows, :]
        running = None
        for k in range(count):
            row = k * held + start
            message = silu_message(outside[row : row + step, :] + gathered[k, rows, :] + side)
            flag = jnp.concatenate([flags[k][start : start + step, :]] * 4, axis=1)
            message = (message * flag).astype(F32)
            running = message if running is None else running + message
        total[rows, :] = running.astype(BF16)


def layer_update_kernel(
    meta, gathered, recv, line, cross, senders, live, now, now_other, self_term,
    w3, w3_other, w0, w0_other, out, edge_cross, edge_line, halo, total, held_now,
):
    mine, rest = window(meta[0]), window(1 - meta[0])
    layer_sum(meta, gathered, recv, cross, line, senders, live, halo, total)
    summed = total[...]
    for cols, w in ((mine, w3), (rest, w3_other)):
        step = silu(self_term[:, cols].astype(F32) + dot(summed, w[...]))
        far = now_other[extra_rows(meta), cols].astype(F32)
        held_now[pl.ds(0, HALF), cols] = (now[:, cols].astype(F32) + step[:HALF]).astype(BF16)
        held_now[pl.ds(HALF, MARGIN), cols] = (far + step[HALF:]).astype(BF16)
    out[...] = held_now[pl.ds(0, HALF), :]
    put_edges(meta, held_now, w0, w0_other, edge_cross, edge_line)


def layer_sum_kernel(meta, gathered, recv, cross, line, senders, live, out, halo):
    layer_sum(meta, gathered, recv, cross, line, senders, live, halo, out)


def last_update_kernel(
    meta, now_own, now_other, self_own, self_other, sum_own, sum_other, w3, w3_other,
    w0, w0_other, out, sent, now,
):
    mine, rest = window(meta[0]), window(1 - meta[0])
    for rows, latent, self_term, summed in (
        (mine, now_own, self_own, sum_own),
        (rest, now_other, self_other, sum_other),
    ):
        for cols, w in ((mine, w3), (rest, w3_other)):
            step = silu(self_term[:, cols] + dot(summed[...], w[...]))
            now[:, cols] = (latent[:, cols].astype(F32) + step).astype(BF16)
        out[rows, :] = now[:, mine]
        for cols, w in ((mine, w0), (rest, w0_other)):
            sent[rows, cols] = dot(now[...], w[...]).astype(BF16)


def decode_prepare_kernel(
    meta, own, other, w1, w1_other, w2, targets, mesh_now,
    before_own, before_near, before_skip, self_term, mesh_out, recv,
):
    mesh_out[...] = mesh_now[...]
    mine, rest = window(meta[0]), window(1 - meta[0])
    for start in range(0, own.shape[0], HALF):
        rows = pl.ds(start, HALF)
        a, b = own[rows, :], other[rows, :]
        recv[rows, mine] = (dot(a, w1[mine, :]) + dot(b, w1[rest, :])).astype(BF16)
        recv[rows, rest] = (dot(a, w1_other[mine, :]) + dot(b, w1_other[rest, :])).astype(BF16)
        self_term[rows, :] = (dot(a, w2[mine, :]) + dot(b, w2[rest, :])).astype(BF16)
    half = before_own.shape[0]
    gather_slots(targets[REACH, :, window(meta[0], half)], recv, before_own)
    gather_slots(targets[near_offset(meta)], recv, before_near)
    gather_slots(targets[skip_offset(meta)], recv, before_skip)


def decode_messages(meta, offset, columns, sent, before, senders, message):
    from_row = senders[offset, :, columns]
    for start in range(0, before.shape[0], HALF):
        rows = pl.ds(start, HALF)
        hot = hot_columns(column(from_row[:, start : start + HALF]), sent.shape[0])
        pre = dot(hot, sent[...]) + before[rows, :].astype(F32)
        message[rows, :] = silu_message(pre)


def decode_scatter(row, message, total, first, out):
    for start in range(0, out.shape[0], HALF):
        value = dot(hot_rows(row - (first + start), HALF), message[...])
        if total is not None:
            value = value + total[pl.ds(first + start, HALF), :].astype(F32)
        out[pl.ds(start, HALF), :] = value.astype(BF16)


def decode_own_kernel(meta, sent, before, senders, targets, live, out, message):
    columns = window(meta[0], before.shape[0])
    decode_messages(meta, REACH, columns, sent, before, senders, message)
    decode_scatter(live_targets(targets, live, REACH, columns), message, None, 0, out)


def decode_near_kernel(meta, sent, before, senders, targets, live, total, out, message):
    offset = near_offset(meta)
    decode_messages(meta, offset, slice(None), sent, before, senders, message)
    decode_scatter(live_targets(targets, live, offset), message, total, 0, out)


def decode_skip_kernel(meta, sent, before, senders, targets, live, total, out, message):
    offset = skip_offset(meta)
    decode_messages(meta, offset, slice(None), sent, before, senders, message)
    decode_scatter(live_targets(targets, live, offset), message, total, 0, out)


def decode_rest_kernel(meta, message, targets, live, total, out):
    row = live_targets(targets, live, skip_offset(meta))
    decode_scatter(row, message, total, out.shape[0], out)


def final_kernel(first, meta, own, self_term, sum_own, sum_other, weights, *refs):
    out, w3 = refs[-1], weights.at[3]
    for start in range(0, out.shape[0], HALF):
        rows, from_rows = pl.ds(start, HALF), pl.ds(first + start, HALF)
        summed = sum_own[rows, :] + sum_other[rows, :]
        step = silu(self_term[from_rows, :].astype(F32) + dot(summed, w3[...]))
        out[rows, :] = (own[from_rows, :].astype(F32) + step).astype(BF16)


def body(
    grid_latent,
    mesh_latent,
    encode_weights,
    layer_weights,
    decode_weights,
    encode_senders,
    encode_targets,
    encode_live,
    mesh_senders,
    mesh_live,
    decode_senders,
    decode_targets,
    decode_live,
):
    meta = jnp.stack([lax.axis_index("feat"), lax.axis_index("band")]).astype(I32)
    grid_rows, cols = grid_latent.shape
    mesh_rows = mesh_latent.shape[0]
    full = 2 * cols
    senders, targets, live = (x.transpose(1, 0, 2) for x in (encode_senders, encode_targets, encode_live))
    slots = senders.shape[2]

    grid_other = swap(grid_latent)
    encode_other = swap(encode_weights)
    mesh_other = swap(mesh_latent)
    (begun,) = call(
        encode_begin_kernel,
        "encode_begin",
        (meta, grid_latent, encode_weights),
        [SMEM, whole(grid_latent), part(encode_weights, 0)],
        [shape(HALF, cols, dtype=F32)],
        2 * HALF * cols * cols,
    )
    grid_other, mesh_other = lax.optimization_barrier((grid_other, mesh_other))
    operands = (meta, grid_latent, grid_other, begun, encode_weights, encode_other, senders)
    sent, near_piece = call(
        encode_near_kernel,
        "encode_near",
        operands,
        [SMEM] + [whole(x) for x in operands[1:4]]
        + [part(encode_weights, 0), part(encode_other, 0), whole(senders)],
        [shape(grid_rows, full), shape(slots, full)],
        2 * full * (grid_rows * full + slots * grid_rows),
    )
    near_rows = exchange(near_piece, near_shift)
    layer_other = swap(after(layer_weights, near_piece))
    operands = (
        meta, mesh_latent, mesh_other, encode_weights, encode_other, sent, senders, targets
    )
    skip_piece, recv, before_near = call(
        encode_skip_kernel,
        "encode_skip",
        operands,
        [SMEM, whole(mesh_latent), whole(mesh_other)]
        + [part(encode_weights, 1), part(encode_other, 1)]
        + [whole(sent), whole(senders), whole(targets)],
        [shape(slots, full), shape(mesh_rows, full), shape(slots, full)],
        2 * full * (mesh_rows * full + slots * (grid_rows + mesh_rows)),
    )
    skip_rows = exchange(skip_piece, skip_shift)
    operands = (
        meta, near_rows, before_near, recv, sent, mesh_latent, mesh_other,
        encode_weights, encode_other, senders, targets, live,
    )
    total, before_skip, self_term = call(
        encode_near_sum_kernel,
        "encode_near_sum",
        operands,
        [SMEM] + [whole(x) for x in operands[1:7]]
        + [part(encode_weights, 2), part(encode_other, 2)]
        + [whole(x) for x in operands[9:]],
        [
            shape(mesh_rows, full, dtype=F32),
            shape(slots, full),
            shape(HELD, full),
        ],
        2 * full * mesh_rows * slots * 3,
        [pltpu.VMEM((slots, full), BF16), pltpu.VMEM((HALF, full), BF16)],
    )
    operands = (meta, skip_rows, before_skip, targets, live, total)
    sum_own, sum_other = call(
        encode_skip_sum_kernel,
        "encode_skip_sum",
        operands,
        [SMEM, whole(skip_rows), whole(before_skip), whole(targets), whole(live), whole(total)],
        [shape(HELD, full), shape(HELD, full)],
        2 * full * mesh_rows * slots,
        [pltpu.VMEM((slots, full), BF16), pltpu.VMEM((2, HALF, full), BF16)],
    )
    sum_arrived = swap(sum_other)
    decode_other = swap(after(decode_weights, sum_other))
    operands = (
        meta, mesh_latent, mesh_other, self_term, sum_own, sum_arrived,
        encode_weights, encode_other, layer_weights, layer_other,
    )
    now, cross_edge, line_edge = call(
        encode_update_kernel,
        "encode_update",
        operands,
        [SMEM] + [whole(x) for x in operands[1:6]]
        + [part(encode_weights, 3), part(encode_other, 3)]
        + [part(layer_weights, 0, 0), part(layer_other, 0, 0)],
        [shape(HALF, full), shape(MARGIN, full), shape(MARGIN, full)],
        2 * HALF * full * full,
        [pltpu.VMEM((HELD, full), BF16)],
    )

    senders_t, live_t = mesh_senders.T, mesh_live.T
    degree = senders_t.shape[0]
    for layer in range(LAYERS):
        last = layer == LAYERS - 1
        cross = exchange(cross_edge, cross_pairs)
        line = exchange(line_edge, line_pairs)
        now_other = swap(now)
        operands = (meta, now, now_other) + (layer_weights, layer_other) * 3
        results = call(
            functools.partial(layer_project_kernel, last),
            f"layer_project_{layer}",
            operands,
            [SMEM, whole(now), whole(now_other)]
            + [part(operands[3 + i], layer, i // 2) for i in range(6)],
            [shape(HALF, full)] * 2 + [shape(HALF if last else HELD, full)] * 2
            + [shape(HALF, full)] * last,
            2 * HALF * full * full * 4,
        )
        sent_own, sent_other, recv, self_own = results[:4]
        operands = (meta, sent_own, sent_other, senders_t)
        (gathered,) = call(
            layer_gather_kernel,
            f"layer_gather_{layer}",
            operands,
            [SMEM, whole(sent_own), whole(sent_other), whole(senders_t)],
            [shape(degree, HALF if last else HELD, full)],
            2 * degree * HALF * full * mesh_rows,
        )
        halo = (cross, line) if last else (line, cross)
        operands = (meta, gathered, recv) + halo + (senders_t, live_t)
        scratch = [pltpu.VMEM((2 * MARGIN, full), BF16)]
        sum_specs = (
            [SMEM] + [whole(x) for x in operands[1:5]]
            + [whole(senders_t), whole(live_t)]
        )
        if last:
            (summed,) = call(
                layer_sum_kernel,
                f"layer_sum_{layer}",
                operands,
                sum_specs,
                [shape(HALF, full)],
                2 * degree * HALF * full * 2 * MARGIN,
                scratch,
            )
            continue
        operands += (now, now_other, self_own) + (layer_weights, layer_other) * 2
        now, cross_edge, line_edge = call(
            layer_update_kernel,
            f"layer_update_{layer}",
            operands,
            sum_specs + [whole(now), whole(now_other), whole(self_own)]
            + [part(layer_weights, layer, 3), part(layer_other, layer, 3)]
            + [part(layer_weights, layer + 1, 0), part(layer_other, layer + 1, 0)],
            [shape(HALF, full), shape(MARGIN, full), shape(MARGIN, full)],
            2 * HALF * full * (degree * 2 * MARGIN + full),
            scratch + [pltpu.VMEM((HELD, full), BF16)] * 2,
        )
    operands = (
        meta, now, now_other, self_own, results[4], summed, swap(summed),
        layer_weights, layer_other, decode_weights, decode_other,
    )
    mesh_now, sent = call(
        last_update_kernel,
        "last_update",
        operands,
        [SMEM] + [whole(x) for x in operands[1:7]]
        + [part(layer_weights, LAYERS - 1, 3), part(layer_other, LAYERS - 1, 3)]
        + [part(decode_weights, 0), part(decode_other, 0)],
        [shape(mesh_rows, cols), shape(mesh_rows, full)],
        2 * mesh_rows * full * full * 2,
        [pltpu.VMEM((HALF, full), BF16)],
    )

    near_rows = exchange(sent, near_shift)
    skip_rows = exchange(sent, skip_shift)
    senders, targets, live = (x.transpose(1, 0, 2) for x in (decode_senders, decode_targets, decode_live))
    slots = senders.shape[2]
    operands = (
        meta, grid_latent, grid_other, decode_weights, decode_other, decode_weights, targets,
        mesh_now,
    )
    before_own, before_near, before_skip, self_term, mesh_now = call(
        decode_prepare_kernel,
        "decode_prepare",
        operands,
        [SMEM, whole(grid_latent), whole(grid_other)]
        + [part(decode_weights, 1), part(decode_other, 1), part(decode_weights, 2), whole(targets)]
        + [whole(mesh_now)],
        [
            shape(slots // 2, full),
            shape(slots, full),
            shape(slots, full),
            shape(grid_rows, cols),
            shape(mesh_rows, cols),
        ],
        2 * full * grid_rows * (full + 5 * slots // 2),
        [pltpu.VMEM((grid_rows, full), BF16)],
    )
    flops = 2 * full * slots * (grid_rows + mesh_rows)
    message_space = [pltpu.VMEM((slots, full), BF16)]
    operands = (meta, sent, before_own, senders, targets, live)
    (total,) = call(
        decode_own_kernel,
        "decode_own",
        operands,
        [SMEM] + [whole(x) for x in operands[1:]],
        [shape(grid_rows, full)],
        flops // 2,
        [pltpu.VMEM(before_own.shape, BF16)],
    )
    operands = (meta, near_rows, before_near, senders, targets, live, total)
    (total,) = call(
        decode_near_kernel,
        "decode_near",
        operands,
        [SMEM] + [whole(x) for x in operands[1:]],
        [shape(grid_rows, full)],
        flops,
        message_space,
    )
    half = grid_rows // 2
    operands = (meta, skip_rows, before_skip, senders, targets, live, total)
    head, message = call(
        decode_skip_kernel,
        "decode_skip",
        operands,
        [SMEM] + [whole(x) for x in operands[1:]],
        [shape(half, full), shape(slots, full)],
        flops,
    )
    operands = (meta, message, targets, live, total)
    (tail,) = call(
        decode_rest_kernel,
        "decode_rest",
        operands,
        [SMEM] + [whole(x) for x in operands[1:]],
        [shape(half, full)],
        flops // 2,
    )
    grid_now = None
    for index, summed in enumerate((head, tail)):
        block = pl.BlockSpec((half, cols), lambda i, index=index: (index, 0))
        operands = (meta, grid_latent, self_term, summed, swap(summed), decode_weights)
        specs = [SMEM] + [whole(x) for x in operands[1:]]
        aliases = {}
        if index:
            operands, specs, aliases = operands + (grid_now,), specs + [pl.BlockSpec(memory_space=pl.ANY)], {6: 0}
        grid_now = pl.pallas_call(
            functools.partial(final_kernel, index * half),
            name=f"final_update_{index}",
            grid=(1,),
            in_specs=specs,
            out_specs=block,
            out_shape=shape(grid_rows, cols),
            input_output_aliases=aliases,
            compiler_params=pltpu.CompilerParams(vmem_limit_bytes=VMEM_LIMIT),
        )(*operands)
    return mesh_now, grid_now


def solution(mesh):
    placed = (
        P("band", "feat"),
        P("band", "feat"),
        P(None, None, "feat"),
        P(None, None, None, "feat"),
        P(None, None, "feat"),
        P("band", None, None),
        P("band", None, None),
        P("band", None, None),
        P("band", None),
        P("band", None),
        P("band", None, None),
        P("band", None, None),
        P("band", None, None),
    )
    return jax.shard_map(
        body,
        mesh=mesh,
        in_specs=placed,
        out_specs=(P("band", "feat"), P("band", "feat")),
        check_vma=False,
    )
```

```python
import functools

import jax
import jax.numpy as jnp
from jax import lax
from jax.experimental import pallas as pl
from jax.experimental.pallas import tpu as pltpu
from jax.sharding import PartitionSpec as P

REACH = 2
LAYERS = 2
MARGIN = 64
HALF = 256
HELD = HALF + MARGIN
LANES = 128
F32 = jnp.float32
BF16 = jnp.bfloat16
I32 = jnp.int32
VMEM_LIMIT = 36 * 1024 * 1024


def swap(value):
    return lax.ppermute(value, "feat", [(0, 1), (1, 0)])


def flat(partners):
    return [(2 * s + c, 2 * t + e) for (s, c), (t, e) in partners.items()]


def shift(steps, up, count):
    partners = {}
    for s in range(count):
        partners[s, up] = (s + steps, up) if s + steps < count else (s, 1 - up)
        partners[s, 1 - up] = (s - steps, 1 - up) if s >= steps else (s, up)
    return flat(partners)


near_shift = functools.partial(shift, 1, 0)
skip_shift = functools.partial(shift, 2, 0)


def cross_pairs(count):
    partners = {}
    for s in range(count):
        other = s + 1 if s % 2 else s - 1
        for c in range(2):
            partners[s, c] = (other, c) if 0 <= other < count else (s, 1 - c)
    return flat(partners)


def line_pairs(count):
    return flat({(s, c): (s ^ 1, c) for s in range(count) for c in range(2)})


def exchange(value, pairs):
    return lax.ppermute(value, ("band", "feat"), pairs(lax.axis_size("band")))


def after(value, other):
    return lax.optimization_barrier((value, other))[0]


def silu(v):
    half = 0.5 * v
    return half + half * jnp.tanh(half)


def silu_message(v):
    half = v.astype(BF16) * BF16(0.5)
    return half + half * jnp.tanh(half)


def dot(a, b):
    return jnp.dot(a, b, preferred_element_type=F32)


def window(index, size=HALF):
    return pl.ds(pl.multiple_of(index * size, size), size)


def extra_rows(meta):
    return pl.ds(pl.multiple_of((1 - meta[0]) * (HALF - MARGIN), MARGIN), MARGIN)


def margin_rows(meta):
    return pl.ds(pl.multiple_of((1 - meta[0]) * (2 * HALF - MARGIN), MARGIN), MARGIN)


def near_offset(meta):
    return 3 - 2 * meta[0]


def skip_offset(meta):
    return 4 - 4 * meta[0]


def column(row):
    parts = [
        jnp.broadcast_to(row[:, start : start + LANES], (LANES, LANES)).T
        for start in range(0, row.shape[1], LANES)
    ]
    return parts[0] if len(parts) == 1 else jnp.concatenate(parts, axis=0)


def hot_columns(col, width):
    col = col.astype(jnp.int16)
    ids = lax.broadcasted_iota(I32, col.shape, 1).astype(jnp.int16)
    one, zero = BF16(1), BF16(0)
    parts = [
        jnp.where(col == ids + jnp.int16(start), one, zero) for start in range(0, width, LANES)
    ]
    return parts[0] if len(parts) == 1 else jnp.concatenate(parts, axis=1)


def hot_rows(row, height):
    ids = lax.broadcasted_iota(I32, (height, row.shape[1]), 0)
    return jnp.where(row == ids, 1.0, 0.0).astype(BF16)


class Part:
    def __init__(self, spec, index):
        self.spec, self.index = spec, index


def call(kernel, name, operands, specs, outs, flops, scratch=()):
    def viewed(*refs):
        refs = [
            ref.at[specs[i].index] if i < len(specs) and isinstance(specs[i], Part) else ref
            for i, ref in enumerate(refs)
        ]
        kernel(*refs)

    size = sum(x.size * x.dtype.itemsize for x in outs)
    return pl.pallas_call(
        viewed,
        name=name,
        grid=(1,),
        in_specs=[spec.spec if isinstance(spec, Part) else spec for spec in specs],
        out_specs=[whole(x) for x in outs],
        out_shape=list(outs),
        scratch_shapes=list(scratch),
        compiler_params=pltpu.CompilerParams(vmem_limit_bytes=VMEM_LIMIT),
        cost_estimate=pl.CostEstimate(
            flops=flops // 64, bytes_accessed=size // 64, transcendentals=0
        ),
    )(*operands)


def whole(x):
    return pl.BlockSpec(x.shape, lambda i, n=len(x.shape): (0,) * n)


def part(x, *index):
    return Part(whole(x), index)


SMEM = pl.BlockSpec(memory_space=pltpu.SMEM)


def shape(*dims, dtype=BF16):
    return jax.ShapeDtypeStruct(dims, dtype)


def encode_begin_kernel(meta, own, w_own, out):
    for start in range(0, own.shape[0], HALF):
        rows = pl.ds(start, HALF)
        out[rows, :] = dot(own[rows, :], w_own[window(meta[0]), :])


def gather_slots(senders_row, sent, out):
    for start in range(0, senders_row.shape[1], HALF):
        col = column(senders_row[:, start : start + HALF])
        out[pl.ds(start, HALF), :] = dot(hot_columns(col, sent.shape[0]), sent[...]).astype(BF16)


def encode_near_kernel(meta, own, other, begun, w_own, w_other, senders, sent, piece):
    mine, rest = window(meta[0]), window(1 - meta[0])
    for start in range(0, own.shape[0], HALF):
        rows = pl.ds(start, HALF)
        a, b = own[rows, :], other[rows, :]
        sent[rows, mine] = (begun[rows, :] + dot(b, w_own[rest, :])).astype(BF16)
        sent[rows, rest] = (dot(a, w_other[mine, :]) + dot(b, w_other[rest, :])).astype(BF16)
    gather_slots(senders[near_offset(meta)], sent, piece)


def live_targets(targets, live, offset, columns=slice(None)):
    return jnp.where(live[offset, :, columns] > 0, targets[offset, :, columns], -1)


def encode_skip_kernel(
    meta, own, other, w1, w1_other, sent, senders, targets, piece, recv, before
):
    gather_slots(senders[skip_offset(meta)], sent, piece)
    mine, rest = window(meta[0]), window(1 - meta[0])
    for start in range(0, own.shape[0], HALF):
        rows = pl.ds(start, HALF)
        a, b = own[rows, :], other[rows, :]
        recv[rows, mine] = (dot(a, w1[mine, :]) + dot(b, w1[rest, :])).astype(BF16)
        recv[rows, rest] = (dot(a, w1_other[mine, :]) + dot(b, w1_other[rest, :])).astype(BF16)
    gather_slots(targets[near_offset(meta)], recv, before)


def encode_near_sum_kernel(
    meta, rows, before, recv, sent, own, other, w2, w2_other, senders, targets, live,
    total, before_skip, self_term, message, own_message,
):
    mine, rest = window(meta[0]), window(1 - meta[0])
    nodes = recv.shape[0]
    from_rows = hot_columns(column(senders[REACH, :, mine]), sent.shape[0])
    to_rows = hot_columns(column(targets[REACH, :, mine]), nodes)
    own_message[...] = silu_message(dot(from_rows, sent[...]) + dot(to_rows, recv[...]))
    message[...] = silu_message(rows[...] + before[...])
    row = live_targets(targets, live, near_offset(meta))
    own_row = live_targets(targets, live, REACH, mine)
    for start in range(0, nodes, HALF):
        value = dot(hot_rows(row - start, HALF), message[...])
        value = value + dot(hot_rows(own_row - start, HALF), own_message[...])
        total[pl.ds(start, HALF), :] = value
    gather_slots(targets[skip_offset(meta)], recv, before_skip)
    far = margin_rows(meta)
    for held, rows in ((pl.ds(0, HALF), mine), (pl.ds(HALF, MARGIN), far)):
        a, b = own[rows, :], other[rows, :]
        self_term[held, mine] = (dot(a, w2[mine, :]) + dot(b, w2[rest, :])).astype(BF16)
        self_term[held, rest] = (dot(a, w2_other[mine, :]) + dot(b, w2_other[rest, :])).astype(BF16)


def encode_skip_sum_kernel(
    meta, rows, before, targets, live, total, out_own, out_other, message, halves
):
    message[...] = silu_message(rows[...] + before[...])
    row = live_targets(targets, live, skip_offset(meta))
    for index, half in enumerate((1 - meta[0], meta[0])):
        value = dot(hot_rows(row - half * HALF, HALF), message[...]) + total[window(half), :]
        halves[index] = value.astype(BF16)
    held, far = pl.ds(0, HALF), pl.ds(HALF, MARGIN)
    out_own[held, :] = halves[1]
    out_own[far, :] = halves[0, extra_rows(meta), :]
    out_other[held, :] = halves[0]
    start = pl.multiple_of(meta[0] * (HALF - MARGIN), MARGIN)
    out_other[far, :] = halves[1, pl.ds(start, MARGIN), :]


def put_edges(meta, now, w0, w0_other, cross, line):
    mine, rest = window(meta[0]), window(1 - meta[0])
    odd = meta[1] % 2
    head, tail = HALF * meta[0], HALF - MARGIN * meta[0]
    for edge, start in (
        (cross, (1 - odd) * head + odd * tail),
        (line, (1 - odd) * tail + odd * head),
    ):
        rows = now[pl.ds(pl.multiple_of(start, MARGIN), MARGIN), :]
        edge[:, mine] = dot(rows, w0[...]).astype(BF16)
        edge[:, rest] = dot(rows, w0_other[...]).astype(BF16)


def encode_update_kernel(
    meta, own, other, self_term, sum_own, sum_other, w3, w3_other, w0, w0_other,
    now, cross, line, held_now,
):
    mine, rest = window(meta[0]), window(1 - meta[0])
    summed = sum_own[...] + sum_other[...]
    far = margin_rows(meta)
    for cols, latent, w in ((mine, own, w3), (rest, other, w3_other)):
        step = silu(self_term[:, cols].astype(F32) + dot(summed, w[...]))
        for held, rows in ((slice(0, HALF), mine), (slice(HALF, HELD), far)):
            held_now[held, cols] = (latent[rows, :].astype(F32) + step[held, :]).astype(BF16)
    now[...] = held_now[pl.ds(0, HALF), :]
    put_edges(meta, held_now, w0, w0_other, cross, line)


def layer_project_kernel(
    last, meta, own, other, w0, w0_other, w1, w1_other, w2, w2_other,
    sent_own, sent_other, recv, self_own, *self_other,
):
    mine, rest = window(meta[0]), window(1 - meta[0])
    held, far = pl.ds(0, HALF), pl.ds(HALF, MARGIN)
    for cols, w in ((mine, w0), (rest, w0_other)):
        sent_own[:, cols] = dot(own[...], w[...]).astype(BF16)
        sent_other[:, cols] = dot(other[...], w[...]).astype(BF16)
    for cols, w in ((mine, w1), (rest, w1_other)):
        recv[held, cols] = dot(own[...], w[...]).astype(BF16)
        if not last:
            recv[far, cols] = dot(other[extra_rows(meta), :], w[...]).astype(BF16)
    for cols, w in ((mine, w2), (rest, w2_other)):
        self_own[held, cols] = dot(own[...], w[...]).astype(BF16)
        if last:
            self_other[0][:, cols] = dot(other[...], w[...]).astype(BF16)
        else:
            self_own[far, cols] = dot(other[extra_rows(meta), :], w[...]).astype(BF16)


def held_slots(meta, slots):
    tail = pltpu.roll(slots[:, 2 * HALF - LANES :], LANES - MARGIN, 1)
    far = jnp.where(meta[0] == 0, tail, slots[:, :LANES])
    return jnp.concatenate([slots[:, window(meta[0])], far], axis=1)


def layer_gather_kernel(meta, own, other, senders, out):
    base = meta[1] * (2 * HALF)
    nodes = out.shape[1]
    held = held_slots(meta, senders) - base
    for k in range(senders.shape[0]):
        local = held[k : k + 1, :]
        col = column(local - meta[0] * HALF)[:nodes]
        col_other = column(local - (1 - meta[0]) * HALF)[:nodes]
        value = dot(hot_columns(col, HALF), own[...])
        value = value + dot(hot_columns(col_other, HALF), other[...])
        out[k] = value.astype(BF16)


def layer_sum(meta, gathered, recv, cross, line, senders, live, halo, total):
    nodes = 2 * HALF
    base = meta[1] * nodes
    count, held = gathered.shape[0], gathered.shape[1]
    hots, flags = [], []
    slots, alive = held_slots(meta, senders) - base, held_slots(meta, live)
    for k in range(count):
        local = slots[k : k + 1, :]
        where = jnp.where(local < 0, local + MARGIN, local - nodes + MARGIN)
        where = jnp.where((local >= 0) & (local < nodes), -1, where)
        hots.append(hot_columns(column(where)[:held], 2 * MARGIN))
        flags.append(column(alive[k : k + 1, :])[:held].astype(BF16))
    odd = meta[1] % 2
    halo[pl.ds(pl.multiple_of(odd * MARGIN, MARGIN), MARGIN), :] = cross[...]
    halo[pl.ds(pl.multiple_of((1 - odd) * MARGIN, MARGIN), MARGIN), :] = line[...]
    outside = dot(jnp.concatenate(hots, axis=0), halo[...]).astype(BF16)
    step = 32
    for start in range(0, held, step):
        rows = pl.ds(start, step)
        side = recv[rows, :]
        running = None
        for k in range(count):
            row = k * held + start
            message = silu_message(outside[row : row + step, :] + gathered[k, rows, :] + side)
            flag = jnp.concatenate([flags[k][start : start + step, :]] * 4, axis=1)
            message = (message * flag).astype(F32)
            running = message if running is None else running + message
        total[rows, :] = running.astype(BF16)


def layer_update_kernel(
    meta, gathered, recv, line, cross, senders, live, now, now_other, self_term,
    w3, w3_other, w0, w0_other, out, edge_cross, edge_line, halo, total, held_now,
):
    mine, rest = window(meta[0]), window(1 - meta[0])
    layer_sum(meta, gathered, recv, cross, line, senders, live, halo, total)
    summed = total[...]
    for cols, w in ((mine, w3), (rest, w3_other)):
        step = silu(self_term[:, cols].astype(F32) + dot(summed, w[...]))
        far = now_other[extra_rows(meta), cols].astype(F32)
        held_now[pl.ds(0, HALF), cols] = (now[:, cols].astype(F32) + step[:HALF]).astype(BF16)
        held_now[pl.ds(HALF, MARGIN), cols] = (far + step[HALF:]).astype(BF16)
    out[...] = held_now[pl.ds(0, HALF), :]
    put_edges(meta, held_now, w0, w0_other, edge_cross, edge_line)


def layer_sum_kernel(meta, gathered, recv, cross, line, senders, live, out, halo):
    layer_sum(meta, gathered, recv, cross, line, senders, live, halo, out)


def last_update_kernel(
    meta, now_own, now_other, self_own, self_other, sum_own, sum_other, w3, w3_other,
    w0, w0_other, out, sent, now,
):
    mine, rest = window(meta[0]), window(1 - meta[0])
    for rows, latent, self_term, summed in (
        (mine, now_own, self_own, sum_own),
        (rest, now_other, self_other, sum_other),
    ):
        for cols, w in ((mine, w3), (rest, w3_other)):
            step = silu(self_term[:, cols] + dot(summed[...], w[...]))
            now[:, cols] = (latent[:, cols].astype(F32) + step).astype(BF16)
        out[rows, :] = now[:, mine]
        for cols, w in ((mine, w0), (rest, w0_other)):
            sent[rows, cols] = dot(now[...], w[...]).astype(BF16)


def decode_prepare_kernel(
    meta, own, other, w1, w1_other, w2, targets, mesh_now,
    before_own, before_near, before_skip, self_term, mesh_out, recv,
):
    mesh_out[...] = mesh_now[...]
    mine, rest = window(meta[0]), window(1 - meta[0])
    for start in range(0, own.shape[0], HALF):
        rows = pl.ds(start, HALF)
        a, b = own[rows, :], other[rows, :]
        recv[rows, mine] = (dot(a, w1[mine, :]) + dot(b, w1[rest, :])).astype(BF16)
        recv[rows, rest] = (dot(a, w1_other[mine, :]) + dot(b, w1_other[rest, :])).astype(BF16)
        self_term[rows, :] = (dot(a, w2[mine, :]) + dot(b, w2[rest, :])).astype(BF16)
    half = before_own.shape[0]
    gather_slots(targets[REACH, :, window(meta[0], half)], recv, before_own)
    gather_slots(targets[near_offset(meta)], recv, before_near)
    gather_slots(targets[skip_offset(meta)], recv, before_skip)


def decode_messages(meta, offset, columns, sent, before, senders, message):
    from_row = senders[offset, :, columns]
    for start in range(0, before.shape[0], HALF):
        rows = pl.ds(start, HALF)
        hot = hot_columns(column(from_row[:, start : start + HALF]), sent.shape[0])
        pre = dot(hot, sent[...]) + before[rows, :].astype(F32)
        message[rows, :] = silu_message(pre)


def decode_scatter(row, message, total, first, out):
    for start in range(0, out.shape[0], HALF):
        value = dot(hot_rows(row - (first + start), HALF), message[...])
        if total is not None:
            value = value + total[pl.ds(first + start, HALF), :].astype(F32)
        out[pl.ds(start, HALF), :] = value.astype(BF16)


def decode_own_kernel(meta, sent, before, senders, targets, live, out, message):
    columns = window(meta[0], before.shape[0])
    decode_messages(meta, REACH, columns, sent, before, senders, message)
    decode_scatter(live_targets(targets, live, REACH, columns), message, None, 0, out)


def decode_sum_kernel(
    offset_of, meta, sent, before, senders, targets, live, total, out, message
):
    offset = offset_of(meta)
    decode_messages(meta, offset, slice(None), sent, before, senders, message)
    decode_scatter(live_targets(targets, live, offset), message, total, 0, out)


def decode_rest_kernel(offset_of, meta, message, targets, live, total, out):
    row = live_targets(targets, live, offset_of(meta))
    decode_scatter(row, message, total, out.shape[0], out)


def final_kernel(first, meta, own, self_term, sum_own, sum_other, weights, *refs):
    out, w3 = refs[-1], weights.at[3]
    for start in range(0, out.shape[0], HALF):
        rows, from_rows = pl.ds(start, HALF), pl.ds(first + start, HALF)
        summed = sum_own[rows, :] + sum_other[rows, :]
        step = silu(self_term[from_rows, :].astype(F32) + dot(summed, w3[...]))
        out[rows, :] = (own[from_rows, :].astype(F32) + step).astype(BF16)


def body(
    grid_latent,
    mesh_latent,
    encode_weights,
    layer_weights,
    decode_weights,
    encode_senders,
    encode_targets,
    encode_live,
    mesh_senders,
    mesh_live,
    decode_senders,
    decode_targets,
    decode_live,
):
    meta = jnp.stack([lax.axis_index("feat"), lax.axis_index("band")]).astype(I32)
    grid_rows, cols = grid_latent.shape
    mesh_rows = mesh_latent.shape[0]
    full = 2 * cols
    senders, targets, live = (x.transpose(1, 0, 2) for x in (encode_senders, encode_targets, encode_live))
    slots = senders.shape[2]

    grid_other = swap(grid_latent)
    encode_other = swap(encode_weights)
    mesh_other = swap(mesh_latent)
    (begun,) = call(
        encode_begin_kernel,
        "encode_begin",
        (meta, grid_latent, encode_weights),
        [SMEM, whole(grid_latent), part(encode_weights, 0)],
        [shape(grid_rows, cols, dtype=F32)],
        2 * grid_rows * cols * cols,
    )
    grid_other, mesh_other = lax.optimization_barrier((grid_other, mesh_other))
    operands = (meta, grid_latent, grid_other, begun, encode_weights, encode_other, senders)
    sent, near_piece = call(
        encode_near_kernel,
        "encode_near",
        operands,
        [SMEM] + [whole(x) for x in operands[1:4]]
        + [part(encode_weights, 0), part(encode_other, 0), whole(senders)],
        [shape(grid_rows, full), shape(slots, full)],
        2 * full * (grid_rows * full + slots * grid_rows),
    )
    near_rows = exchange(near_piece, near_shift)
    layer_other = swap(after(layer_weights, near_piece))
    operands = (
        meta, mesh_latent, mesh_other, encode_weights, encode_other, sent, senders, targets
    )
    skip_piece, recv, before_near = call(
        encode_skip_kernel,
        "encode_skip",
        operands,
        [SMEM, whole(mesh_latent), whole(mesh_other)]
        + [part(encode_weights, 1), part(encode_other, 1)]
        + [whole(sent), whole(senders), whole(targets)],
        [shape(slots, full), shape(mesh_rows, full), shape(slots, full)],
        2 * full * (mesh_rows * full + slots * (grid_rows + mesh_rows)),
    )
    skip_rows = exchange(skip_piece, skip_shift)
    operands = (
        meta, near_rows, before_near, recv, sent, mesh_latent, mesh_other,
        encode_weights, encode_other, senders, targets, live,
    )
    total, before_skip, self_term = call(
        encode_near_sum_kernel,
        "encode_near_sum",
        operands,
        [SMEM] + [whole(x) for x in operands[1:7]]
        + [part(encode_weights, 2), part(encode_other, 2)]
        + [whole(x) for x in operands[9:]],
        [
            shape(mesh_rows, full, dtype=F32),
            shape(slots, full),
            shape(HELD, full),
        ],
        2 * full * mesh_rows * slots * 3,
        [pltpu.VMEM((slots, full), BF16), pltpu.VMEM((HALF, full), BF16)],
    )
    operands = (meta, skip_rows, before_skip, targets, live, total)
    sum_own, sum_other = call(
        encode_skip_sum_kernel,
        "encode_skip_sum",
        operands,
        [SMEM, whole(skip_rows), whole(before_skip), whole(targets), whole(live), whole(total)],
        [shape(HELD, full), shape(HELD, full)],
        2 * full * mesh_rows * slots,
        [pltpu.VMEM((slots, full), BF16), pltpu.VMEM((2, HALF, full), BF16)],
    )
    sum_arrived = swap(sum_other)
    decode_other = swap(after(decode_weights, sum_other))
    operands = (
        meta, mesh_latent, mesh_other, self_term, sum_own, sum_arrived,
        encode_weights, encode_other, layer_weights, layer_other,
    )
    now, cross_edge, line_edge = call(
        encode_update_kernel,
        "encode_update",
        operands,
        [SMEM] + [whole(x) for x in operands[1:6]]
        + [part(encode_weights, 3), part(encode_other, 3)]
        + [part(layer_weights, 0, 0), part(layer_other, 0, 0)],
        [shape(HALF, full), shape(MARGIN, full), shape(MARGIN, full)],
        2 * HALF * full * full,
        [pltpu.VMEM((HELD, full), BF16)],
    )

    senders_t, live_t = mesh_senders.T, mesh_live.T
    degree = senders_t.shape[0]
    for layer in range(LAYERS):
        last = layer == LAYERS - 1
        cross = exchange(cross_edge, cross_pairs)
        line = exchange(line_edge, line_pairs)
        now_other = swap(now)
        operands = (meta, now, now_other) + (layer_weights, layer_other) * 3
        results = call(
            functools.partial(layer_project_kernel, last),
            f"layer_project_{layer}",
            operands,
            [SMEM, whole(now), whole(now_other)]
            + [part(operands[3 + i], layer, i // 2) for i in range(6)],
            [shape(HALF, full)] * 2 + [shape(HALF if last else HELD, full)] * 2
            + [shape(HALF, full)] * last,
            2 * HALF * full * full * 4,
        )
        sent_own, sent_other, recv, self_own = results[:4]
        operands = (meta, sent_own, sent_other, senders_t)
        (gathered,) = call(
            layer_gather_kernel,
            f"layer_gather_{layer}",
            operands,
            [SMEM, whole(sent_own), whole(sent_other), whole(senders_t)],
            [shape(degree, HALF if last else HELD, full)],
            2 * degree * HALF * full * mesh_rows,
        )
        halo = (cross, line) if last else (line, cross)
        operands = (meta, gathered, recv) + halo + (senders_t, live_t)
        scratch = [pltpu.VMEM((2 * MARGIN, full), BF16)]
        sum_specs = (
            [SMEM] + [whole(x) for x in operands[1:5]]
            + [whole(senders_t), whole(live_t)]
        )
        if last:
            (summed,) = call(
                layer_sum_kernel,
                f"layer_sum_{layer}",
                operands,
                sum_specs,
                [shape(HALF, full)],
                2 * degree * HALF * full * 2 * MARGIN,
                scratch,
            )
            continue
        operands += (now, now_other, self_own) + (layer_weights, layer_other) * 2
        now, cross_edge, line_edge = call(
            layer_update_kernel,
            f"layer_update_{layer}",
            operands,
            sum_specs + [whole(now), whole(now_other), whole(self_own)]
            + [part(layer_weights, layer, 3), part(layer_other, layer, 3)]
            + [part(layer_weights, layer + 1, 0), part(layer_other, layer + 1, 0)],
            [shape(HALF, full), shape(MARGIN, full), shape(MARGIN, full)],
            2 * HALF * full * (degree * 2 * MARGIN + full),
            scratch + [pltpu.VMEM((HELD, full), BF16)] * 2,
        )
    operands = (
        meta, now, now_other, self_own, results[4], summed, swap(summed),
        layer_weights, layer_other, decode_weights, decode_other,
    )
    mesh_now, sent = call(
        last_update_kernel,
        "last_update",
        operands,
        [SMEM] + [whole(x) for x in operands[1:7]]
        + [part(layer_weights, LAYERS - 1, 3), part(layer_other, LAYERS - 1, 3)]
        + [part(decode_weights, 0), part(decode_other, 0)],
        [shape(mesh_rows, cols), shape(mesh_rows, full)],
        2 * mesh_rows * full * full * 2,
        [pltpu.VMEM((HALF, full), BF16)],
    )

    near_rows = exchange(sent, near_shift)
    skip_rows = exchange(sent, skip_shift)
    senders, targets, live = (x.transpose(1, 0, 2) for x in (decode_senders, decode_targets, decode_live))
    slots = senders.shape[2]
    operands = (
        meta, grid_latent, grid_other, decode_weights, decode_other, decode_weights, targets,
        mesh_now,
    )
    before_own, before_near, before_skip, self_term, mesh_now = call(
        decode_prepare_kernel,
        "decode_prepare",
        operands,
        [SMEM, whole(grid_latent), whole(grid_other)]
        + [part(decode_weights, 1), part(decode_other, 1), part(decode_weights, 2), whole(targets)]
        + [whole(mesh_now)],
        [
            shape(slots // 2, full),
            shape(slots, full),
            shape(slots, full),
            shape(grid_rows, cols),
            shape(mesh_rows, cols),
        ],
        2 * full * grid_rows * (full + 5 * slots // 2),
        [pltpu.VMEM((grid_rows, full), BF16)],
    )
    flops = 2 * full * slots * (grid_rows + mesh_rows)
    message_space = [pltpu.VMEM((slots, full), BF16)]
    operands = (meta, sent, before_own, senders, targets, live)
    (total,) = call(
        decode_own_kernel,
        "decode_own",
        operands,
        [SMEM] + [whole(x) for x in operands[1:]],
        [shape(grid_rows, full)],
        flops // 2,
        [pltpu.VMEM(before_own.shape, BF16)],
    )
    operands = (meta, skip_rows, before_skip, senders, targets, live, total)
    (total,) = call(
        functools.partial(decode_sum_kernel, skip_offset),
        "decode_skip",
        operands,
        [SMEM] + [whole(x) for x in operands[1:]],
        [shape(grid_rows, full)],
        flops,
        message_space,
    )
    half = grid_rows // 2
    operands = (meta, near_rows, before_near, senders, targets, live, total)
    head, message = call(
        functools.partial(decode_sum_kernel, near_offset),
        "decode_near",
        operands,
        [SMEM] + [whole(x) for x in operands[1:]],
        [shape(half, full), shape(slots, full)],
        flops,
    )
    operands = (meta, message, targets, live, total)
    (tail,) = call(
        functools.partial(decode_rest_kernel, near_offset),
        "decode_rest",
        operands,
        [SMEM] + [whole(x) for x in operands[1:]],
        [shape(half, full)],
        flops // 2,
    )
    grid_now = None
    for index, summed in enumerate((head, tail)):
        block = pl.BlockSpec((half, cols), lambda i, index=index: (index, 0))
        operands = (meta, grid_latent, self_term, summed, swap(summed), decode_weights)
        specs = [SMEM] + [whole(x) for x in operands[1:]]
        aliases = {}
        if index:
            operands, specs, aliases = operands + (grid_now,), specs + [pl.BlockSpec(memory_space=pl.ANY)], {6: 0}
        grid_now = pl.pallas_call(
            functools.partial(final_kernel, index * half),
            name=f"final_update_{index}",
            grid=(1,),
            in_specs=specs,
            out_specs=block,
            out_shape=shape(grid_rows, cols),
            input_output_aliases=aliases,
            compiler_params=pltpu.CompilerParams(vmem_limit_bytes=VMEM_LIMIT),
        )(*operands)
    return mesh_now, grid_now


def solution(mesh):
    placed = (
        P("band", "feat"),
        P("band", "feat"),
        P(None, None, "feat"),
        P(None, None, None, "feat"),
        P(None, None, "feat"),
        P("band", None, None),
        P("band", None, None),
        P("band", None, None),
        P("band", None),
        P("band", None),
        P("band", None, None),
        P("band", None, None),
        P("band", None, None),
    )
    return jax.shard_map(
        body,
        mesh=mesh,
        in_specs=placed,
        out_specs=(P("band", "feat"), P("band", "feat")),
        check_vma=False,
    )
```

```python
import functools

import jax
import jax.numpy as jnp
from jax import lax
from jax.experimental import pallas as pl
from jax.experimental.pallas import tpu as pltpu
from jax.sharding import PartitionSpec as P

REACH = 2
LAYERS = 2
MARGIN = 64
HALF = 256
HELD = HALF + MARGIN
LANES = 128
F32 = jnp.float32
BF16 = jnp.bfloat16
I32 = jnp.int32
VMEM_LIMIT = 36 * 1024 * 1024


def swap(value):
    return lax.ppermute(value, "feat", [(0, 1), (1, 0)])


def flat(partners):
    return [(2 * s + c, 2 * t + e) for (s, c), (t, e) in partners.items()]


def shift(steps, up, count):
    partners = {}
    for s in range(count):
        partners[s, up] = (s + steps, up) if s + steps < count else (s, 1 - up)
        partners[s, 1 - up] = (s - steps, 1 - up) if s >= steps else (s, up)
    return flat(partners)


near_shift = functools.partial(shift, 1, 0)
skip_shift = functools.partial(shift, 2, 0)


def cross_pairs(count):
    partners = {}
    for s in range(count):
        other = s + 1 if s % 2 else s - 1
        for c in range(2):
            partners[s, c] = (other, c) if 0 <= other < count else (s, 1 - c)
    return flat(partners)


def line_pairs(count):
    return flat({(s, c): (s ^ 1, c) for s in range(count) for c in range(2)})


def exchange(value, pairs):
    return lax.ppermute(value, ("band", "feat"), pairs(lax.axis_size("band")))


def after(value, other):
    return lax.optimization_barrier((value, other))[0]


def silu(v):
    half = 0.5 * v
    return half + half * jnp.tanh(half)


def silu_message(v):
    half = v.astype(BF16) * BF16(0.5)
    return half + half * jnp.tanh(half)


def dot(a, b):
    return jnp.dot(a, b, preferred_element_type=F32)


def window(index, size=HALF):
    return pl.ds(pl.multiple_of(index * size, size), size)


def extra_rows(meta):
    return pl.ds(pl.multiple_of((1 - meta[0]) * (HALF - MARGIN), MARGIN), MARGIN)


def margin_rows(meta):
    return pl.ds(pl.multiple_of((1 - meta[0]) * (2 * HALF - MARGIN), MARGIN), MARGIN)


def near_offset(meta):
    return 3 - 2 * meta[0]


def skip_offset(meta):
    return 4 - 4 * meta[0]


def column(row):
    parts = [
        jnp.broadcast_to(row[:, start : start + LANES], (LANES, LANES)).T
        for start in range(0, row.shape[1], LANES)
    ]
    return parts[0] if len(parts) == 1 else jnp.concatenate(parts, axis=0)


def hot_columns(col, width):
    col = col.astype(jnp.int16)
    ids = lax.broadcasted_iota(I32, col.shape, 1).astype(jnp.int16)
    one, zero = BF16(1), BF16(0)
    parts = [
        jnp.where(col == ids + jnp.int16(start), one, zero) for start in range(0, width, LANES)
    ]
    return parts[0] if len(parts) == 1 else jnp.concatenate(parts, axis=1)


def hot_rows(row, height):
    ids = lax.broadcasted_iota(I32, (height, row.shape[1]), 0)
    return jnp.where(row == ids, 1.0, 0.0).astype(BF16)


class Part:
    def __init__(self, spec, index):
        self.spec, self.index = spec, index


def call(kernel, name, operands, specs, outs, flops, scratch=()):
    def viewed(*refs):
        refs = [
            ref.at[specs[i].index] if i < len(specs) and isinstance(specs[i], Part) else ref
            for i, ref in enumerate(refs)
        ]
        kernel(*refs)

    size = sum(x.size * x.dtype.itemsize for x in outs)
    return pl.pallas_call(
        viewed,
        name=name,
        grid=(1,),
        in_specs=[spec.spec if isinstance(spec, Part) else spec for spec in specs],
        out_specs=[whole(x) for x in outs],
        out_shape=list(outs),
        scratch_shapes=list(scratch),
        compiler_params=pltpu.CompilerParams(vmem_limit_bytes=VMEM_LIMIT),
        cost_estimate=pl.CostEstimate(
            flops=flops // 64, bytes_accessed=size // 64, transcendentals=0
        ),
    )(*operands)


def whole(x):
    return pl.BlockSpec(x.shape, lambda i, n=len(x.shape): (0,) * n)


def part(x, *index):
    return Part(whole(x), index)


SMEM = pl.BlockSpec(memory_space=pltpu.SMEM)


def shape(*dims, dtype=BF16):
    return jax.ShapeDtypeStruct(dims, dtype)


def encode_begin_kernel(meta, own, w_own, out):
    for start in range(0, own.shape[0], HALF):
        rows = pl.ds(start, HALF)
        out[rows, :] = dot(own[rows, :], w_own[window(meta[0]), :])


def gather_slots(senders_row, sent, out):
    for start in range(0, senders_row.shape[1], HALF):
        col = column(senders_row[:, start : start + HALF])
        out[pl.ds(start, HALF), :] = dot(hot_columns(col, sent.shape[0]), sent[...]).astype(BF16)


def encode_skip_kernel(meta, own, other, begun, w_own, w_other, senders, sent, piece):
    mine, rest = window(meta[0]), window(1 - meta[0])
    for start in range(0, own.shape[0], HALF):
        rows = pl.ds(start, HALF)
        a, b = own[rows, :], other[rows, :]
        sent[rows, mine] = (begun[rows, :] + dot(b, w_own[rest, :])).astype(BF16)
        sent[rows, rest] = (dot(a, w_other[mine, :]) + dot(b, w_other[rest, :])).astype(BF16)
    gather_slots(senders[skip_offset(meta)], sent, piece)


def live_targets(targets, live, offset, columns=slice(None)):
    return jnp.where(live[offset, :, columns] > 0, targets[offset, :, columns], -1)


def encode_near_kernel(
    meta, own, other, w1, w1_other, sent, senders, targets, piece, recv, before
):
    gather_slots(senders[near_offset(meta)], sent, piece)
    mine, rest = window(meta[0]), window(1 - meta[0])
    for start in range(0, own.shape[0], HALF):
        rows = pl.ds(start, HALF)
        a, b = own[rows, :], other[rows, :]
        recv[rows, mine] = (dot(a, w1[mine, :]) + dot(b, w1[rest, :])).astype(BF16)
        recv[rows, rest] = (dot(a, w1_other[mine, :]) + dot(b, w1_other[rest, :])).astype(BF16)
    gather_slots(targets[skip_offset(meta)], recv, before)


def encode_skip_sum_kernel(
    meta, rows, before, recv, sent, own, other, w2, w2_other, senders, targets, live,
    total, before_near, self_term, message, own_message,
):
    mine, rest = window(meta[0]), window(1 - meta[0])
    nodes = recv.shape[0]
    from_rows = hot_columns(column(senders[REACH, :, mine]), sent.shape[0])
    to_rows = hot_columns(column(targets[REACH, :, mine]), nodes)
    own_message[...] = silu_message(dot(from_rows, sent[...]) + dot(to_rows, recv[...]))
    message[...] = silu_message(rows[...] + before[...])
    row = live_targets(targets, live, skip_offset(meta))
    own_row = live_targets(targets, live, REACH, mine)
    for start in range(0, nodes, HALF):
        value = dot(hot_rows(row - start, HALF), message[...])
        value = value + dot(hot_rows(own_row - start, HALF), own_message[...])
        total[pl.ds(start, HALF), :] = value
    gather_slots(targets[near_offset(meta)], recv, before_near)
    far = margin_rows(meta)
    for held, rows in ((pl.ds(0, HALF), mine), (pl.ds(HALF, MARGIN), far)):
        a, b = own[rows, :], other[rows, :]
        self_term[held, mine] = (dot(a, w2[mine, :]) + dot(b, w2[rest, :])).astype(BF16)
        self_term[held, rest] = (dot(a, w2_other[mine, :]) + dot(b, w2_other[rest, :])).astype(BF16)


def encode_near_sum_kernel(
    meta, rows, before, targets, live, total, out_own, out_other, message, halves
):
    message[...] = silu_message(rows[...] + before[...])
    row = live_targets(targets, live, near_offset(meta))
    for index, half in enumerate((1 - meta[0], meta[0])):
        value = dot(hot_rows(row - half * HALF, HALF), message[...]) + total[window(half), :]
        halves[index] = value.astype(BF16)
    held, far = pl.ds(0, HALF), pl.ds(HALF, MARGIN)
    out_own[held, :] = halves[1]
    out_own[far, :] = halves[0, extra_rows(meta), :]
    out_other[held, :] = halves[0]
    start = pl.multiple_of(meta[0] * (HALF - MARGIN), MARGIN)
    out_other[far, :] = halves[1, pl.ds(start, MARGIN), :]


def put_edges(meta, now, w0, w0_other, cross, line):
    mine, rest = window(meta[0]), window(1 - meta[0])
    odd = meta[1] % 2
    head, tail = HALF * meta[0], HALF - MARGIN * meta[0]
    for edge, start in (
        (cross, (1 - odd) * head + odd * tail),
        (line, (1 - odd) * tail + odd * head),
    ):
        rows = now[pl.ds(pl.multiple_of(start, MARGIN), MARGIN), :]
        edge[:, mine] = dot(rows, w0[...]).astype(BF16)
        edge[:, rest] = dot(rows, w0_other[...]).astype(BF16)


def encode_update_kernel(
    meta, own, other, self_term, sum_own, sum_other, w3, w3_other, w0, w0_other,
    now, cross, line, held_now,
):
    mine, rest = window(meta[0]), window(1 - meta[0])
    summed = sum_own[...] + sum_other[...]
    far = margin_rows(meta)
    for cols, latent, w in ((mine, own, w3), (rest, other, w3_other)):
        step = silu(self_term[:, cols].astype(F32) + dot(summed, w[...]))
        for held, rows in ((slice(0, HALF), mine), (slice(HALF, HELD), far)):
            held_now[held, cols] = (latent[rows, :].astype(F32) + step[held, :]).astype(BF16)
    now[...] = held_now[pl.ds(0, HALF), :]
    put_edges(meta, held_now, w0, w0_other, cross, line)


def layer_project_kernel(
    last, meta, own, other, w0, w0_other, w1, w1_other, w2, w2_other,
    sent_own, sent_other, recv, self_own, *self_other,
):
    mine, rest = window(meta[0]), window(1 - meta[0])
    held, far = pl.ds(0, HALF), pl.ds(HALF, MARGIN)
    for cols, w in ((mine, w0), (rest, w0_other)):
        sent_own[:, cols] = dot(own[...], w[...]).astype(BF16)
        sent_other[:, cols] = dot(other[...], w[...]).astype(BF16)
    for cols, w in ((mine, w1), (rest, w1_other)):
        recv[held, cols] = dot(own[...], w[...]).astype(BF16)
        if not last:
            recv[far, cols] = dot(other[extra_rows(meta), :], w[...]).astype(BF16)
    for cols, w in ((mine, w2), (rest, w2_other)):
        self_own[held, cols] = dot(own[...], w[...]).astype(BF16)
        if last:
            self_other[0][:, cols] = dot(other[...], w[...]).astype(BF16)
        else:
            self_own[far, cols] = dot(other[extra_rows(meta), :], w[...]).astype(BF16)


def held_slots(meta, slots):
    tail = pltpu.roll(slots[:, 2 * HALF - LANES :], LANES - MARGIN, 1)
    far = jnp.where(meta[0] == 0, tail, slots[:, :LANES])
    return jnp.concatenate([slots[:, window(meta[0])], far], axis=1)


def layer_gather_kernel(meta, own, other, senders, out):
    base = meta[1] * (2 * HALF)
    nodes = out.shape[1]
    held = held_slots(meta, senders) - base
    for k in range(senders.shape[0]):
        local = held[k : k + 1, :]
        col = column(local - meta[0] * HALF)[:nodes]
        col_other = column(local - (1 - meta[0]) * HALF)[:nodes]
        value = dot(hot_columns(col, HALF), own[...])
        value = value + dot(hot_columns(col_other, HALF), other[...])
        out[k] = value.astype(BF16)


def layer_sum(meta, gathered, recv, cross, line, senders, live, halo, total):
    nodes = 2 * HALF
    base = meta[1] * nodes
    count, held = gathered.shape[0], gathered.shape[1]
    hots, flags = [], []
    slots, alive = held_slots(meta, senders) - base, held_slots(meta, live)
    for k in range(count):
        local = slots[k : k + 1, :]
        where = jnp.where(local < 0, local + MARGIN, local - nodes + MARGIN)
        where = jnp.where((local >= 0) & (local < nodes), -1, where)
        hots.append(hot_columns(column(where)[:held], 2 * MARGIN))
        flags.append(column(alive[k : k + 1, :])[:held].astype(BF16))
    odd = meta[1] % 2
    halo[pl.ds(pl.multiple_of(odd * MARGIN, MARGIN), MARGIN), :] = cross[...]
    halo[pl.ds(pl.multiple_of((1 - odd) * MARGIN, MARGIN), MARGIN), :] = line[...]
    outside = dot(jnp.concatenate(hots, axis=0), halo[...]).astype(BF16)
    step = 32
    for start in range(0, held, step):
        rows = pl.ds(start, step)
        side = recv[rows, :]
        running = None
        for k in range(count):
            row = k * held + start
            message = silu_message(outside[row : row + step, :] + gathered[k, rows, :] + side)
            flag = jnp.concatenate([flags[k][start : start + step, :]] * 4, axis=1)
            message = (message * flag).astype(F32)
            running = message if running is None else running + message
        total[rows, :] = running.astype(BF16)


def layer_update_kernel(
    meta, gathered, recv, line, cross, senders, live, now, now_other, self_term,
    w3, w3_other, w0, w0_other, out, edge_cross, edge_line, halo, total, held_now,
):
    mine, rest = window(meta[0]), window(1 - meta[0])
    layer_sum(meta, gathered, recv, cross, line, senders, live, halo, total)
    summed = total[...]
    for cols, w in ((mine, w3), (rest, w3_other)):
        step = silu(self_term[:, cols].astype(F32) + dot(summed, w[...]))
        far = now_other[extra_rows(meta), cols].astype(F32)
        held_now[pl.ds(0, HALF), cols] = (now[:, cols].astype(F32) + step[:HALF]).astype(BF16)
        held_now[pl.ds(HALF, MARGIN), cols] = (far + step[HALF:]).astype(BF16)
    out[...] = held_now[pl.ds(0, HALF), :]
    put_edges(meta, held_now, w0, w0_other, edge_cross, edge_line)


def layer_sum_kernel(meta, gathered, recv, cross, line, senders, live, out, halo):
    layer_sum(meta, gathered, recv, cross, line, senders, live, halo, out)


def last_update_kernel(
    meta, now_own, now_other, self_own, self_other, sum_own, sum_other, w3, w3_other,
    w0, w0_other, out, sent, now,
):
    mine, rest = window(meta[0]), window(1 - meta[0])
    for rows, latent, self_term, summed in (
        (mine, now_own, self_own, sum_own),
        (rest, now_other, self_other, sum_other),
    ):
        for cols, w in ((mine, w3), (rest, w3_other)):
            step = silu(self_term[:, cols] + dot(summed[...], w[...]))
            now[:, cols] = (latent[:, cols].astype(F32) + step).astype(BF16)
        out[rows, :] = now[:, mine]
        for cols, w in ((mine, w0), (rest, w0_other)):
            sent[rows, cols] = dot(now[...], w[...]).astype(BF16)


def decode_prepare_kernel(
    meta, own, other, w1, w1_other, w2, targets, mesh_now,
    before_own, before_near, before_skip, self_term, mesh_out, recv,
):
    mesh_out[...] = mesh_now[...]
    mine, rest = window(meta[0]), window(1 - meta[0])
    for start in range(0, own.shape[0], HALF):
        rows = pl.ds(start, HALF)
        a, b = own[rows, :], other[rows, :]
        recv[rows, mine] = (dot(a, w1[mine, :]) + dot(b, w1[rest, :])).astype(BF16)
        recv[rows, rest] = (dot(a, w1_other[mine, :]) + dot(b, w1_other[rest, :])).astype(BF16)
        self_term[rows, :] = (dot(a, w2[mine, :]) + dot(b, w2[rest, :])).astype(BF16)
    half = before_own.shape[0]
    gather_slots(targets[REACH, :, window(meta[0], half)], recv, before_own)
    gather_slots(targets[near_offset(meta)], recv, before_near)
    gather_slots(targets[skip_offset(meta)], recv, before_skip)


def decode_messages(meta, offset, columns, sent, before, senders, message):
    from_row = senders[offset, :, columns]
    for start in range(0, before.shape[0], HALF):
        rows = pl.ds(start, HALF)
        hot = hot_columns(column(from_row[:, start : start + HALF]), sent.shape[0])
        pre = dot(hot, sent[...]) + before[rows, :].astype(F32)
        message[rows, :] = silu_message(pre)


def decode_scatter(row, message, total, first, out):
    for start in range(0, out.shape[0], HALF):
        value = dot(hot_rows(row - (first + start), HALF), message[...])
        if total is not None:
            value = value + total[pl.ds(first + start, HALF), :].astype(F32)
        out[pl.ds(start, HALF), :] = value.astype(BF16)


def decode_own_kernel(meta, sent, before, senders, targets, live, out, message):
    columns = window(meta[0], before.shape[0])
    decode_messages(meta, REACH, columns, sent, before, senders, message)
    decode_scatter(live_targets(targets, live, REACH, columns), message, None, 0, out)


def decode_sum_kernel(
    offset_of, meta, sent, before, senders, targets, live, total, out, message
):
    offset = offset_of(meta)
    decode_messages(meta, offset, slice(None), sent, before, senders, message)
    decode_scatter(live_targets(targets, live, offset), message, total, 0, out)


def decode_rest_kernel(offset_of, meta, message, targets, live, total, out):
    row = live_targets(targets, live, offset_of(meta))
    decode_scatter(row, message, total, out.shape[0], out)


def final_kernel(first, meta, own, self_term, sum_own, sum_other, weights, *refs):
    out, w3 = refs[-1], weights.at[3]
    for start in range(0, out.shape[0], HALF):
        rows, from_rows = pl.ds(start, HALF), pl.ds(first + start, HALF)
        summed = sum_own[rows, :] + sum_other[rows, :]
        step = silu(self_term[from_rows, :].astype(F32) + dot(summed, w3[...]))
        out[rows, :] = (own[from_rows, :].astype(F32) + step).astype(BF16)


def body(
    grid_latent,
    mesh_latent,
    encode_weights,
    layer_weights,
    decode_weights,
    encode_senders,
    encode_targets,
    encode_live,
    mesh_senders,
    mesh_live,
    decode_senders,
    decode_targets,
    decode_live,
):
    meta = jnp.stack([lax.axis_index("feat"), lax.axis_index("band")]).astype(I32)
    grid_rows, cols = grid_latent.shape
    mesh_rows = mesh_latent.shape[0]
    full = 2 * cols
    senders, targets, live = (x.transpose(1, 0, 2) for x in (encode_senders, encode_targets, encode_live))
    slots = senders.shape[2]

    grid_other = swap(grid_latent)
    encode_other = swap(encode_weights)
    mesh_other = swap(mesh_latent)
    (begun,) = call(
        encode_begin_kernel,
        "encode_begin",
        (meta, grid_latent, encode_weights),
        [SMEM, whole(grid_latent), part(encode_weights, 0)],
        [shape(grid_rows, cols, dtype=F32)],
        2 * grid_rows * cols * cols,
    )
    grid_other, mesh_other = lax.optimization_barrier((grid_other, mesh_other))
    operands = (meta, grid_latent, grid_other, begun, encode_weights, encode_other, senders)
    sent, skip_piece = call(
        encode_skip_kernel,
        "encode_skip",
        operands,
        [SMEM] + [whole(x) for x in operands[1:4]]
        + [part(encode_weights, 0), part(encode_other, 0), whole(senders)],
        [shape(grid_rows, full), shape(slots, full)],
        2 * full * (grid_rows * full + slots * grid_rows),
    )
    skip_rows = exchange(skip_piece, skip_shift)
    layer_other = swap(after(layer_weights, skip_piece))
    operands = (
        meta, mesh_latent, mesh_other, encode_weights, encode_other, sent, senders, targets
    )
    near_piece, recv, before_skip = call(
        encode_near_kernel,
        "encode_near",
        operands,
        [SMEM, whole(mesh_latent), whole(mesh_other)]
        + [part(encode_weights, 1), part(encode_other, 1)]
        + [whole(sent), whole(senders), whole(targets)],
        [shape(slots, full), shape(mesh_rows, full), shape(slots, full)],
        2 * full * (mesh_rows * full + slots * (grid_rows + mesh_rows)),
    )
    near_rows = exchange(near_piece, near_shift)
    operands = (
        meta, skip_rows, before_skip, recv, sent, mesh_latent, mesh_other,
        encode_weights, encode_other, senders, targets, live,
    )
    total, before_near, self_term = call(
        encode_skip_sum_kernel,
        "encode_skip_sum",
        operands,
        [SMEM] + [whole(x) for x in operands[1:7]]
        + [part(encode_weights, 2), part(encode_other, 2)]
        + [whole(x) for x in operands[9:]],
        [
            shape(mesh_rows, full, dtype=F32),
            shape(slots, full),
            shape(HELD, full),
        ],
        2 * full * mesh_rows * slots * 3,
        [pltpu.VMEM((slots, full), BF16), pltpu.VMEM((HALF, full), BF16)],
    )
    operands = (meta, near_rows, before_near, targets, live, total)
    sum_own, sum_other = call(
        encode_near_sum_kernel,
        "encode_near_sum",
        operands,
        [SMEM, whole(near_rows), whole(before_near), whole(targets), whole(live), whole(total)],
        [shape(HELD, full), shape(HELD, full)],
        2 * full * mesh_rows * slots,
        [pltpu.VMEM((slots, full), BF16), pltpu.VMEM((2, HALF, full), BF16)],
    )
    sum_arrived = swap(sum_other)
    decode_other = swap(after(decode_weights, sum_other))
    operands = (
        meta, mesh_latent, mesh_other, self_term, sum_own, sum_arrived,
        encode_weights, encode_other, layer_weights, layer_other,
    )
    now, cross_edge, line_edge = call(
        encode_update_kernel,
        "encode_update",
        operands,
        [SMEM] + [whole(x) for x in operands[1:6]]
        + [part(encode_weights, 3), part(encode_other, 3)]
        + [part(layer_weights, 0, 0), part(layer_other, 0, 0)],
        [shape(HALF, full), shape(MARGIN, full), shape(MARGIN, full)],
        2 * HALF * full * full,
        [pltpu.VMEM((HELD, full), BF16)],
    )

    senders_t, live_t = mesh_senders.T, mesh_live.T
    degree = senders_t.shape[0]
    for layer in range(LAYERS):
        last = layer == LAYERS - 1
        cross = exchange(cross_edge, cross_pairs)
        line = exchange(line_edge, line_pairs)
        now_other = swap(now)
        operands = (meta, now, now_other) + (layer_weights, layer_other) * 3
        results = call(
            functools.partial(layer_project_kernel, last),
            f"layer_project_{layer}",
            operands,
            [SMEM, whole(now), whole(now_other)]
            + [part(operands[3 + i], layer, i // 2) for i in range(6)],
            [shape(HALF, full)] * 2 + [shape(HALF if last else HELD, full)] * 2
            + [shape(HALF, full)] * last,
            2 * HALF * full * full * 4,
        )
        sent_own, sent_other, recv, self_own = results[:4]
        operands = (meta, sent_own, sent_other, senders_t)
        (gathered,) = call(
            layer_gather_kernel,
            f"layer_gather_{layer}",
            operands,
            [SMEM, whole(sent_own), whole(sent_other), whole(senders_t)],
            [shape(degree, HALF if last else HELD, full)],
            2 * degree * HALF * full * mesh_rows,
        )
        halo = (cross, line) if last else (line, cross)
        operands = (meta, gathered, recv) + halo + (senders_t, live_t)
        scratch = [pltpu.VMEM((2 * MARGIN, full), BF16)]
        sum_specs = (
            [SMEM] + [whole(x) for x in operands[1:5]]
            + [whole(senders_t), whole(live_t)]
        )
        if last:
            (summed,) = call(
                layer_sum_kernel,
                f"layer_sum_{layer}",
                operands,
                sum_specs,
                [shape(HALF, full)],
                2 * degree * HALF * full * 2 * MARGIN,
                scratch,
            )
            continue
        operands += (now, now_other, self_own) + (layer_weights, layer_other) * 2
        now, cross_edge, line_edge = call(
            layer_update_kernel,
            f"layer_update_{layer}",
            operands,
            sum_specs + [whole(now), whole(now_other), whole(self_own)]
            + [part(layer_weights, layer, 3), part(layer_other, layer, 3)]
            + [part(layer_weights, layer + 1, 0), part(layer_other, layer + 1, 0)],
            [shape(HALF, full), shape(MARGIN, full), shape(MARGIN, full)],
            2 * HALF * full * (degree * 2 * MARGIN + full),
            scratch + [pltpu.VMEM((HELD, full), BF16)] * 2,
        )
    operands = (
        meta, now, now_other, self_own, results[4], summed, swap(summed),
        layer_weights, layer_other, decode_weights, decode_other,
    )
    mesh_now, sent = call(
        last_update_kernel,
        "last_update",
        operands,
        [SMEM] + [whole(x) for x in operands[1:7]]
        + [part(layer_weights, LAYERS - 1, 3), part(layer_other, LAYERS - 1, 3)]
        + [part(decode_weights, 0), part(decode_other, 0)],
        [shape(mesh_rows, cols), shape(mesh_rows, full)],
        2 * mesh_rows * full * full * 2,
        [pltpu.VMEM((HALF, full), BF16)],
    )

    near_rows = exchange(sent, near_shift)
    skip_rows = exchange(sent, skip_shift)
    senders, targets, live = (x.transpose(1, 0, 2) for x in (decode_senders, decode_targets, decode_live))
    slots = senders.shape[2]
    operands = (
        meta, grid_latent, grid_other, decode_weights, decode_other, decode_weights, targets,
        mesh_now,
    )
    before_own, before_near, before_skip, self_term, mesh_now = call(
        decode_prepare_kernel,
        "decode_prepare",
        operands,
        [SMEM, whole(grid_latent), whole(grid_other)]
        + [part(decode_weights, 1), part(decode_other, 1), part(decode_weights, 2), whole(targets)]
        + [whole(mesh_now)],
        [
            shape(slots // 2, full),
            shape(slots, full),
            shape(slots, full),
            shape(grid_rows, cols),
            shape(mesh_rows, cols),
        ],
        2 * full * grid_rows * (full + 5 * slots // 2),
        [pltpu.VMEM((grid_rows, full), BF16)],
    )
    flops = 2 * full * slots * (grid_rows + mesh_rows)
    message_space = [pltpu.VMEM((slots, full), BF16)]
    operands = (meta, sent, before_own, senders, targets, live)
    (total,) = call(
        decode_own_kernel,
        "decode_own",
        operands,
        [SMEM] + [whole(x) for x in operands[1:]],
        [shape(grid_rows, full)],
        flops // 2,
        [pltpu.VMEM(before_own.shape, BF16)],
    )
    operands = (meta, skip_rows, before_skip, senders, targets, live, total)
    (total,) = call(
        functools.partial(decode_sum_kernel, skip_offset),
        "decode_skip",
        operands,
        [SMEM] + [whole(x) for x in operands[1:]],
        [shape(grid_rows, full)],
        flops,
        message_space,
    )
    half = grid_rows // 2
    operands = (meta, near_rows, before_near, senders, targets, live, total)
    head, message = call(
        functools.partial(decode_sum_kernel, near_offset),
        "decode_near",
        operands,
        [SMEM] + [whole(x) for x in operands[1:]],
        [shape(half, full), shape(slots, full)],
        flops,
    )
    operands = (meta, message, targets, live, total)
    (tail,) = call(
        functools.partial(decode_rest_kernel, near_offset),
        "decode_rest",
        operands,
        [SMEM] + [whole(x) for x in operands[1:]],
        [shape(half, full)],
        flops // 2,
    )
    grid_now = None
    for index, summed in enumerate((head, tail)):
        block = pl.BlockSpec((half, cols), lambda i, index=index: (index, 0))
        operands = (meta, grid_latent, self_term, summed, swap(summed), decode_weights)
        specs = [SMEM] + [whole(x) for x in operands[1:]]
        aliases = {}
        if index:
            operands, specs, aliases = operands + (grid_now,), specs + [pl.BlockSpec(memory_space=pl.ANY)], {6: 0}
        grid_now = pl.pallas_call(
            functools.partial(final_kernel, index * half),
            name=f"final_update_{index}",
            grid=(1,),
            in_specs=specs,
            out_specs=block,
            out_shape=shape(grid_rows, cols),
            input_output_aliases=aliases,
            compiler_params=pltpu.CompilerParams(vmem_limit_bytes=VMEM_LIMIT),
        )(*operands)
    return mesh_now, grid_now


def solution(mesh):
    placed = (
        P("band", "feat"),
        P("band", "feat"),
        P(None, None, "feat"),
        P(None, None, None, "feat"),
        P(None, None, "feat"),
        P("band", None, None),
        P("band", None, None),
        P("band", None, None),
        P("band", None),
        P("band", None),
        P("band", None, None),
        P("band", None, None),
        P("band", None, None),
    )
    return jax.shard_map(
        body,
        mesh=mesh,
        in_specs=placed,
        out_specs=(P("band", "feat"), P("band", "feat")),
        check_vma=False,
    )
```

```python
import functools

import jax
import jax.numpy as jnp
from jax import lax
from jax.experimental import pallas as pl
from jax.experimental.pallas import tpu as pltpu
from jax.sharding import PartitionSpec as P

REACH = 2
LAYERS = 2
MARGIN = 64
HALF = 256
HELD = HALF + MARGIN
LANES = 128
F32 = jnp.float32
BF16 = jnp.bfloat16
I32 = jnp.int32
VMEM_LIMIT = 36 * 1024 * 1024


def swap(value):
    return lax.ppermute(value, "feat", [(0, 1), (1, 0)])


def flat(partners):
    return [(2 * s + c, 2 * t + e) for (s, c), (t, e) in partners.items()]


def shift(steps, up, count):
    partners = {}
    for s in range(count):
        partners[s, up] = (s + steps, up) if s + steps < count else (s, 1 - up)
        partners[s, 1 - up] = (s - steps, 1 - up) if s >= steps else (s, up)
    return flat(partners)


near_shift = functools.partial(shift, 1, 0)
skip_shift = functools.partial(shift, 2, 0)


def cross_pairs(count):
    partners = {}
    for s in range(count):
        other = s + 1 if s % 2 else s - 1
        for c in range(2):
            partners[s, c] = (other, c) if 0 <= other < count else (s, 1 - c)
    return flat(partners)


def line_pairs(count):
    return flat({(s, c): (s ^ 1, c) for s in range(count) for c in range(2)})


def exchange(value, pairs):
    return lax.ppermute(value, ("band", "feat"), pairs(lax.axis_size("band")))


def after(value, other):
    return lax.optimization_barrier((value, other))[0]


def silu(v):
    half = 0.5 * v
    return half + half * jnp.tanh(half)


def silu_message(v):
    half = v.astype(BF16) * BF16(0.5)
    return half + half * jnp.tanh(half)


def dot(a, b):
    return jnp.dot(a, b, preferred_element_type=F32)


def window(index, size=HALF):
    return pl.ds(pl.multiple_of(index * size, size), size)


def extra_rows(meta):
    return pl.ds(pl.multiple_of((1 - meta[0]) * (HALF - MARGIN), MARGIN), MARGIN)


def margin_rows(meta):
    return pl.ds(pl.multiple_of((1 - meta[0]) * (2 * HALF - MARGIN), MARGIN), MARGIN)


def near_offset(meta):
    return 3 - 2 * meta[0]


def skip_offset(meta):
    return 4 - 4 * meta[0]


def column(row):
    parts = [
        jnp.broadcast_to(row[:, start : start + LANES], (LANES, LANES)).T
        for start in range(0, row.shape[1], LANES)
    ]
    return parts[0] if len(parts) == 1 else jnp.concatenate(parts, axis=0)


def hot_columns(col, width):
    col = col.astype(jnp.int16)
    ids = lax.broadcasted_iota(I32, col.shape, 1).astype(jnp.int16)
    one, zero = BF16(1), BF16(0)
    parts = [
        jnp.where(col == ids + jnp.int16(start), one, zero) for start in range(0, width, LANES)
    ]
    return parts[0] if len(parts) == 1 else jnp.concatenate(parts, axis=1)


def hot_rows(row, height):
    ids = lax.broadcasted_iota(I32, (height, row.shape[1]), 0)
    return jnp.where(row == ids, 1.0, 0.0).astype(BF16)


class Part:
    def __init__(self, spec, index):
        self.spec, self.index = spec, index


def call(kernel, name, operands, specs, outs, flops, scratch=()):
    def viewed(*refs):
        refs = [
            ref.at[specs[i].index] if i < len(specs) and isinstance(specs[i], Part) else ref
            for i, ref in enumerate(refs)
        ]
        kernel(*refs)

    size = sum(x.size * x.dtype.itemsize for x in outs)
    return pl.pallas_call(
        viewed,
        name=name,
        grid=(1,),
        in_specs=[spec.spec if isinstance(spec, Part) else spec for spec in specs],
        out_specs=[whole(x) for x in outs],
        out_shape=list(outs),
        scratch_shapes=list(scratch),
        compiler_params=pltpu.CompilerParams(vmem_limit_bytes=VMEM_LIMIT),
        cost_estimate=pl.CostEstimate(
            flops=flops // 64, bytes_accessed=size // 64, transcendentals=0
        ),
    )(*operands)


def whole(x):
    return pl.BlockSpec(x.shape, lambda i, n=len(x.shape): (0,) * n)


def part(x, *index):
    return Part(whole(x), index)


SMEM = pl.BlockSpec(memory_space=pltpu.SMEM)


def shape(*dims, dtype=BF16):
    return jax.ShapeDtypeStruct(dims, dtype)


def encode_begin_kernel(meta, own, w_own, out):
    for start in range(0, own.shape[0], HALF):
        rows = pl.ds(start, HALF)
        out[rows, :] = dot(own[rows, :], w_own[window(meta[0]), :])


def gather_slots(senders_row, sent, out):
    for start in range(0, senders_row.shape[1], HALF):
        col = column(senders_row[:, start : start + HALF])
        out[pl.ds(start, HALF), :] = dot(hot_columns(col, sent.shape[0]), sent[...]).astype(BF16)


def encode_skip_kernel(meta, own, other, begun, w_own, w_other, senders, sent, piece):
    mine, rest = window(meta[0]), window(1 - meta[0])
    for start in range(0, own.shape[0], HALF):
        rows = pl.ds(start, HALF)
        a, b = own[rows, :], other[rows, :]
        sent[rows, mine] = (begun[rows, :] + dot(b, w_own[rest, :])).astype(BF16)
        sent[rows, rest] = (dot(a, w_other[mine, :]) + dot(b, w_other[rest, :])).astype(BF16)
    gather_slots(senders[skip_offset(meta)], sent, piece)


def live_targets(targets, live, offset, columns=slice(None)):
    return jnp.where(live[offset, :, columns] > 0, targets[offset, :, columns], -1)


def encode_near_kernel(meta, sent, senders, piece):
    gather_slots(senders[near_offset(meta)], sent, piece)


def encode_skip_sum_kernel(
    meta, rows, sent, own, other, w1, w1_other, w2, w2_other, senders, targets, live,
    total, before_near, self_term, message, own_message, recv, before,
):
    mine, rest = window(meta[0]), window(1 - meta[0])
    nodes = recv.shape[0]
    for start in range(0, nodes, HALF):
        part_rows = pl.ds(start, HALF)
        a, b = own[part_rows, :], other[part_rows, :]
        recv[part_rows, mine] = (dot(a, w1[mine, :]) + dot(b, w1[rest, :])).astype(BF16)
        recv[part_rows, rest] = (dot(a, w1_other[mine, :]) + dot(b, w1_other[rest, :])).astype(BF16)
    gather_slots(targets[skip_offset(meta)], recv, before)
    from_rows = hot_columns(column(senders[REACH, :, mine]), sent.shape[0])
    to_rows = hot_columns(column(targets[REACH, :, mine]), nodes)
    own_message[...] = silu_message(dot(from_rows, sent[...]) + dot(to_rows, recv[...]))
    message[...] = silu_message(rows[...] + before[...])
    row = live_targets(targets, live, skip_offset(meta))
    own_row = live_targets(targets, live, REACH, mine)
    for start in range(0, nodes, HALF):
        value = dot(hot_rows(row - start, HALF), message[...])
        value = value + dot(hot_rows(own_row - start, HALF), own_message[...])
        total[pl.ds(start, HALF), :] = value
    gather_slots(targets[near_offset(meta)], recv, before_near)
    far = margin_rows(meta)
    for held, rows in ((pl.ds(0, HALF), mine), (pl.ds(HALF, MARGIN), far)):
        a, b = own[rows, :], other[rows, :]
        self_term[held, mine] = (dot(a, w2[mine, :]) + dot(b, w2[rest, :])).astype(BF16)
        self_term[held, rest] = (dot(a, w2_other[mine, :]) + dot(b, w2_other[rest, :])).astype(BF16)


def encode_near_sum_kernel(
    meta, rows, before, targets, live, total, out_own, out_other, message, halves
):
    message[...] = silu_message(rows[...] + before[...])
    row = live_targets(targets, live, near_offset(meta))
    for index, half in enumerate((1 - meta[0], meta[0])):
        value = dot(hot_rows(row - half * HALF, HALF), message[...]) + total[window(half), :]
        halves[index] = value.astype(BF16)
    held, far = pl.ds(0, HALF), pl.ds(HALF, MARGIN)
    out_own[held, :] = halves[1]
    out_own[far, :] = halves[0, extra_rows(meta), :]
    out_other[held, :] = halves[0]
    start = pl.multiple_of(meta[0] * (HALF - MARGIN), MARGIN)
    out_other[far, :] = halves[1, pl.ds(start, MARGIN), :]


def put_edges(meta, now, w0, w0_other, cross, line):
    mine, rest = window(meta[0]), window(1 - meta[0])
    odd = meta[1] % 2
    head, tail = HALF * meta[0], HALF - MARGIN * meta[0]
    for edge, start in (
        (cross, (1 - odd) * head + odd * tail),
        (line, (1 - odd) * tail + odd * head),
    ):
        rows = now[pl.ds(pl.multiple_of(start, MARGIN), MARGIN), :]
        edge[:, mine] = dot(rows, w0[...]).astype(BF16)
        edge[:, rest] = dot(rows, w0_other[...]).astype(BF16)


def encode_update_kernel(
    meta, own, other, self_term, sum_own, sum_other, w3, w3_other, w0, w0_other,
    now, cross, line, held_now,
):
    mine, rest = window(meta[0]), window(1 - meta[0])
    summed = sum_own[...] + sum_other[...]
    far = margin_rows(meta)
    for cols, latent, w in ((mine, own, w3), (rest, other, w3_other)):
        step = silu(self_term[:, cols].astype(F32) + dot(summed, w[...]))
        for held, rows in ((slice(0, HALF), mine), (slice(HALF, HELD), far)):
            held_now[held, cols] = (latent[rows, :].astype(F32) + step[held, :]).astype(BF16)
    now[...] = held_now[pl.ds(0, HALF), :]
    put_edges(meta, held_now, w0, w0_other, cross, line)


def layer_project_kernel(
    last, meta, own, other, w0, w0_other, w1, w1_other, w2, w2_other,
    sent_own, sent_other, recv, self_own, *self_other,
):
    mine, rest = window(meta[0]), window(1 - meta[0])
    held, far = pl.ds(0, HALF), pl.ds(HALF, MARGIN)
    for cols, w in ((mine, w0), (rest, w0_other)):
        sent_own[:, cols] = dot(own[...], w[...]).astype(BF16)
        sent_other[:, cols] = dot(other[...], w[...]).astype(BF16)
    for cols, w in ((mine, w1), (rest, w1_other)):
        recv[held, cols] = dot(own[...], w[...]).astype(BF16)
        if not last:
            recv[far, cols] = dot(other[extra_rows(meta), :], w[...]).astype(BF16)
    for cols, w in ((mine, w2), (rest, w2_other)):
        self_own[held, cols] = dot(own[...], w[...]).astype(BF16)
        if last:
            self_other[0][:, cols] = dot(other[...], w[...]).astype(BF16)
        else:
            self_own[far, cols] = dot(other[extra_rows(meta), :], w[...]).astype(BF16)


def held_slots(meta, slots):
    tail = pltpu.roll(slots[:, 2 * HALF - LANES :], LANES - MARGIN, 1)
    far = jnp.where(meta[0] == 0, tail, slots[:, :LANES])
    return jnp.concatenate([slots[:, window(meta[0])], far], axis=1)


def layer_gather_kernel(meta, own, other, senders, out):
    base = meta[1] * (2 * HALF)
    nodes = out.shape[1]
    held = held_slots(meta, senders) - base
    for k in range(senders.shape[0]):
        local = held[k : k + 1, :]
        col = column(local - meta[0] * HALF)[:nodes]
        col_other = column(local - (1 - meta[0]) * HALF)[:nodes]
        value = dot(hot_columns(col, HALF), own[...])
        value = value + dot(hot_columns(col_other, HALF), other[...])
        out[k] = value.astype(BF16)


def layer_sum(meta, gathered, recv, cross, line, senders, live, halo, total):
    nodes = 2 * HALF
    base = meta[1] * nodes
    count, held = gathered.shape[0], gathered.shape[1]
    hots, flags = [], []
    slots, alive = held_slots(meta, senders) - base, held_slots(meta, live)
    for k in range(count):
        local = slots[k : k + 1, :]
        where = jnp.where(local < 0, local + MARGIN, local - nodes + MARGIN)
        where = jnp.where((local >= 0) & (local < nodes), -1, where)
        hots.append(hot_columns(column(where)[:held], 2 * MARGIN))
        flags.append(column(alive[k : k + 1, :])[:held].astype(BF16))
    odd = meta[1] % 2
    halo[pl.ds(pl.multiple_of(odd * MARGIN, MARGIN), MARGIN), :] = cross[...]
    halo[pl.ds(pl.multiple_of((1 - odd) * MARGIN, MARGIN), MARGIN), :] = line[...]
    outside = dot(jnp.concatenate(hots, axis=0), halo[...]).astype(BF16)
    step = 32
    for start in range(0, held, step):
        rows = pl.ds(start, step)
        side = recv[rows, :]
        running = None
        for k in range(count):
            row = k * held + start
            message = silu_message(outside[row : row + step, :] + gathered[k, rows, :] + side)
            flag = jnp.concatenate([flags[k][start : start + step, :]] * 4, axis=1)
            message = (message * flag).astype(F32)
            running = message if running is None else running + message
        total[rows, :] = running.astype(BF16)


def layer_update_kernel(
    meta, gathered, recv, line, cross, senders, live, now, now_other, self_term,
    w3, w3_other, w0, w0_other, out, edge_cross, edge_line, halo, total, held_now,
):
    mine, rest = window(meta[0]), window(1 - meta[0])
    layer_sum(meta, gathered, recv, cross, line, senders, live, halo, total)
    summed = total[...]
    for cols, w in ((mine, w3), (rest, w3_other)):
        step = silu(self_term[:, cols].astype(F32) + dot(summed, w[...]))
        far = now_other[extra_rows(meta), cols].astype(F32)
        held_now[pl.ds(0, HALF), cols] = (now[:, cols].astype(F32) + step[:HALF]).astype(BF16)
        held_now[pl.ds(HALF, MARGIN), cols] = (far + step[HALF:]).astype(BF16)
    out[...] = held_now[pl.ds(0, HALF), :]
    put_edges(meta, held_now, w0, w0_other, edge_cross, edge_line)


def layer_sum_kernel(meta, gathered, recv, cross, line, senders, live, out, halo):
    layer_sum(meta, gathered, recv, cross, line, senders, live, halo, out)


def last_update_kernel(
    meta, now_own, now_other, self_own, self_other, sum_own, sum_other, w3, w3_other,
    w0, w0_other, out, sent, now,
):
    mine, rest = window(meta[0]), window(1 - meta[0])
    for rows, latent, self_term, summed in (
        (mine, now_own, self_own, sum_own),
        (rest, now_other, self_other, sum_other),
    ):
        for cols, w in ((mine, w3), (rest, w3_other)):
            step = silu(self_term[:, cols] + dot(summed[...], w[...]))
            now[:, cols] = (latent[:, cols].astype(F32) + step).astype(BF16)
        out[rows, :] = now[:, mine]
        for cols, w in ((mine, w0), (rest, w0_other)):
            sent[rows, cols] = dot(now[...], w[...]).astype(BF16)


def decode_prepare_kernel(
    meta, own, other, w1, w1_other, w2, targets, mesh_now,
    before_own, before_near, before_skip, self_term, mesh_out, recv,
):
    mesh_out[...] = mesh_now[...]
    mine, rest = window(meta[0]), window(1 - meta[0])
    for start in range(0, own.shape[0], HALF):
        rows = pl.ds(start, HALF)
        a, b = own[rows, :], other[rows, :]
        recv[rows, mine] = (dot(a, w1[mine, :]) + dot(b, w1[rest, :])).astype(BF16)
        recv[rows, rest] = (dot(a, w1_other[mine, :]) + dot(b, w1_other[rest, :])).astype(BF16)
        self_term[rows, :] = (dot(a, w2[mine, :]) + dot(b, w2[rest, :])).astype(BF16)
    half = before_own.shape[0]
    gather_slots(targets[REACH, :, window(meta[0], half)], recv, before_own)
    gather_slots(targets[near_offset(meta)], recv, before_near)
    gather_slots(targets[skip_offset(meta)], recv, before_skip)


def decode_messages(meta, offset, columns, sent, before, senders, message):
    from_row = senders[offset, :, columns]
    for start in range(0, before.shape[0], HALF):
        rows = pl.ds(start, HALF)
        hot = hot_columns(column(from_row[:, start : start + HALF]), sent.shape[0])
        pre = dot(hot, sent[...]) + before[rows, :].astype(F32)
        message[rows, :] = silu_message(pre)


def decode_scatter(row, message, total, first, out):
    for start in range(0, out.shape[0], HALF):
        value = dot(hot_rows(row - (first + start), HALF), message[...])
        if total is not None:
            value = value + total[pl.ds(first + start, HALF), :].astype(F32)
        out[pl.ds(start, HALF), :] = value.astype(BF16)


def decode_own_kernel(meta, sent, before, senders, targets, live, out, message):
    columns = window(meta[0], before.shape[0])
    decode_messages(meta, REACH, columns, sent, before, senders, message)
    decode_scatter(live_targets(targets, live, REACH, columns), message, None, 0, out)


def decode_sum_kernel(
    offset_of, meta, sent, before, senders, targets, live, total, out, message
):
    offset = offset_of(meta)
    decode_messages(meta, offset, slice(None), sent, before, senders, message)
    decode_scatter(live_targets(targets, live, offset), message, total, 0, out)


def decode_rest_kernel(offset_of, meta, message, targets, live, total, out):
    row = live_targets(targets, live, offset_of(meta))
    decode_scatter(row, message, total, out.shape[0], out)


def final_kernel(first, meta, own, self_term, sum_own, sum_other, weights, *refs):
    out, w3 = refs[-1], weights.at[3]
    for start in range(0, out.shape[0], HALF):
        rows, from_rows = pl.ds(start, HALF), pl.ds(first + start, HALF)
        summed = sum_own[rows, :] + sum_other[rows, :]
        step = silu(self_term[from_rows, :].astype(F32) + dot(summed, w3[...]))
        out[rows, :] = (own[from_rows, :].astype(F32) + step).astype(BF16)


def body(
    grid_latent,
    mesh_latent,
    encode_weights,
    layer_weights,
    decode_weights,
    encode_senders,
    encode_targets,
    encode_live,
    mesh_senders,
    mesh_live,
    decode_senders,
    decode_targets,
    decode_live,
):
    meta = jnp.stack([lax.axis_index("feat"), lax.axis_index("band")]).astype(I32)
    grid_rows, cols = grid_latent.shape
    mesh_rows = mesh_latent.shape[0]
    full = 2 * cols
    senders, targets, live = (x.transpose(1, 0, 2) for x in (encode_senders, encode_targets, encode_live))
    slots = senders.shape[2]

    grid_other = swap(grid_latent)
    encode_other = swap(encode_weights)
    mesh_other = swap(mesh_latent)
    (begun,) = call(
        encode_begin_kernel,
        "encode_begin",
        (meta, grid_latent, encode_weights),
        [SMEM, whole(grid_latent), part(encode_weights, 0)],
        [shape(grid_rows, cols, dtype=F32)],
        2 * grid_rows * cols * cols,
    )
    grid_other, mesh_other = lax.optimization_barrier((grid_other, mesh_other))
    operands = (meta, grid_latent, grid_other, begun, encode_weights, encode_other, senders)
    sent, skip_piece = call(
        encode_skip_kernel,
        "encode_skip",
        operands,
        [SMEM] + [whole(x) for x in operands[1:4]]
        + [part(encode_weights, 0), part(encode_other, 0), whole(senders)],
        [shape(grid_rows, full), shape(slots, full)],
        2 * full * (grid_rows * full + slots * grid_rows),
    )
    skip_rows = exchange(skip_piece, skip_shift)
    layer_other = swap(after(layer_weights, skip_piece))
    operands = (meta, sent, senders)
    (near_piece,) = call(
        encode_near_kernel,
        "encode_near",
        operands,
        [SMEM, whole(sent), whole(senders)],
        [shape(slots, full)],
        2 * full * slots * grid_rows,
    )
    near_rows = exchange(near_piece, near_shift)
    operands = (
        meta, skip_rows, sent, mesh_latent, mesh_other, encode_weights, encode_other,
        encode_weights, encode_other, senders, targets, live,
    )
    total, before_near, self_term = call(
        encode_skip_sum_kernel,
        "encode_skip_sum",
        operands,
        [SMEM] + [whole(x) for x in operands[1:5]]
        + [part(operands[5 + i], 1 + i // 2) for i in range(4)]
        + [whole(x) for x in operands[9:]],
        [
            shape(mesh_rows, full, dtype=F32),
            shape(slots, full),
            shape(HELD, full),
        ],
        2 * full * mesh_rows * slots * 3,
        [
            pltpu.VMEM((slots, full), BF16),
            pltpu.VMEM((HALF, full), BF16),
            pltpu.VMEM((mesh_rows, full), BF16),
            pltpu.VMEM((slots, full), BF16),
        ],
    )
    operands = (meta, near_rows, before_near, targets, live, total)
    sum_own, sum_other = call(
        encode_near_sum_kernel,
        "encode_near_sum",
        operands,
        [SMEM, whole(near_rows), whole(before_near), whole(targets), whole(live), whole(total)],
        [shape(HELD, full), shape(HELD, full)],
        2 * full * mesh_rows * slots,
        [pltpu.VMEM((slots, full), BF16), pltpu.VMEM((2, HALF, full), BF16)],
    )
    sum_arrived = swap(sum_other)
    decode_other = swap(after(decode_weights, sum_other))
    operands = (
        meta, mesh_latent, mesh_other, self_term, sum_own, sum_arrived,
        encode_weights, encode_other, layer_weights, layer_other,
    )
    now, cross_edge, line_edge = call(
        encode_update_kernel,
        "encode_update",
        operands,
        [SMEM] + [whole(x) for x in operands[1:6]]
        + [part(encode_weights, 3), part(encode_other, 3)]
        + [part(layer_weights, 0, 0), part(layer_other, 0, 0)],
        [shape(HALF, full), shape(MARGIN, full), shape(MARGIN, full)],
        2 * HALF * full * full,
        [pltpu.VMEM((HELD, full), BF16)],
    )

    senders_t, live_t = mesh_senders.T, mesh_live.T
    degree = senders_t.shape[0]
    for layer in range(LAYERS):
        last = layer == LAYERS - 1
        cross = exchange(cross_edge, cross_pairs)
        line = exchange(line_edge, line_pairs)
        now_other = swap(now)
        operands = (meta, now, now_other) + (layer_weights, layer_other) * 3
        results = call(
            functools.partial(layer_project_kernel, last),
            f"layer_project_{layer}",
            operands,
            [SMEM, whole(now), whole(now_other)]
            + [part(operands[3 + i], layer, i // 2) for i in range(6)],
            [shape(HALF, full)] * 2 + [shape(HALF if last else HELD, full)] * 2
            + [shape(HALF, full)] * last,
            2 * HALF * full * full * 4,
        )
        sent_own, sent_other, recv, self_own = results[:4]
        operands = (meta, sent_own, sent_other, senders_t)
        (gathered,) = call(
            layer_gather_kernel,
            f"layer_gather_{layer}",
            operands,
            [SMEM, whole(sent_own), whole(sent_other), whole(senders_t)],
            [shape(degree, HALF if last else HELD, full)],
            2 * degree * HALF * full * mesh_rows,
        )
        halo = (cross, line) if last else (line, cross)
        operands = (meta, gathered, recv) + halo + (senders_t, live_t)
        scratch = [pltpu.VMEM((2 * MARGIN, full), BF16)]
        sum_specs = (
            [SMEM] + [whole(x) for x in operands[1:5]]
            + [whole(senders_t), whole(live_t)]
        )
        if last:
            (summed,) = call(
                layer_sum_kernel,
                f"layer_sum_{layer}",
                operands,
                sum_specs,
                [shape(HALF, full)],
                2 * degree * HALF * full * 2 * MARGIN,
                scratch,
            )
            continue
        operands += (now, now_other, self_own) + (layer_weights, layer_other) * 2
        now, cross_edge, line_edge = call(
            layer_update_kernel,
            f"layer_update_{layer}",
            operands,
            sum_specs + [whole(now), whole(now_other), whole(self_own)]
            + [part(layer_weights, layer, 3), part(layer_other, layer, 3)]
            + [part(layer_weights, layer + 1, 0), part(layer_other, layer + 1, 0)],
            [shape(HALF, full), shape(MARGIN, full), shape(MARGIN, full)],
            2 * HALF * full * (degree * 2 * MARGIN + full),
            scratch + [pltpu.VMEM((HELD, full), BF16)] * 2,
        )
    operands = (
        meta, now, now_other, self_own, results[4], summed, swap(summed),
        layer_weights, layer_other, decode_weights, decode_other,
    )
    mesh_now, sent = call(
        last_update_kernel,
        "last_update",
        operands,
        [SMEM] + [whole(x) for x in operands[1:7]]
        + [part(layer_weights, LAYERS - 1, 3), part(layer_other, LAYERS - 1, 3)]
        + [part(decode_weights, 0), part(decode_other, 0)],
        [shape(mesh_rows, cols), shape(mesh_rows, full)],
        2 * mesh_rows * full * full * 2,
        [pltpu.VMEM((HALF, full), BF16)],
    )

    near_rows = exchange(sent, near_shift)
    skip_rows = exchange(sent, skip_shift)
    senders, targets, live = (x.transpose(1, 0, 2) for x in (decode_senders, decode_targets, decode_live))
    slots = senders.shape[2]
    operands = (
        meta, grid_latent, grid_other, decode_weights, decode_other, decode_weights, targets,
        mesh_now,
    )
    before_own, before_near, before_skip, self_term, mesh_now = call(
        decode_prepare_kernel,
        "decode_prepare",
        operands,
        [SMEM, whole(grid_latent), whole(grid_other)]
        + [part(decode_weights, 1), part(decode_other, 1), part(decode_weights, 2), whole(targets)]
        + [whole(mesh_now)],
        [
            shape(slots // 2, full),
            shape(slots, full),
            shape(slots, full),
            shape(grid_rows, cols),
            shape(mesh_rows, cols),
        ],
        2 * full * grid_rows * (full + 5 * slots // 2),
        [pltpu.VMEM((grid_rows, full), BF16)],
    )
    flops = 2 * full * slots * (grid_rows + mesh_rows)
    message_space = [pltpu.VMEM((slots, full), BF16)]
    operands = (meta, sent, before_own, senders, targets, live)
    (total,) = call(
        decode_own_kernel,
        "decode_own",
        operands,
        [SMEM] + [whole(x) for x in operands[1:]],
        [shape(grid_rows, full)],
        flops // 2,
        [pltpu.VMEM(before_own.shape, BF16)],
    )
    operands = (meta, skip_rows, before_skip, senders, targets, live, total)
    (total,) = call(
        functools.partial(decode_sum_kernel, skip_offset),
        "decode_skip",
        operands,
        [SMEM] + [whole(x) for x in operands[1:]],
        [shape(grid_rows, full)],
        flops,
        message_space,
    )
    half = grid_rows // 2
    operands = (meta, near_rows, before_near, senders, targets, live, total)
    head, message = call(
        functools.partial(decode_sum_kernel, near_offset),
        "decode_near",
        operands,
        [SMEM] + [whole(x) for x in operands[1:]],
        [shape(half, full), shape(slots, full)],
        flops,
    )
    operands = (meta, message, targets, live, total)
    (tail,) = call(
        functools.partial(decode_rest_kernel, near_offset),
        "decode_rest",
        operands,
        [SMEM] + [whole(x) for x in operands[1:]],
        [shape(half, full)],
        flops // 2,
    )
    grid_now = None
    for index, summed in enumerate((head, tail)):
        block = pl.BlockSpec((half, cols), lambda i, index=index: (index, 0))
        operands = (meta, grid_latent, self_term, summed, swap(summed), decode_weights)
        specs = [SMEM] + [whole(x) for x in operands[1:]]
        aliases = {}
        if index:
            operands, specs, aliases = operands + (grid_now,), specs + [pl.BlockSpec(memory_space=pl.ANY)], {6: 0}
        grid_now = pl.pallas_call(
            functools.partial(final_kernel, index * half),
            name=f"final_update_{index}",
            grid=(1,),
            in_specs=specs,
            out_specs=block,
            out_shape=shape(grid_rows, cols),
            input_output_aliases=aliases,
            compiler_params=pltpu.CompilerParams(vmem_limit_bytes=VMEM_LIMIT),
        )(*operands)
    return mesh_now, grid_now


def solution(mesh):
    placed = (
        P("band", "feat"),
        P("band", "feat"),
        P(None, None, "feat"),
        P(None, None, None, "feat"),
        P(None, None, "feat"),
        P("band", None, None),
        P("band", None, None),
        P("band", None, None),
        P("band", None),
        P("band", None),
        P("band", None, None),
        P("band", None, None),
        P("band", None, None),
    )
    return jax.shard_map(
        body,
        mesh=mesh,
        in_specs=placed,
        out_specs=(P("band", "feat"), P("band", "feat")),
        check_vma=False,
    )
```

```python
import functools

import jax
import jax.numpy as jnp
from jax import lax
from jax.experimental import pallas as pl
from jax.experimental.pallas import tpu as pltpu
from jax.sharding import PartitionSpec as P

REACH = 2
LAYERS = 2
MARGIN = 64
HALF = 256
HELD = HALF + MARGIN
LANES = 128
F32 = jnp.float32
BF16 = jnp.bfloat16
I32 = jnp.int32
VMEM_LIMIT = 36 * 1024 * 1024


def swap(value):
    return lax.ppermute(value, "feat", [(0, 1), (1, 0)])


def flat(partners):
    return [(2 * s + c, 2 * t + e) for (s, c), (t, e) in partners.items()]


def shift(steps, up, count):
    partners = {}
    for s in range(count):
        partners[s, up] = (s + steps, up) if s + steps < count else (s, 1 - up)
        partners[s, 1 - up] = (s - steps, 1 - up) if s >= steps else (s, up)
    return flat(partners)


near_shift = functools.partial(shift, 1, 0)
skip_shift = functools.partial(shift, 2, 0)


def cross_pairs(count):
    partners = {}
    for s in range(count):
        other = s + 1 if s % 2 else s - 1
        for c in range(2):
            partners[s, c] = (other, c) if 0 <= other < count else (s, 1 - c)
    return flat(partners)


def line_pairs(count):
    return flat({(s, c): (s ^ 1, c) for s in range(count) for c in range(2)})


def exchange(value, pairs):
    return lax.ppermute(value, ("band", "feat"), pairs(lax.axis_size("band")))


def after(value, other):
    return lax.optimization_barrier((value, other))[0]


def silu(v):
    half = 0.5 * v
    return half + half * jnp.tanh(half)


def silu_message(v):
    half = v.astype(BF16) * BF16(0.5)
    return half + half * jnp.tanh(half)


def dot(a, b):
    return jnp.dot(a, b, preferred_element_type=F32)


def window(index, size=HALF):
    return pl.ds(pl.multiple_of(index * size, size), size)


def extra_rows(meta):
    return pl.ds(pl.multiple_of((1 - meta[0]) * (HALF - MARGIN), MARGIN), MARGIN)


def margin_rows(meta):
    return pl.ds(pl.multiple_of((1 - meta[0]) * (2 * HALF - MARGIN), MARGIN), MARGIN)


def near_offset(meta):
    return 3 - 2 * meta[0]


def skip_offset(meta):
    return 4 - 4 * meta[0]


def column(row):
    parts = [
        jnp.broadcast_to(row[:, start : start + LANES], (LANES, LANES)).T
        for start in range(0, row.shape[1], LANES)
    ]
    return parts[0] if len(parts) == 1 else jnp.concatenate(parts, axis=0)


def hot_columns(col, width):
    col = col.astype(jnp.int16)
    ids = lax.broadcasted_iota(I32, col.shape, 1).astype(jnp.int16)
    one, zero = BF16(1), BF16(0)
    parts = [
        jnp.where(col == ids + jnp.int16(start), one, zero) for start in range(0, width, LANES)
    ]
    return parts[0] if len(parts) == 1 else jnp.concatenate(parts, axis=1)


def hot_rows(row, height):
    ids = lax.broadcasted_iota(I32, (height, row.shape[1]), 0)
    return jnp.where(row == ids, 1.0, 0.0).astype(BF16)


class Part:
    def __init__(self, spec, index):
        self.spec, self.index = spec, index


def call(kernel, name, operands, specs, outs, flops, scratch=()):
    def viewed(*refs):
        refs = [
            ref.at[specs[i].index] if i < len(specs) and isinstance(specs[i], Part) else ref
            for i, ref in enumerate(refs)
        ]
        kernel(*refs)

    size = sum(x.size * x.dtype.itemsize for x in outs)
    return pl.pallas_call(
        viewed,
        name=name,
        grid=(1,),
        in_specs=[spec.spec if isinstance(spec, Part) else spec for spec in specs],
        out_specs=[whole(x) for x in outs],
        out_shape=list(outs),
        scratch_shapes=list(scratch),
        compiler_params=pltpu.CompilerParams(vmem_limit_bytes=VMEM_LIMIT),
        cost_estimate=pl.CostEstimate(
            flops=flops // 64, bytes_accessed=size // 64, transcendentals=0
        ),
    )(*operands)


def whole(x):
    return pl.BlockSpec(x.shape, lambda i, n=len(x.shape): (0,) * n)


def part(x, *index):
    return Part(whole(x), index)


SMEM = pl.BlockSpec(memory_space=pltpu.SMEM)


def shape(*dims, dtype=BF16):
    return jax.ShapeDtypeStruct(dims, dtype)


def encode_begin_kernel(meta, own, w_own, out):
    for start in range(0, own.shape[0], HALF):
        rows = pl.ds(start, HALF)
        out[rows, :] = dot(own[rows, :], w_own[window(meta[0]), :])


def gather_slots(senders_row, sent, out):
    for start in range(0, senders_row.shape[1], HALF):
        col = column(senders_row[:, start : start + HALF])
        out[pl.ds(start, HALF), :] = dot(hot_columns(col, sent.shape[0]), sent[...]).astype(BF16)


def encode_skip_kernel(meta, own, other, begun, w_own, w_other, senders, sent, piece):
    mine, rest = window(meta[0]), window(1 - meta[0])
    for start in range(0, own.shape[0], HALF):
        rows = pl.ds(start, HALF)
        a, b = own[rows, :], other[rows, :]
        sent[rows, mine] = (begun[rows, :] + dot(b, w_own[rest, :])).astype(BF16)
        sent[rows, rest] = (dot(a, w_other[mine, :]) + dot(b, w_other[rest, :])).astype(BF16)
    gather_slots(senders[skip_offset(meta)], sent, piece)


def live_targets(targets, live, offset, columns=slice(None)):
    return jnp.where(live[offset, :, columns] > 0, targets[offset, :, columns], -1)


def encode_near_kernel(meta, sent, senders, piece):
    gather_slots(senders[near_offset(meta)], sent, piece)


def encode_skip_sum_kernel(
    meta, rows, sent, own, other, w1, w1_other, w2, w2_other, senders, targets, live,
    total, before_near, self_term, message, own_message, recv, before,
):
    mine, rest = window(meta[0]), window(1 - meta[0])
    nodes = recv.shape[0]
    for start in range(0, nodes, HALF):
        part_rows = pl.ds(start, HALF)
        a, b = own[part_rows, :], other[part_rows, :]
        recv[part_rows, mine] = (dot(a, w1[mine, :]) + dot(b, w1[rest, :])).astype(BF16)
        recv[part_rows, rest] = (dot(a, w1_other[mine, :]) + dot(b, w1_other[rest, :])).astype(BF16)
    gather_slots(targets[skip_offset(meta)], recv, before)
    from_rows = hot_columns(column(senders[REACH, :, mine]), sent.shape[0])
    to_rows = hot_columns(column(targets[REACH, :, mine]), nodes)
    own_message[...] = silu_message(dot(from_rows, sent[...]) + dot(to_rows, recv[...]))
    message[...] = silu_message(rows[...] + before[...])
    row = live_targets(targets, live, skip_offset(meta))
    own_row = live_targets(targets, live, REACH, mine)
    for start in range(0, nodes, HALF):
        value = dot(hot_rows(row - start, HALF), message[...])
        value = value + dot(hot_rows(own_row - start, HALF), own_message[...])
        total[pl.ds(start, HALF), :] = value
    gather_slots(targets[near_offset(meta)], recv, before_near)
    far = margin_rows(meta)
    for held, rows in ((pl.ds(0, HALF), mine), (pl.ds(HALF, MARGIN), far)):
        a, b = own[rows, :], other[rows, :]
        self_term[held, mine] = (dot(a, w2[mine, :]) + dot(b, w2[rest, :])).astype(BF16)
        self_term[held, rest] = (dot(a, w2_other[mine, :]) + dot(b, w2_other[rest, :])).astype(BF16)


def encode_near_sum_kernel(
    meta, rows, before, targets, live, total, out_own, out_other, message, halves
):
    message[...] = silu_message(rows[...] + before[...])
    row = live_targets(targets, live, near_offset(meta))
    for index, half in enumerate((1 - meta[0], meta[0])):
        value = dot(hot_rows(row - half * HALF, HALF), message[...]) + total[window(half), :]
        halves[index] = value.astype(BF16)
    held, far = pl.ds(0, HALF), pl.ds(HALF, MARGIN)
    out_own[held, :] = halves[1]
    out_own[far, :] = halves[0, extra_rows(meta), :]
    out_other[held, :] = halves[0]
    start = pl.multiple_of(meta[0] * (HALF - MARGIN), MARGIN)
    out_other[far, :] = halves[1, pl.ds(start, MARGIN), :]


def put_edges(meta, now, w0, w0_other, cross, line):
    mine, rest = window(meta[0]), window(1 - meta[0])
    odd = meta[1] % 2
    head, tail = HALF * meta[0], HALF - MARGIN * meta[0]
    for edge, start in (
        (cross, (1 - odd) * head + odd * tail),
        (line, (1 - odd) * tail + odd * head),
    ):
        rows = now[pl.ds(pl.multiple_of(start, MARGIN), MARGIN), :]
        edge[:, mine] = dot(rows, w0[...]).astype(BF16)
        edge[:, rest] = dot(rows, w0_other[...]).astype(BF16)


def encode_update_kernel(
    meta, own, other, self_term, sum_own, sum_other, w3, w3_other, w0, w0_other,
    now, cross, line, held_now,
):
    mine, rest = window(meta[0]), window(1 - meta[0])
    summed = sum_own[...] + sum_other[...]
    far = margin_rows(meta)
    for cols, latent, w in ((mine, own, w3), (rest, other, w3_other)):
        step = silu(self_term[:, cols].astype(F32) + dot(summed, w[...]))
        for held, rows in ((slice(0, HALF), mine), (slice(HALF, HELD), far)):
            held_now[held, cols] = (latent[rows, :].astype(F32) + step[held, :]).astype(BF16)
    now[...] = held_now[pl.ds(0, HALF), :]
    put_edges(meta, held_now, w0, w0_other, cross, line)


def layer_project_kernel(
    last, meta, own, other, w0, w0_other, w1, w1_other, w2, w2_other,
    sent_own, sent_other, recv, self_own, *self_other,
):
    mine, rest = window(meta[0]), window(1 - meta[0])
    held, far = pl.ds(0, HALF), pl.ds(HALF, MARGIN)
    for cols, w in ((mine, w0), (rest, w0_other)):
        sent_own[:, cols] = dot(own[...], w[...]).astype(BF16)
        sent_other[:, cols] = dot(other[...], w[...]).astype(BF16)
    for cols, w in ((mine, w1), (rest, w1_other)):
        recv[held, cols] = dot(own[...], w[...]).astype(BF16)
        if not last:
            recv[far, cols] = dot(other[extra_rows(meta), :], w[...]).astype(BF16)
    for cols, w in ((mine, w2), (rest, w2_other)):
        self_own[held, cols] = dot(own[...], w[...]).astype(BF16)
        if last:
            self_other[0][:, cols] = dot(other[...], w[...]).astype(BF16)
        else:
            self_own[far, cols] = dot(other[extra_rows(meta), :], w[...]).astype(BF16)


def held_slots(meta, slots):
    tail = pltpu.roll(slots[:, 2 * HALF - LANES :], LANES - MARGIN, 1)
    far = jnp.where(meta[0] == 0, tail, slots[:, :LANES])
    return jnp.concatenate([slots[:, window(meta[0])], far], axis=1)


def layer_gather_kernel(meta, own, other, senders, out):
    base = meta[1] * (2 * HALF)
    nodes = out.shape[1]
    held = held_slots(meta, senders) - base
    for k in range(senders.shape[0]):
        local = held[k : k + 1, :]
        col = column(local - meta[0] * HALF)[:nodes]
        col_other = column(local - (1 - meta[0]) * HALF)[:nodes]
        value = dot(hot_columns(col, HALF), own[...])
        value = value + dot(hot_columns(col_other, HALF), other[...])
        out[k] = value.astype(BF16)


def layer_sum(meta, gathered, recv, cross, line, senders, live, halo, total):
    nodes = 2 * HALF
    base = meta[1] * nodes
    count, held = gathered.shape[0], gathered.shape[1]
    hots, flags = [], []
    slots, alive = held_slots(meta, senders) - base, held_slots(meta, live)
    for k in range(count):
        local = slots[k : k + 1, :]
        where = jnp.where(local < 0, local + MARGIN, local - nodes + MARGIN)
        where = jnp.where((local >= 0) & (local < nodes), -1, where)
        hots.append(hot_columns(column(where)[:held], 2 * MARGIN))
        flags.append(column(alive[k : k + 1, :])[:held].astype(BF16))
    odd = meta[1] % 2
    halo[pl.ds(pl.multiple_of(odd * MARGIN, MARGIN), MARGIN), :] = cross[...]
    halo[pl.ds(pl.multiple_of((1 - odd) * MARGIN, MARGIN), MARGIN), :] = line[...]
    outside = dot(jnp.concatenate(hots, axis=0), halo[...]).astype(BF16)
    step = 32
    for start in range(0, held, step):
        rows = pl.ds(start, step)
        side = recv[rows, :]
        running = None
        for k in range(count):
            row = k * held + start
            message = silu_message(outside[row : row + step, :] + gathered[k, rows, :] + side)
            flag = jnp.concatenate([flags[k][start : start + step, :]] * 4, axis=1)
            message = (message * flag).astype(F32)
            running = message if running is None else running + message
        total[rows, :] = running.astype(BF16)


def layer_update_kernel(
    meta, gathered, recv, line, cross, senders, live, now, now_other, self_term,
    w3, w3_other, w0, w0_other, out, edge_cross, edge_line, halo, total, held_now,
):
    mine, rest = window(meta[0]), window(1 - meta[0])
    layer_sum(meta, gathered, recv, cross, line, senders, live, halo, total)
    summed = total[...]
    for cols, w in ((mine, w3), (rest, w3_other)):
        step = silu(self_term[:, cols].astype(F32) + dot(summed, w[...]))
        far = now_other[extra_rows(meta), cols].astype(F32)
        held_now[pl.ds(0, HALF), cols] = (now[:, cols].astype(F32) + step[:HALF]).astype(BF16)
        held_now[pl.ds(HALF, MARGIN), cols] = (far + step[HALF:]).astype(BF16)
    out[...] = held_now[pl.ds(0, HALF), :]
    put_edges(meta, held_now, w0, w0_other, edge_cross, edge_line)


def layer_sum_kernel(meta, gathered, recv, cross, line, senders, live, out, halo):
    layer_sum(meta, gathered, recv, cross, line, senders, live, halo, out)


def last_update_kernel(
    meta, now_own, now_other, self_own, self_other, sum_own, sum_other, w3, w3_other,
    w0, w0_other, out, sent, now,
):
    mine, rest = window(meta[0]), window(1 - meta[0])
    for rows, latent, self_term, summed in (
        (mine, now_own, self_own, sum_own),
        (rest, now_other, self_other, sum_other),
    ):
        for cols, w in ((mine, w3), (rest, w3_other)):
            step = silu(self_term[:, cols] + dot(summed[...], w[...]))
            now[:, cols] = (latent[:, cols].astype(F32) + step).astype(BF16)
        out[rows, :] = now[:, mine]
        for cols, w in ((mine, w0), (rest, w0_other)):
            sent[rows, cols] = dot(now[...], w[...]).astype(BF16)


def decode_prepare_kernel(
    meta, own, other, w1, w1_other, w2, targets, mesh_now,
    before_own, before_near, before_skip, self_term, mesh_out, recv,
):
    mesh_out[...] = mesh_now[...]
    mine, rest = window(meta[0]), window(1 - meta[0])
    for start in range(0, own.shape[0], HALF):
        rows = pl.ds(start, HALF)
        a, b = own[rows, :], other[rows, :]
        recv[rows, mine] = (dot(a, w1[mine, :]) + dot(b, w1[rest, :])).astype(BF16)
        recv[rows, rest] = (dot(a, w1_other[mine, :]) + dot(b, w1_other[rest, :])).astype(BF16)
        self_term[rows, :] = (dot(a, w2[mine, :]) + dot(b, w2[rest, :])).astype(BF16)
    half = before_own.shape[0]
    gather_slots(targets[REACH, :, window(meta[0], half)], recv, before_own)
    gather_slots(targets[near_offset(meta)], recv, before_near)
    gather_slots(targets[skip_offset(meta)], recv, before_skip)


def decode_messages(meta, offset, columns, sent, before, senders, message):
    from_row = senders[offset, :, columns]
    for start in range(0, before.shape[0], HALF):
        rows = pl.ds(start, HALF)
        hot = hot_columns(column(from_row[:, start : start + HALF]), sent.shape[0])
        pre = dot(hot, sent[...]) + before[rows, :].astype(F32)
        message[rows, :] = silu_message(pre)


def decode_scatter(row, message, total, first, out):
    for start in range(0, out.shape[0], HALF):
        value = dot(hot_rows(row - (first + start), HALF), message[...])
        if total is not None:
            value = value + total[pl.ds(first + start, HALF), :].astype(F32)
        out[pl.ds(start, HALF), :] = value.astype(BF16)


def decode_own_kernel(meta, sent, before, senders, targets, live, out, message):
    columns = window(meta[0], before.shape[0])
    decode_messages(meta, REACH, columns, sent, before, senders, message)
    decode_scatter(live_targets(targets, live, REACH, columns), message, None, 0, out)


def decode_sum_kernel(
    offset_of, meta, sent, before, senders, targets, live, total, out, message
):
    offset = offset_of(meta)
    decode_messages(meta, offset, slice(None), sent, before, senders, message)
    decode_scatter(live_targets(targets, live, offset), message, total, 0, out)


def decode_rest_kernel(offset_of, meta, message, targets, live, total, out):
    row = live_targets(targets, live, offset_of(meta))
    decode_scatter(row, message, total, total.shape[0] - out.shape[0], out)


def final_kernel(meta, own, self_term, head, head_in, tail, tail_in, w3, out):
    for start in range(0, out.shape[0], HALF):
        rows = pl.ds(start, HALF)
        first = start < head.shape[0]
        sums, lead = ((head, head_in), 0) if first else ((tail, tail_in), head.shape[0])
        part_rows = pl.ds(start - lead, HALF)
        summed = sums[0][part_rows, :] + sums[1][part_rows, :]
        step = silu(self_term[rows, :].astype(F32) + dot(summed, w3[...]))
        out[rows, :] = (own[rows, :].astype(F32) + step).astype(BF16)


def body(
    grid_latent,
    mesh_latent,
    encode_weights,
    layer_weights,
    decode_weights,
    encode_senders,
    encode_targets,
    encode_live,
    mesh_senders,
    mesh_live,
    decode_senders,
    decode_targets,
    decode_live,
):
    meta = jnp.stack([lax.axis_index("feat"), lax.axis_index("band")]).astype(I32)
    grid_rows, cols = grid_latent.shape
    mesh_rows = mesh_latent.shape[0]
    full = 2 * cols
    senders, targets, live = (x.transpose(1, 0, 2) for x in (encode_senders, encode_targets, encode_live))
    slots = senders.shape[2]

    grid_other = swap(grid_latent)
    encode_other = swap(encode_weights)
    mesh_other = swap(mesh_latent)
    (begun,) = call(
        encode_begin_kernel,
        "encode_begin",
        (meta, grid_latent, encode_weights),
        [SMEM, whole(grid_latent), part(encode_weights, 0)],
        [shape(grid_rows, cols, dtype=F32)],
        2 * grid_rows * cols * cols,
    )
    grid_other, mesh_other = lax.optimization_barrier((grid_other, mesh_other))
    operands = (meta, grid_latent, grid_other, begun, encode_weights, encode_other, senders)
    sent, skip_piece = call(
        encode_skip_kernel,
        "encode_skip",
        operands,
        [SMEM] + [whole(x) for x in operands[1:4]]
        + [part(encode_weights, 0), part(encode_other, 0), whole(senders)],
        [shape(grid_rows, full), shape(slots, full)],
        2 * full * (grid_rows * full + slots * grid_rows),
    )
    skip_rows = exchange(skip_piece, skip_shift)
    layer_other = swap(after(layer_weights, skip_piece))
    operands = (meta, sent, senders)
    (near_piece,) = call(
        encode_near_kernel,
        "encode_near",
        operands,
        [SMEM, whole(sent), whole(senders)],
        [shape(slots, full)],
        2 * full * slots * grid_rows,
    )
    near_rows = exchange(near_piece, near_shift)
    operands = (
        meta, skip_rows, sent, mesh_latent, mesh_other, encode_weights, encode_other,
        encode_weights, encode_other, senders, targets, live,
    )
    total, before_near, self_term = call(
        encode_skip_sum_kernel,
        "encode_skip_sum",
        operands,
        [SMEM] + [whole(x) for x in operands[1:5]]
        + [part(operands[5 + i], 1 + i // 2) for i in range(4)]
        + [whole(x) for x in operands[9:]],
        [
            shape(mesh_rows, full, dtype=F32),
            shape(slots, full),
            shape(HELD, full),
        ],
        2 * full * mesh_rows * slots * 3,
        [
            pltpu.VMEM((slots, full), BF16),
            pltpu.VMEM((HALF, full), BF16),
            pltpu.VMEM((mesh_rows, full), BF16),
            pltpu.VMEM((slots, full), BF16),
        ],
    )
    operands = (meta, near_rows, before_near, targets, live, total)
    sum_own, sum_other = call(
        encode_near_sum_kernel,
        "encode_near_sum",
        operands,
        [SMEM, whole(near_rows), whole(before_near), whole(targets), whole(live), whole(total)],
        [shape(HELD, full), shape(HELD, full)],
        2 * full * mesh_rows * slots,
        [pltpu.VMEM((slots, full), BF16), pltpu.VMEM((2, HALF, full), BF16)],
    )
    sum_arrived = swap(sum_other)
    decode_other = swap(after(decode_weights, sum_other))
    operands = (
        meta, mesh_latent, mesh_other, self_term, sum_own, sum_arrived,
        encode_weights, encode_other, layer_weights, layer_other,
    )
    now, cross_edge, line_edge = call(
        encode_update_kernel,
        "encode_update",
        operands,
        [SMEM] + [whole(x) for x in operands[1:6]]
        + [part(encode_weights, 3), part(encode_other, 3)]
        + [part(layer_weights, 0, 0), part(layer_other, 0, 0)],
        [shape(HALF, full), shape(MARGIN, full), shape(MARGIN, full)],
        2 * HALF * full * full,
        [pltpu.VMEM((HELD, full), BF16)],
    )

    senders_t, live_t = mesh_senders.T, mesh_live.T
    degree = senders_t.shape[0]
    for layer in range(LAYERS):
        last = layer == LAYERS - 1
        cross = exchange(cross_edge, cross_pairs)
        line = exchange(line_edge, line_pairs)
        now_other = swap(now)
        operands = (meta, now, now_other) + (layer_weights, layer_other) * 3
        results = call(
            functools.partial(layer_project_kernel, last),
            f"layer_project_{layer}",
            operands,
            [SMEM, whole(now), whole(now_other)]
            + [part(operands[3 + i], layer, i // 2) for i in range(6)],
            [shape(HALF, full)] * 2 + [shape(HALF if last else HELD, full)] * 2
            + [shape(HALF, full)] * last,
            2 * HALF * full * full * 4,
        )
        sent_own, sent_other, recv, self_own = results[:4]
        operands = (meta, sent_own, sent_other, senders_t)
        (gathered,) = call(
            layer_gather_kernel,
            f"layer_gather_{layer}",
            operands,
            [SMEM, whole(sent_own), whole(sent_other), whole(senders_t)],
            [shape(degree, HALF if last else HELD, full)],
            2 * degree * HALF * full * mesh_rows,
        )
        halo = (cross, line) if last else (line, cross)
        operands = (meta, gathered, recv) + halo + (senders_t, live_t)
        scratch = [pltpu.VMEM((2 * MARGIN, full), BF16)]
        sum_specs = (
            [SMEM] + [whole(x) for x in operands[1:5]]
            + [whole(senders_t), whole(live_t)]
        )
        if last:
            (summed,) = call(
                layer_sum_kernel,
                f"layer_sum_{layer}",
                operands,
                sum_specs,
                [shape(HALF, full)],
                2 * degree * HALF * full * 2 * MARGIN,
                scratch,
            )
            continue
        operands += (now, now_other, self_own) + (layer_weights, layer_other) * 2
        now, cross_edge, line_edge = call(
            layer_update_kernel,
            f"layer_update_{layer}",
            operands,
            sum_specs + [whole(now), whole(now_other), whole(self_own)]
            + [part(layer_weights, layer, 3), part(layer_other, layer, 3)]
            + [part(layer_weights, layer + 1, 0), part(layer_other, layer + 1, 0)],
            [shape(HALF, full), shape(MARGIN, full), shape(MARGIN, full)],
            2 * HALF * full * (degree * 2 * MARGIN + full),
            scratch + [pltpu.VMEM((HELD, full), BF16)] * 2,
        )
    operands = (
        meta, now, now_other, self_own, results[4], summed, swap(summed),
        layer_weights, layer_other, decode_weights, decode_other,
    )
    mesh_now, sent = call(
        last_update_kernel,
        "last_update",
        operands,
        [SMEM] + [whole(x) for x in operands[1:7]]
        + [part(layer_weights, LAYERS - 1, 3), part(layer_other, LAYERS - 1, 3)]
        + [part(decode_weights, 0), part(decode_other, 0)],
        [shape(mesh_rows, cols), shape(mesh_rows, full)],
        2 * mesh_rows * full * full * 2,
        [pltpu.VMEM((HALF, full), BF16)],
    )

    near_rows = exchange(sent, near_shift)
    skip_rows = exchange(sent, skip_shift)
    senders, targets, live = (x.transpose(1, 0, 2) for x in (decode_senders, decode_targets, decode_live))
    slots = senders.shape[2]
    operands = (
        meta, grid_latent, grid_other, decode_weights, decode_other, decode_weights, targets,
        mesh_now,
    )
    before_own, before_near, before_skip, self_term, mesh_now = call(
        decode_prepare_kernel,
        "decode_prepare",
        operands,
        [SMEM, whole(grid_latent), whole(grid_other)]
        + [part(decode_weights, 1), part(decode_other, 1), part(decode_weights, 2), whole(targets)]
        + [whole(mesh_now)],
        [
            shape(slots // 2, full),
            shape(slots, full),
            shape(slots, full),
            shape(grid_rows, cols),
            shape(mesh_rows, cols),
        ],
        2 * full * grid_rows * (full + 5 * slots // 2),
        [pltpu.VMEM((grid_rows, full), BF16)],
    )
    flops = 2 * full * slots * (grid_rows + mesh_rows)
    message_space = [pltpu.VMEM((slots, full), BF16)]
    operands = (meta, sent, before_own, senders, targets, live)
    (total,) = call(
        decode_own_kernel,
        "decode_own",
        operands,
        [SMEM] + [whole(x) for x in operands[1:]],
        [shape(grid_rows, full)],
        flops // 2,
        [pltpu.VMEM(before_own.shape, BF16)],
    )
    operands = (meta, skip_rows, before_skip, senders, targets, live, total)
    (total,) = call(
        functools.partial(decode_sum_kernel, skip_offset),
        "decode_skip",
        operands,
        [SMEM] + [whole(x) for x in operands[1:]],
        [shape(grid_rows, full)],
        flops,
        message_space,
    )
    rest = HALF
    operands = (meta, near_rows, before_near, senders, targets, live, total)
    head, message = call(
        functools.partial(decode_sum_kernel, near_offset),
        "decode_near",
        operands,
        [SMEM] + [whole(x) for x in operands[1:]],
        [shape(grid_rows - rest, full), shape(slots, full)],
        flops,
    )
    operands = (meta, message, targets, live, total)
    (tail,) = call(
        functools.partial(decode_rest_kernel, near_offset),
        "decode_rest",
        operands,
        [SMEM] + [whole(x) for x in operands[1:]],
        [shape(rest, full)],
        flops // 2,
    )
    operands = (
        meta, grid_latent, self_term, head, swap(head), tail, swap(tail), decode_weights
    )
    (grid_now,) = call(
        final_kernel,
        "final_update",
        operands,
        [SMEM] + [whole(x) for x in operands[1:7]] + [part(decode_weights, 3)],
        [shape(grid_rows, cols)],
        2 * full * grid_rows * cols,
    )
    return mesh_now, grid_now


def solution(mesh):
    placed = (
        P("band", "feat"),
        P("band", "feat"),
        P(None, None, "feat"),
        P(None, None, None, "feat"),
        P(None, None, "feat"),
        P("band", None, None),
        P("band", None, None),
        P("band", None, None),
        P("band", None),
        P("band", None),
        P("band", None, None),
        P("band", None, None),
        P("band", None, None),
    )
    return jax.shard_map(
        body,
        mesh=mesh,
        in_specs=placed,
        out_specs=(P("band", "feat"), P("band", "feat")),
        check_vma=False,
    )
```
